32 devices in a mesh: stn: 16 (over z, y, x), chan: 2 (over core).
Axes of the slice: x: 2, y: 2, z: 4, core: 2. Of those that a mesh axis runs over, the one named last changes fastest.
Arguments:
- voltages: bfloat16 [32, 2, 143, 2048], P(('stn', 'chan')), may hold values from -6 to 6
- flags: float32 [16, 128], P('stn'), may hold values from 0 to 1, as said below
- station_row: int32 [16], P('stn'), may hold values from 0 to 15, each once
Outputs:
- visibility: bfloat16 [2048, 32, 32], P(('stn', 'chan'))
The draws below stay inside these ranges and needn't reach their ends.
Inputs may be any that keep to these rules, and one draw needn't show every extreme that they name: `flags`: 0 marks a flagged spectrum of a station, 1 a fully usable one; some stations have 0 at all 128 spectra. `station_row`: every row pair is given to exactly one station.
All inputs are finite; a program needn't handle non-finite values.
Results may differ from the reference program's by a relative error of at most 0.006.
Values may be sent and summed in bfloat16 or wider, within the bound.
A program may use at most 64 MiB of HBM per device.

```python
import math
import jax
import jax.numpy as jnp
from jax import lax

CH = 2048
TAPS = 16
SPECTRA = 128
INPUTS = 32
STATIONS = 16
FRAMES = 143


def draw_flags(key, part):
    first, second, third, fourth, fifth = jax.random.split(jax.random.fold_in(key, 11), 5)
    level = jax.random.uniform(first, (STATIONS, SPECTRA), jnp.float32, 0.25, 1.0)
    full = jax.random.randint(second, (STATIONS, SPECTRA), 0, 4) == 0
    dropped = jax.random.randint(third, (STATIONS, SPECTRA), 0, 8) == 0
    lost = jax.random.randint(fourth, (STATIONS, 1), 0, 16) == 0
    chosen = jax.random.randint(fifth, (), 0, STATIONS)
    lost = jnp.logical_or(lost, (jnp.arange(STATIONS) == chosen)[:, None])
    value = jnp.where(full, 1.0, level)
    value = jnp.where(dropped, 0.0, value)
    value = jnp.where(lost, 0.0, value)
    return value.astype(jnp.float32)


def shard_levels(stream_key, extent, shards, low, high):
    gain = 1.0
    for axis_at, shards_of in shards:
        steps = jax.random.uniform(jax.random.fold_in(jax.random.fold_in(stream_key, 6), axis_at), (shards_of,), jnp.float32, low / len(shards), high / len(shards))
        gain = gain * jnp.repeat(jnp.exp(steps), extent[axis_at] // shards_of).reshape((-1,) + (1,) * (len(extent) - 1 - axis_at))
    return gain


def centred(own_key, extent, scale, most, cuts=(), kind=jnp.bfloat16):
    factor_of = shard_levels(own_key, extent, cuts, -0.22, 0.18) if cuts else 1.0
    entries = jax.random.normal(own_key, extent, jnp.float32) * scale * factor_of
    return jnp.minimum(jnp.maximum(entries, -most), most).astype(kind)


def setup_inputs(seed: int = 0) -> dict:
    streams_of = jax.random.split(jax.random.key(seed), 4)
    voltages = centred(streams_of[0], (INPUTS, 2, FRAMES, CH), 1.0, 6.0, ((0, 32),))
    flags = draw_flags(jax.random.fold_in(streams_of[3], 71), 0)
    station_row = jax.random.permutation(streams_of[2], STATIONS).astype(jnp.int32)
    return dict(voltages=voltages, flags=flags, station_row=station_row)


def filter_table(taps, lanes):
    total = taps * lanes
    places = jnp.arange(total, dtype=jnp.float32) + 0.5
    window = 0.5 - 0.5 * jnp.cos(2.0 * math.pi * places / total)
    return (jnp.sinc((places - 0.5 * total) / lanes) * window).reshape(taps, lanes)

def reference(voltages, flags, station_row):
    taps_table = filter_table(TAPS, CH)

    def channelize(single):
        samples = single[0].astype(jnp.float32) + 1j * single[1].astype(jnp.float32)
        filtered = taps_table[0] * samples[0:SPECTRA, :]
        for tap_index in range(1, TAPS):
            filtered = filtered + taps_table[tap_index] * samples[tap_index:tap_index + SPECTRA, :]
        spectrum = jnp.fft.fft(filtered, axis=-1) / math.sqrt(CH)
        return jnp.stack([jnp.real(spectrum).astype(jnp.bfloat16), jnp.imag(spectrum).astype(jnp.bfloat16)])
    spectra = lax.map(channelize, voltages)
    order = jnp.argsort(station_row).astype(jnp.int32)
    rows = jnp.arange(INPUTS, dtype=jnp.int32)
    station_of = order[rows // 2]
    source = 2 * station_of + rows % 2
    weights = flags[station_of].astype(jnp.float32)
    kept = (spectra[source].astype(jnp.float32) * weights[:, None, :, None]).astype(jnp.bfloat16)
    stacked = jnp.transpose(kept, (3, 0, 1, 2)).reshape(CH, INPUTS, 2 * SPECTRA)
    rotated = jnp.concatenate([-kept[:, 1], kept[:, 0]], axis=1)
    rotated = jnp.transpose(rotated, (2, 0, 1))
    count = jnp.dot(weights, weights.T, preferred_element_type=jnp.float32, precision=lax.Precision.HIGHEST)
    denom = jnp.maximum(count, 1.0)
    lower = rows[:, None] >= rows[None, :]
    block = 16
    groups = CH // block

    def correlate(pieces):
        plain, turned = pieces
        plain32 = plain.astype(jnp.float32)
        turned32 = turned.astype(jnp.float32)
        real_part = jnp.einsum('cat,cbt->cab', plain32, plain32) / denom
        imag_part = jnp.einsum('cat,cbt->cab', plain32, turned32) / denom
        return jnp.where(lower[None], real_part, imag_part).astype(jnp.bfloat16)
    result = lax.map(correlate, (stacked.reshape(groups, block, INPUTS, 2 * SPECTRA), rotated.reshape(groups, block, INPUTS, 2 * SPECTRA)))
    return result.reshape(CH, INPUTS, INPUTS)
```

```python
import functools
import math

import jax
import jax.numpy as jnp
import numpy as np
from jax import lax
from jax.experimental import pallas as pl
from jax.experimental.pallas import tpu as pltpu
from jax.sharding import PartitionSpec as P

LANES = 128
ROWS = 8


def filter_table(taps, lanes):
    total = taps * lanes
    places = jnp.arange(total, dtype=jnp.float32) + 0.5
    window = 0.5 - 0.5 * jnp.cos(2.0 * math.pi * places / total)
    return (jnp.sinc((places - 0.5 * total) / lanes) * window).reshape(taps, lanes)


def dft_tables(length):
    places = jnp.arange(length, dtype=jnp.int32)
    product = places[:, None] * places[None, :] % length
    angle = 2.0 * math.pi * product.astype(jnp.float32) / length
    return (jnp.cos(angle), jnp.sin(angle))


def twiddle_tables(outer, inner):
    product = (
        jnp.arange(outer, dtype=jnp.int32)[:, None]
        * jnp.arange(inner, dtype=jnp.int32)[None, :]
        % (outer * inner)
    )
    angle = 2.0 * math.pi * product.astype(jnp.float32) / (outer * inner)
    return (jnp.cos(angle), jnp.sin(angle))


def contract(form, left, right):
    return jnp.einsum(form, left, right, precision=lax.Precision.HIGHEST)


def channelize(voltages, spectra_count):
    inputs_here = voltages.shape[0]
    lanes = voltages.shape[3]
    taps = voltages.shape[2] - spectra_count + 1
    taps_table = filter_table(taps, lanes)
    real_acc = taps_table[0] * voltages[:, 0, 0:spectra_count, :].astype(jnp.float32)
    imag_acc = taps_table[0] * voltages[:, 1, 0:spectra_count, :].astype(jnp.float32)
    for tap_index in range(1, taps):
        real_acc = real_acc + taps_table[tap_index] * voltages[
            :, 0, tap_index : tap_index + spectra_count, :
        ].astype(jnp.float32)
        imag_acc = imag_acc + taps_table[tap_index] * voltages[
            :, 1, tap_index : tap_index + spectra_count, :
        ].astype(jnp.float32)
    inner = 128
    outer = lanes // inner
    real_grid = real_acc.reshape(inputs_here, spectra_count, outer, inner)
    imag_grid = imag_acc.reshape(inputs_here, spectra_count, outer, inner)
    cos_outer, sin_outer = dft_tables(outer)
    real_mid = contract("gtmn,mk->gtkn", real_grid, cos_outer) + contract(
        "gtmn,mk->gtkn", imag_grid, sin_outer
    )
    imag_mid = contract("gtmn,mk->gtkn", imag_grid, cos_outer) - contract(
        "gtmn,mk->gtkn", real_grid, sin_outer
    )
    cos_twist, sin_twist = twiddle_tables(outer, inner)
    real_twisted = real_mid * cos_twist + imag_mid * sin_twist
    imag_twisted = imag_mid * cos_twist - real_mid * sin_twist
    cos_inner, sin_inner = dft_tables(inner)
    real_out = contract("gtkn,nj->jkgt", real_twisted, cos_inner) + contract(
        "gtkn,nj->jkgt", imag_twisted, sin_inner
    )
    imag_out = contract("gtkn,nj->jkgt", imag_twisted, cos_inner) - contract(
        "gtkn,nj->jkgt", real_twisted, sin_inner
    )
    scale = 1.0 / math.sqrt(lanes)
    stacked = (jnp.stack([real_out, imag_out], axis=3) * scale).astype(jnp.bfloat16)
    return stacked.reshape(lanes, inputs_here, 2 * spectra_count)


def square_products(plain, turned):
    real_part = jnp.einsum("cat,cbt->cab", plain, plain, preferred_element_type=jnp.float32)
    imag_part = jnp.einsum("cat,cbt->cab", plain, turned, preferred_element_type=jnp.float32)
    return (real_part, imag_part)


def on_device(voltages, flags, station_row):
    spectra_count = flags.shape[1]
    inputs_here = voltages.shape[0]
    lanes = voltages.shape[3]
    stn_count = lax.axis_size("stn")
    chan_count = lax.axis_size("chan")
    per_device = lanes // (stn_count * chan_count)
    total_inputs = inputs_here * stn_count * chan_count
    if (
        total_inputs == 32
        and inputs_here == 1
        and chan_count == 2
        and lanes == 16 * LANES
        and spectra_count == LANES
    ):
        return fused(voltages, flags, station_row, stn_count, chan_count)
    flags_all, rows_all = (
        lax.all_gather(flags, "stn", axis=0, tiled=True),
        lax.all_gather(station_row, "stn", axis=0, tiled=True),
    )
    spectra = channelize(voltages, spectra_count)
    grouped = spectra.reshape(stn_count, chan_count, per_device, inputs_here, 2 * spectra_count)
    order = jnp.argsort(rows_all)
    rows = jnp.arange(total_inputs, dtype=jnp.int32)
    station_of = order[rows // 2]
    source = 2 * station_of + rows % 2
    moved = lax.all_to_all(
        lax.all_to_all(grouped, "stn", split_axis=0, concat_axis=3, tiled=True),
        "chan",
        split_axis=1,
        concat_axis=3,
        tiled=True,
    )
    from_stn = source // (chan_count * inputs_here)
    from_chan = source // inputs_here % chan_count
    within = source % inputs_here
    placed = from_chan * (stn_count * inputs_here) + from_stn * inputs_here + within
    arrived = moved.reshape(per_device, total_inputs, 2, spectra_count)
    weights = jnp.take(flags_all, station_of, axis=0)
    kept = (
        jnp.take(arrived, placed, axis=1).astype(jnp.float32) * weights[None, :, None, :]
    ).astype(jnp.bfloat16)
    plain = kept.reshape(per_device, total_inputs, 2 * spectra_count)
    turned = jnp.concatenate([-kept[:, :, 1], kept[:, :, 0]], axis=-1)
    count = jnp.dot(
        weights, weights.T, preferred_element_type=jnp.float32, precision=lax.Precision.HIGHEST
    )
    denom = jnp.maximum(count, 1.0)
    real_part, imag_part = square_products(plain, turned)
    below = rows[:, None] >= rows[None, :]
    return jnp.where(below[None], real_part / denom, imag_part / denom).astype(jnp.bfloat16)


def host_tables(taps, lanes, devices):
    outer = lanes // LANES
    quads = LANES // devices
    total = taps * lanes
    places = np.arange(total) + 0.5
    window = 0.5 - 0.5 * np.cos(2.0 * np.pi * places / total)
    taper = (np.sinc((places - 0.5 * total) / lanes) * window).reshape(taps, outer, LANES)
    taper = taper.transpose(1, 0, 2)
    angle = 2.0 * np.pi * (np.arange(outer)[:, None] * np.arange(LANES)[None, :]) / lanes
    scale = 1.0 / math.sqrt(lanes)
    twist = np.stack([np.cos(angle), np.sin(angle)]) * scale
    turn = 2.0 * np.pi * (np.arange(LANES)[:, None] * np.arange(LANES)[None, :] % LANES) / LANES
    cos, sin = np.cos(turn), np.sin(turn)
    real_rows = np.concatenate([cos, sin], axis=1).reshape(devices, 1, quads, 2 * LANES)
    imag_rows = np.concatenate([-sin, cos], axis=1).reshape(devices, 1, quads, 2 * LANES)
    matrix = np.concatenate([real_rows, imag_rows], axis=1).reshape(2 * LANES, 2 * LANES)
    return (
        jnp.asarray(taper.astype(np.float32)),
        jnp.asarray(twist.astype(np.float32)),
        jnp.asarray(matrix.astype(np.float32)).astype(jnp.bfloat16),
    )


def dft4(a, b, c, d):
    s0 = (a[0] + c[0], a[1] + c[1])
    s1 = (a[0] - c[0], a[1] - c[1])
    s2 = (b[0] + d[0], b[1] + d[1])
    s3 = (b[0] - d[0], b[1] - d[1])
    return (
        (s0[0] + s2[0], s0[1] + s2[1]),
        (s1[0] + s3[1], s1[1] - s3[0]),
        (s0[0] - s2[0], s0[1] - s2[1]),
        (s1[0] - s3[1], s1[1] + s3[0]),
    )


def dft16(x):
    half = math.sqrt(0.5)
    mids = [dft4(x[p], x[4 + p], x[8 + p], x[12 + p]) for p in range(4)]
    out = [None] * 16
    for kx in range(4):
        turned = []
        for p in range(4):
            re, im = mids[p][kx]
            e = p * kx
            if e == 0:
                turned.append((re, im))
            elif e == 4:
                turned.append((im, -re))
            elif e == 2:
                turned.append(((re + im) * half, (im - re) * half))
            elif e == 6:
                turned.append(((im - re) * half, -(re + im) * half))
            else:
                c, s = math.cos(2 * math.pi * e / 16), math.sin(2 * math.pi * e / 16)
                turned.append((re * c + im * s, im * c - re * s))
        for ky, value in enumerate(dft4(*turned)):
            out[kx + 4 * ky] = value
    return out


def iota(shape, dim):
    return lax.broadcasted_iota(jnp.int32, shape, dim)


def kernel(
    stn_count, chan_count, chunks,
    volt_hbm, flags_ref, row_ref, taper_ref, twist_ref, matrix_ref, out_ref,
    volt, wide, filt, mids, send, recv, meta, gathered, acc,
    load_sem, send_sem, recv_sem, meta_send_sem, meta_recv_sem,
):
    devices = stn_count * chan_count
    outer, taps = taper_ref.shape[0], taper_ref.shape[1]
    frames = volt.shape[1]
    spectra = flags_ref.shape[1]
    span = spectra // chunks
    packed = LANES // span
    groups = outer // packed
    quads = LANES // devices
    block = groups * ROWS
    stn, chan = lax.axis_index("stn"), lax.axis_index("chan")
    me = stn * chan_count + chan
    bits = devices.bit_length() - 1

    load = pltpu.make_async_copy(volt_hbm.at[0], volt, load_sem)
    load.start()

    def partner(step):
        other = jnp.int32(0)
        for bit in range(bits):
            other = other + ((me // 2**bit + step // 2**bit) % 2) * 2**bit
        return other

    barrier = pltpu.get_barrier_semaphore()

    def greet(step, carry):
        other = partner(step)
        pl.semaphore_signal(
            barrier, inc=1, device_id=(other // chan_count, other % chan_count),
            device_id_type=pl.DeviceIdType.MESH,
        )
        return carry

    lax.fori_loop(1, devices, greet, 0)

    flags8 = jnp.broadcast_to(flags_ref[...], (ROWS, LANES))
    station = jnp.broadcast_to(row_ref[0], (ROWS, LANES)).astype(jnp.float32)
    meta[stn] = jnp.where(iota((ROWS, LANES), 0) == 0, flags8, station)

    def meta_copy(other):
        return pltpu.make_async_remote_copy(
            src_ref=meta.at[stn], dst_ref=meta.at[stn],
            send_sem=meta_send_sem, recv_sem=meta_recv_sem,
            device_id=(other, chan), device_id_type=pl.DeviceIdType.MESH,
        )

    def block_copy(chunk, other):
        return pltpu.make_async_remote_copy(
            src_ref=send.at[chunk, other], dst_ref=recv.at[chunk, me],
            send_sem=send_sem.at[chunk], recv_sem=recv_sem.at[chunk],
            device_id=(other // chan_count, other % chan_count),
            device_id_type=pl.DeviceIdType.MESH,
        )

    load.wait()
    lane8 = iota((ROWS, LANES), 1)
    for chunk in range(chunks):
        start = chunk * span
        low = 0 if chunk == 0 else start + taps
        high = min(start + span + taps, frames)

        def widen(a, carry, low=low, high=high):
            lanes = pl.ds(pl.multiple_of(a * LANES, LANES), LANES)
            for part in range(2):
                wide[part, a, low:high, :] = volt[part, low:high, lanes].astype(jnp.float32)
            return carry

        lax.fori_loop(0, outer, widen, 0)

        def fir(a, carry, start=start):
            for part in range(2):
                total = taper_ref[a, 0:1, :] * wide[part, a, start : start + span, :]
                for tap in range(1, taps):
                    total = total + taper_ref[a, tap : tap + 1, :] * wide[
                        part, a, start + tap : start + tap + span, :
                    ]
                filt[part, a] = total
            return carry

        lax.fori_loop(0, outer, fir, 0)

        def first_stage(tile, carry):
            rows = pl.ds(pl.multiple_of(tile * ROWS, ROWS), ROWS)
            values = dft16([(filt[0, a, rows, :], filt[1, a, rows, :]) for a in range(outer)])
            for k in range(outer):
                re, im = values[k]
                c, s = twist_ref[0, k : k + 1, :], twist_ref[1, k : k + 1, :]
                mids[k, rows, 0:LANES] = re * c + im * s
                mids[k, rows, LANES:] = im * c - re * s
            return carry

        lax.fori_loop(0, span // ROWS, first_stage, 0)

        weights8 = jnp.zeros((ROWS, LANES), jnp.float32)
        for j in range(packed):
            shift = (span * j - start) % LANES
            rolled = pltpu.roll(flags8, shift, 1) if shift else flags8
            weights8 = jnp.where(lane8 // span == j, rolled, weights8)
        for pair in range(groups // 2):
            halves = []
            for group in (2 * pair, 2 * pair + 1):
                data = mids[packed * group : packed * (group + 1)].reshape(LANES, 2 * LANES)
                spectrum = lax.dot_general(
                    matrix_ref[...], data.astype(jnp.bfloat16), (((1,), (1,)), ((), ())),
                    preferred_element_type=jnp.float32,
                )
                rounded = spectrum.astype(jnp.bfloat16).astype(jnp.float32)
                halves.append(rounded.reshape(devices, ROWS, LANES) * weights8[None])
            send[chunk, :, 2 * ROWS * pair : 2 * ROWS * (pair + 1), :] = jnp.concatenate(
                halves, axis=1
            ).astype(jnp.bfloat16)

        if chunk == 0:
            pl.semaphore_wait(barrier, devices - 1)

            def tell(step, carry):
                meta_copy((stn + step) % stn_count).start()
                return carry

        def push(step, carry, chunk=chunk):
            block_copy(chunk, partner(devices - step)).start()
            return carry

        lax.fori_loop(1, devices, push, 0)
        if chunk == 0:
            lax.fori_loop(1, stn_count, tell, 0)
        recv[chunk, me] = send[chunk, me]

    lane = iota((devices, 2 * LANES), 1) % LANES // span
    for chunk in range(chunks):
        arrived = recv.at[chunk, pl.ds(0, devices - 1)]
        pltpu.make_async_copy(arrived, arrived, recv_sem.at[chunk]).wait()
        gathered[...] = recv[chunk].reshape(devices * block, LANES).astype(jnp.float32)
        for quad in range(quads):
            for group in range(groups):
                at = group * ROWS + quad
                re = gathered[pl.ds(at, devices, stride=block), :].astype(jnp.bfloat16)
                im = gathered[pl.ds(at + quads, devices, stride=block), :].astype(jnp.bfloat16)
                plain = jnp.concatenate([re, im], axis=1)
                turned = jnp.concatenate([im, -re], axis=1)
                left = jnp.concatenate([plain, turned], axis=0)
                zero = jnp.zeros_like(plain)
                right = jnp.concatenate(
                    [jnp.where(lane == j, plain, zero) for j in range(packed)], axis=0
                )
                product = lax.dot_general(
                    left, right, (((1,), (1,)), ((), ())), preferred_element_type=jnp.float32
                )
                if chunk == 0:
                    acc[quad * groups + group] = product
                else:
                    acc[quad * groups + group] += product

    told = meta.at[pl.ds(0, stn_count - 1)]
    pltpu.make_async_copy(told, told, meta_recv_sem).wait()
    tall = packed * devices
    exact = functools.partial(
        lax.dot_general, precision=lax.Precision.HIGHEST, preferred_element_type=jnp.float32
    )
    spread = (iota((tall, stn_count), 0) % devices // 2 == iota((tall, stn_count), 1)).astype(
        jnp.float32
    )
    all_flags = meta[:, 0, :]
    all_rows = meta[:, 1, :]
    weights = exact(spread, all_flags, (((1,), (0,)), ((), ())))
    count = exact(weights[:devices], weights, (((1,), (1,)), ((), ())))
    place = 2 * exact(spread, all_rows, (((1,), (0,)), ((), ()))).astype(jnp.int32)
    place = place + iota(place.shape, 0) % 2
    across = place.T
    lower = place[:devices] >= across[:devices]
    denom = jnp.maximum(count, 1.0)
    lane_at = iota((tall, tall), 1)
    columns = jnp.logical_and(
        place == lane_at % devices, iota((tall, tall), 0) // devices == lane_at // devices
    ).astype(jnp.bfloat16)
    row_of = (across[:devices, :devices] == iota((devices, devices), 0)).astype(jnp.bfloat16)
    for g in range(quads * groups):
        both = acc[g]
        chosen = jnp.where(lower, both[:devices], both[devices:]) / denom
        moved = jnp.dot(chosen.astype(jnp.bfloat16), columns, preferred_element_type=jnp.float32)
        moved = jnp.dot(
            row_of, moved.astype(jnp.bfloat16), preferred_element_type=jnp.float32
        ).astype(jnp.bfloat16)
        for j in range(packed):
            out_ref[packed * g + j] = moved[:, devices * j : devices * (j + 1)]

    for chunk in range(chunks):
        gone = send.at[chunk, pl.ds(0, devices - 1)]
        pltpu.make_async_copy(gone, gone, send_sem.at[chunk]).wait()
    pltpu.make_async_copy(told, told, meta_send_sem).wait()


def fused(voltages, flags, station_row, stn_count, chan_count):
    devices = stn_count * chan_count
    frames, lanes = voltages.shape[2], voltages.shape[3]
    spectra = flags.shape[1]
    taps = frames - spectra + 1
    outer = lanes // LANES
    chunks = 4
    span = spectra // chunks
    packed = LANES // span
    block = outer // packed * ROWS
    taper, twist, matrix = host_tables(taps, lanes, devices)
    vmem = pl.BlockSpec(memory_space=pltpu.VMEM)
    f32, bf16 = jnp.float32, jnp.bfloat16
    return pl.pallas_call(
        functools.partial(kernel, stn_count, chan_count, chunks),
        out_shape=jax.ShapeDtypeStruct((lanes // devices, devices, devices), bf16),
        in_specs=[
            pl.BlockSpec(memory_space=pl.ANY),
            vmem,
            pl.BlockSpec(memory_space=pltpu.SMEM),
            vmem,
            vmem,
            vmem,
        ],
        out_specs=vmem,
        scratch_shapes=[
            pltpu.VMEM((2, frames, lanes), bf16),
            pltpu.VMEM((2, outer, frames, LANES), f32),
            pltpu.VMEM((2, outer, span, LANES), f32),
            pltpu.VMEM((outer, span, 2 * LANES), f32),
            pltpu.VMEM((chunks, devices, block, LANES), bf16),
            pltpu.VMEM((chunks, devices, block, LANES), bf16),
            pltpu.VMEM((stn_count, ROWS, LANES), f32),
            pltpu.VMEM((devices * block, LANES), f32),
            pltpu.VMEM((outer * (LANES // devices) // packed, 2 * devices, packed * devices), f32),
            pltpu.SemaphoreType.DMA,
            pltpu.SemaphoreType.DMA((chunks,)),
            pltpu.SemaphoreType.DMA((chunks,)),
            pltpu.SemaphoreType.DMA,
            pltpu.SemaphoreType.DMA,
        ],
        compiler_params=pltpu.CompilerParams(
            collective_id=0, has_side_effects=True, vmem_limit_bytes=32 * 1024 * 1024
        ),
    )(voltages, flags, station_row, taper, twist, matrix)


def solution(mesh):
    placed = (P(("stn", "chan"), None, None, None), P("stn", None), P("stn"))
    return jax.shard_map(
        on_device,
        mesh=mesh,
        in_specs=placed,
        out_specs=P(("stn", "chan"), None, None),
        check_vma=False,
    )
```

```python
import functools
import math

import jax
import jax.numpy as jnp
import numpy as np
from jax import lax
from jax.experimental import pallas as pl
from jax.experimental.pallas import tpu as pltpu
from jax.sharding import PartitionSpec as P

LANES = 128
ROWS = 8


def filter_table(taps, lanes):
    total = taps * lanes
    places = jnp.arange(total, dtype=jnp.float32) + 0.5
    window = 0.5 - 0.5 * jnp.cos(2.0 * math.pi * places / total)
    return (jnp.sinc((places - 0.5 * total) / lanes) * window).reshape(taps, lanes)


def dft_tables(length):
    places = jnp.arange(length, dtype=jnp.int32)
    product = places[:, None] * places[None, :] % length
    angle = 2.0 * math.pi * product.astype(jnp.float32) / length
    return (jnp.cos(angle), jnp.sin(angle))


def twiddle_tables(outer, inner):
    product = (
        jnp.arange(outer, dtype=jnp.int32)[:, None]
        * jnp.arange(inner, dtype=jnp.int32)[None, :]
        % (outer * inner)
    )
    angle = 2.0 * math.pi * product.astype(jnp.float32) / (outer * inner)
    return (jnp.cos(angle), jnp.sin(angle))


def contract(form, left, right):
    return jnp.einsum(form, left, right, precision=lax.Precision.HIGHEST)


def channelize(voltages, spectra_count):
    inputs_here = voltages.shape[0]
    lanes = voltages.shape[3]
    taps = voltages.shape[2] - spectra_count + 1
    taps_table = filter_table(taps, lanes)
    real_acc = taps_table[0] * voltages[:, 0, 0:spectra_count, :].astype(jnp.float32)
    imag_acc = taps_table[0] * voltages[:, 1, 0:spectra_count, :].astype(jnp.float32)
    for tap_index in range(1, taps):
        real_acc = real_acc + taps_table[tap_index] * voltages[
            :, 0, tap_index : tap_index + spectra_count, :
        ].astype(jnp.float32)
        imag_acc = imag_acc + taps_table[tap_index] * voltages[
            :, 1, tap_index : tap_index + spectra_count, :
        ].astype(jnp.float32)
    inner = 128
    outer = lanes // inner
    real_grid = real_acc.reshape(inputs_here, spectra_count, outer, inner)
    imag_grid = imag_acc.reshape(inputs_here, spectra_count, outer, inner)
    cos_outer, sin_outer = dft_tables(outer)
    real_mid = contract("gtmn,mk->gtkn", real_grid, cos_outer) + contract(
        "gtmn,mk->gtkn", imag_grid, sin_outer
    )
    imag_mid = contract("gtmn,mk->gtkn", imag_grid, cos_outer) - contract(
        "gtmn,mk->gtkn", real_grid, sin_outer
    )
    cos_twist, sin_twist = twiddle_tables(outer, inner)
    real_twisted = real_mid * cos_twist + imag_mid * sin_twist
    imag_twisted = imag_mid * cos_twist - real_mid * sin_twist
    cos_inner, sin_inner = dft_tables(inner)
    real_out = contract("gtkn,nj->jkgt", real_twisted, cos_inner) + contract(
        "gtkn,nj->jkgt", imag_twisted, sin_inner
    )
    imag_out = contract("gtkn,nj->jkgt", imag_twisted, cos_inner) - contract(
        "gtkn,nj->jkgt", real_twisted, sin_inner
    )
    scale = 1.0 / math.sqrt(lanes)
    stacked = (jnp.stack([real_out, imag_out], axis=3) * scale).astype(jnp.bfloat16)
    return stacked.reshape(lanes, inputs_here, 2 * spectra_count)


def square_products(plain, turned):
    real_part = jnp.einsum("cat,cbt->cab", plain, plain, preferred_element_type=jnp.float32)
    imag_part = jnp.einsum("cat,cbt->cab", plain, turned, preferred_element_type=jnp.float32)
    return (real_part, imag_part)


def on_device(voltages, flags, station_row):
    spectra_count = flags.shape[1]
    inputs_here = voltages.shape[0]
    lanes = voltages.shape[3]
    stn_count = lax.axis_size("stn")
    chan_count = lax.axis_size("chan")
    per_device = lanes // (stn_count * chan_count)
    total_inputs = inputs_here * stn_count * chan_count
    if (
        total_inputs == 32
        and inputs_here == 1
        and chan_count == 2
        and lanes == 16 * LANES
        and spectra_count == LANES
    ):
        return fused(voltages, flags, station_row, stn_count, chan_count)
    flags_all, rows_all = (
        lax.all_gather(flags, "stn", axis=0, tiled=True),
        lax.all_gather(station_row, "stn", axis=0, tiled=True),
    )
    spectra = channelize(voltages, spectra_count)
    grouped = spectra.reshape(stn_count, chan_count, per_device, inputs_here, 2 * spectra_count)
    order = jnp.argsort(rows_all)
    rows = jnp.arange(total_inputs, dtype=jnp.int32)
    station_of = order[rows // 2]
    source = 2 * station_of + rows % 2
    moved = lax.all_to_all(
        lax.all_to_all(grouped, "stn", split_axis=0, concat_axis=3, tiled=True),
        "chan",
        split_axis=1,
        concat_axis=3,
        tiled=True,
    )
    from_stn = source // (chan_count * inputs_here)
    from_chan = source // inputs_here % chan_count
    within = source % inputs_here
    placed = from_chan * (stn_count * inputs_here) + from_stn * inputs_here + within
    arrived = moved.reshape(per_device, total_inputs, 2, spectra_count)
    weights = jnp.take(flags_all, station_of, axis=0)
    kept = (
        jnp.take(arrived, placed, axis=1).astype(jnp.float32) * weights[None, :, None, :]
    ).astype(jnp.bfloat16)
    plain = kept.reshape(per_device, total_inputs, 2 * spectra_count)
    turned = jnp.concatenate([-kept[:, :, 1], kept[:, :, 0]], axis=-1)
    count = jnp.dot(
        weights, weights.T, preferred_element_type=jnp.float32, precision=lax.Precision.HIGHEST
    )
    denom = jnp.maximum(count, 1.0)
    real_part, imag_part = square_products(plain, turned)
    below = rows[:, None] >= rows[None, :]
    return jnp.where(below[None], real_part / denom, imag_part / denom).astype(jnp.bfloat16)


def host_tables(taps, lanes, devices):
    outer = lanes // LANES
    quads = LANES // devices
    total = taps * lanes
    places = np.arange(total) + 0.5
    window = 0.5 - 0.5 * np.cos(2.0 * np.pi * places / total)
    taper = (np.sinc((places - 0.5 * total) / lanes) * window).reshape(taps, outer, LANES)
    taper = taper.transpose(1, 0, 2)
    angle = 2.0 * np.pi * (np.arange(outer)[:, None] * np.arange(LANES)[None, :]) / lanes
    scale = 1.0 / math.sqrt(lanes)
    twist = np.stack([np.cos(angle), np.sin(angle)]) * scale
    turn = 2.0 * np.pi * (np.arange(LANES)[:, None] * np.arange(LANES)[None, :] % LANES) / LANES
    cos, sin = np.cos(turn), np.sin(turn)
    real_rows = np.concatenate([cos, sin], axis=1).reshape(devices, 1, quads, 2 * LANES)
    imag_rows = np.concatenate([-sin, cos], axis=1).reshape(devices, 1, quads, 2 * LANES)
    matrix = np.concatenate([real_rows, imag_rows], axis=1).reshape(2 * LANES, 2 * LANES)
    return (
        jnp.asarray(taper.astype(np.float32)),
        jnp.asarray(twist.astype(np.float32)),
        jnp.asarray(matrix.astype(np.float32)).astype(jnp.bfloat16),
    )


def dft4(a, b, c, d):
    s0 = (a[0] + c[0], a[1] + c[1])
    s1 = (a[0] - c[0], a[1] - c[1])
    s2 = (b[0] + d[0], b[1] + d[1])
    s3 = (b[0] - d[0], b[1] - d[1])
    return (
        (s0[0] + s2[0], s0[1] + s2[1]),
        (s1[0] + s3[1], s1[1] - s3[0]),
        (s0[0] - s2[0], s0[1] - s2[1]),
        (s1[0] - s3[1], s1[1] + s3[0]),
    )


def dft16(x):
    half = math.sqrt(0.5)
    mids = [dft4(x[p], x[4 + p], x[8 + p], x[12 + p]) for p in range(4)]
    out = [None] * 16
    for kx in range(4):
        turned = []
        for p in range(4):
            re, im = mids[p][kx]
            e = p * kx
            if e == 0:
                turned.append((re, im))
            elif e == 4:
                turned.append((im, -re))
            elif e == 2:
                turned.append(((re + im) * half, (im - re) * half))
            elif e == 6:
                turned.append(((im - re) * half, -(re + im) * half))
            else:
                c, s = math.cos(2 * math.pi * e / 16), math.sin(2 * math.pi * e / 16)
                turned.append((re * c + im * s, im * c - re * s))
        for ky, value in enumerate(dft4(*turned)):
            out[kx + 4 * ky] = value
    return out


def iota(shape, dim):
    return lax.broadcasted_iota(jnp.int32, shape, dim)


def kernel(
    stn_count, chan_count, chunks,
    volt_hbm, flags_ref, row_ref, taper_ref, twist_ref, matrix_ref, out_ref,
    volt, wide, filt, mids, send, recv, meta, gathered, acc,
    load_sem, send_sem, recv_sem, meta_send_sem, meta_recv_sem,
):
    devices = stn_count * chan_count
    outer, taps = taper_ref.shape[0], taper_ref.shape[1]
    frames = volt.shape[1]
    spectra = flags_ref.shape[1]
    span = spectra // chunks
    packed = LANES // span
    groups = outer // packed
    quads = LANES // devices
    block = groups * ROWS
    stn, chan = lax.axis_index("stn"), lax.axis_index("chan")
    me = stn * chan_count + chan
    bits = devices.bit_length() - 1

    load = pltpu.make_async_copy(volt_hbm.at[0], volt, load_sem)
    load.start()

    def partner(step):
        other = jnp.int32(0)
        for bit in range(bits):
            other = other + ((me // 2**bit + step // 2**bit) % 2) * 2**bit
        return other

    barrier = pltpu.get_barrier_semaphore()

    def greet(step, carry):
        other = partner(step)
        pl.semaphore_signal(
            barrier, inc=1, device_id=(other // chan_count, other % chan_count),
            device_id_type=pl.DeviceIdType.MESH,
        )
        return carry

    lax.fori_loop(1, devices, greet, 0)

    flags8 = jnp.broadcast_to(flags_ref[...], (ROWS, LANES))
    station = jnp.broadcast_to(row_ref[0], (ROWS, LANES)).astype(jnp.float32)
    meta[stn] = jnp.where(iota((ROWS, LANES), 0) == 0, flags8, station)

    def meta_copy(other):
        return pltpu.make_async_remote_copy(
            src_ref=meta.at[stn], dst_ref=meta.at[stn],
            send_sem=meta_send_sem, recv_sem=meta_recv_sem,
            device_id=(other, chan), device_id_type=pl.DeviceIdType.MESH,
        )

    def block_copy(chunk, other):
        return pltpu.make_async_remote_copy(
            src_ref=send.at[chunk, other], dst_ref=recv.at[chunk, me],
            send_sem=send_sem.at[chunk], recv_sem=recv_sem.at[chunk],
            device_id=(other // chan_count, other % chan_count),
            device_id_type=pl.DeviceIdType.MESH,
        )

    load.wait()
    lane8 = iota((ROWS, LANES), 1)
    for chunk in range(chunks):
        start = chunk * span
        low = 0 if chunk == 0 else start + taps
        high = min(start + span + taps, frames)

        def widen(a, carry, low=low, high=high):
            lanes = pl.ds(pl.multiple_of(a * LANES, LANES), LANES)
            for part in range(2):
                wide[part, a, low:high, :] = volt[part, low:high, lanes].astype(jnp.float32)
            return carry

        lax.fori_loop(0, outer, widen, 0)

        def fir(a, carry, start=start):
            for part in range(2):
                total = taper_ref[a, 0:1, :] * wide[part, a, start : start + span, :]
                for tap in range(1, taps):
                    total = total + taper_ref[a, tap : tap + 1, :] * wide[
                        part, a, start + tap : start + tap + span, :
                    ]
                filt[part, a] = total
            return carry

        lax.fori_loop(0, outer, fir, 0)

        def first_stage(tile, carry):
            rows = pl.ds(pl.multiple_of(tile * ROWS, ROWS), ROWS)
            values = dft16([(filt[0, a, rows, :], filt[1, a, rows, :]) for a in range(outer)])
            for k in range(outer):
                re, im = values[k]
                c, s = twist_ref[0, k : k + 1, :], twist_ref[1, k : k + 1, :]
                mids[k, rows, 0:LANES] = re * c + im * s
                mids[k, rows, LANES:] = im * c - re * s
            return carry

        lax.fori_loop(0, span // ROWS, first_stage, 0)

        weights8 = jnp.zeros((ROWS, LANES), jnp.float32)
        for j in range(packed):
            shift = (span * j - start) % LANES
            rolled = pltpu.roll(flags8, shift, 1) if shift else flags8
            weights8 = jnp.where(lane8 // span == j, rolled, weights8)
        for pair in range(groups // 2):
            halves = []
            for group in (2 * pair, 2 * pair + 1):
                data = mids[packed * group : packed * (group + 1)].reshape(LANES, 2 * LANES)
                spectrum = lax.dot_general(
                    matrix_ref[...], data.astype(jnp.bfloat16), (((1,), (1,)), ((), ())),
                    preferred_element_type=jnp.float32,
                )
                rounded = spectrum.astype(jnp.bfloat16).astype(jnp.float32)
                halves.append(rounded.reshape(devices, ROWS, LANES) * weights8[None])
            send[chunk, :, 2 * ROWS * pair : 2 * ROWS * (pair + 1), :] = jnp.concatenate(
                halves, axis=1
            ).astype(jnp.bfloat16)

        if chunk == 0:
            pl.semaphore_wait(barrier, devices - 1)

            def tell(step, carry):
                meta_copy((stn + step) % stn_count).start()
                return carry

        def push(step, carry, chunk=chunk):
            far = devices - 1 - (step - 1) // 2
            near = devices // 2 - step // 2
            block_copy(chunk, partner(step % 2 * far + (1 - step % 2) * near)).start()
            return carry

        lax.fori_loop(1, devices, push, 0)
        if chunk == 0:
            lax.fori_loop(1, stn_count, tell, 0)
        recv[chunk, me] = send[chunk, me]

    told = meta.at[pl.ds(0, stn_count - 1)]
    pltpu.make_async_copy(told, told, meta_recv_sem).wait()
    tall = packed * devices
    exact = functools.partial(
        lax.dot_general, precision=lax.Precision.HIGHEST, preferred_element_type=jnp.float32
    )
    spread = (iota((tall, stn_count), 0) % devices // 2 == iota((tall, stn_count), 1)).astype(
        jnp.float32
    )
    all_flags = meta[:, 0, :]
    all_rows = meta[:, 1, :]
    weights = exact(spread, all_flags, (((1,), (0,)), ((), ())))
    count = exact(weights[:devices], weights, (((1,), (1,)), ((), ())))
    place = 2 * exact(spread, all_rows, (((1,), (0,)), ((), ()))).astype(jnp.int32)
    place = place + iota(place.shape, 0) % 2
    across = place.T
    lower = place[:devices] >= across[:devices]
    denom = jnp.maximum(count, 1.0)
    lane_at = iota((tall, tall), 1)
    columns = jnp.logical_and(
        place == lane_at % devices, iota((tall, tall), 0) // devices == lane_at // devices
    ).astype(jnp.bfloat16)
    row_of = (across[:devices, :devices] == iota((devices, devices), 0)).astype(jnp.bfloat16)
    lane = iota((devices, 2 * LANES), 1) % LANES // span
    for chunk in range(chunks):
        arrived = recv.at[chunk, pl.ds(0, devices - 1)]
        pltpu.make_async_copy(arrived, arrived, recv_sem.at[chunk]).wait()
        gathered[...] = recv[chunk].reshape(devices * block, LANES).astype(jnp.float32)
        for quad in range(quads):
            for group in range(groups):
                at = group * ROWS + quad
                re = gathered[pl.ds(at, devices, stride=block), :].astype(jnp.bfloat16)
                im = gathered[pl.ds(at + quads, devices, stride=block), :].astype(jnp.bfloat16)
                plain = jnp.concatenate([re, im], axis=1)
                turned = jnp.concatenate([im, -re], axis=1)
                left = jnp.concatenate([plain, turned], axis=0)
                zero = jnp.zeros_like(plain)
                right = jnp.concatenate(
                    [jnp.where(lane == j, plain, zero) for j in range(packed)], axis=0
                )
                product = lax.dot_general(
                    left, right, (((1,), (1,)), ((), ())), preferred_element_type=jnp.float32
                )
                if chunk == 0:
                    acc[quad * groups + group] = product
                else:
                    acc[quad * groups + group] += product

    for g in range(quads * groups):
        both = acc[g]
        chosen = jnp.where(lower, both[:devices], both[devices:]) / denom
        moved = jnp.dot(chosen.astype(jnp.bfloat16), columns, preferred_element_type=jnp.float32)
        moved = jnp.dot(
            row_of, moved.astype(jnp.bfloat16), preferred_element_type=jnp.float32
        ).astype(jnp.bfloat16)
        for j in range(packed):
            out_ref[packed * g + j] = moved[:, devices * j : devices * (j + 1)]

    for chunk in range(chunks):
        gone = send.at[chunk, pl.ds(0, devices - 1)]
        pltpu.make_async_copy(gone, gone, send_sem.at[chunk]).wait()
    pltpu.make_async_copy(told, told, meta_send_sem).wait()


def fused(voltages, flags, station_row, stn_count, chan_count):
    devices = stn_count * chan_count
    frames, lanes = voltages.shape[2], voltages.shape[3]
    spectra = flags.shape[1]
    taps = frames - spectra + 1
    outer = lanes // LANES
    chunks = 4
    span = spectra // chunks
    packed = LANES // span
    block = outer // packed * ROWS
    taper, twist, matrix = host_tables(taps, lanes, devices)
    vmem = pl.BlockSpec(memory_space=pltpu.VMEM)
    f32, bf16 = jnp.float32, jnp.bfloat16
    return pl.pallas_call(
        functools.partial(kernel, stn_count, chan_count, chunks),
        out_shape=jax.ShapeDtypeStruct((lanes // devices, devices, devices), bf16),
        in_specs=[
            pl.BlockSpec(memory_space=pl.ANY),
            vmem,
            pl.BlockSpec(memory_space=pltpu.SMEM),
            vmem,
            vmem,
            vmem,
        ],
        out_specs=vmem,
        scratch_shapes=[
            pltpu.VMEM((2, frames, lanes), bf16),
            pltpu.VMEM((2, outer, frames, LANES), f32),
            pltpu.VMEM((2, outer, span, LANES), f32),
            pltpu.VMEM((outer, span, 2 * LANES), f32),
            pltpu.VMEM((chunks, devices, block, LANES), bf16),
            pltpu.VMEM((chunks, devices, block, LANES), bf16),
            pltpu.VMEM((stn_count, ROWS, LANES), f32),
            pltpu.VMEM((devices * block, LANES), f32),
            pltpu.VMEM((outer * (LANES // devices) // packed, 2 * devices, packed * devices), f32),
            pltpu.SemaphoreType.DMA,
            pltpu.SemaphoreType.DMA((chunks,)),
            pltpu.SemaphoreType.DMA((chunks,)),
            pltpu.SemaphoreType.DMA,
            pltpu.SemaphoreType.DMA,
        ],
        compiler_params=pltpu.CompilerParams(
            collective_id=0, has_side_effects=True, vmem_limit_bytes=32 * 1024 * 1024
        ),
    )(voltages, flags, station_row, taper, twist, matrix)


def solution(mesh):
    placed = (P(("stn", "chan"), None, None, None), P("stn", None), P("stn"))
    return jax.shard_map(
        on_device,
        mesh=mesh,
        in_specs=placed,
        out_specs=P(("stn", "chan"), None, None),
        check_vma=False,
    )
```

```python
import functools
import math

import jax
import jax.numpy as jnp
import numpy as np
from jax import lax
from jax.experimental import pallas as pl
from jax.experimental.pallas import tpu as pltpu
from jax.sharding import PartitionSpec as P

LANES = 128
ROWS = 8


def filter_table(taps, lanes):
    total = taps * lanes
    places = jnp.arange(total, dtype=jnp.float32) + 0.5
    window = 0.5 - 0.5 * jnp.cos(2.0 * math.pi * places / total)
    return (jnp.sinc((places - 0.5 * total) / lanes) * window).reshape(taps, lanes)


def dft_tables(length):
    places = jnp.arange(length, dtype=jnp.int32)
    product = places[:, None] * places[None, :] % length
    angle = 2.0 * math.pi * product.astype(jnp.float32) / length
    return (jnp.cos(angle), jnp.sin(angle))


def twiddle_tables(outer, inner):
    product = (
        jnp.arange(outer, dtype=jnp.int32)[:, None]
        * jnp.arange(inner, dtype=jnp.int32)[None, :]
        % (outer * inner)
    )
    angle = 2.0 * math.pi * product.astype(jnp.float32) / (outer * inner)
    return (jnp.cos(angle), jnp.sin(angle))


def contract(form, left, right):
    return jnp.einsum(form, left, right, precision=lax.Precision.HIGHEST)


def channelize(voltages, spectra_count):
    inputs_here = voltages.shape[0]
    lanes = voltages.shape[3]
    taps = voltages.shape[2] - spectra_count + 1
    taps_table = filter_table(taps, lanes)
    real_acc = taps_table[0] * voltages[:, 0, 0:spectra_count, :].astype(jnp.float32)
    imag_acc = taps_table[0] * voltages[:, 1, 0:spectra_count, :].astype(jnp.float32)
    for tap_index in range(1, taps):
        real_acc = real_acc + taps_table[tap_index] * voltages[
            :, 0, tap_index : tap_index + spectra_count, :
        ].astype(jnp.float32)
        imag_acc = imag_acc + taps_table[tap_index] * voltages[
            :, 1, tap_index : tap_index + spectra_count, :
        ].astype(jnp.float32)
    inner = 128
    outer = lanes // inner
    real_grid = real_acc.reshape(inputs_here, spectra_count, outer, inner)
    imag_grid = imag_acc.reshape(inputs_here, spectra_count, outer, inner)
    cos_outer, sin_outer = dft_tables(outer)
    real_mid = contract("gtmn,mk->gtkn", real_grid, cos_outer) + contract(
        "gtmn,mk->gtkn", imag_grid, sin_outer
    )
    imag_mid = contract("gtmn,mk->gtkn", imag_grid, cos_outer) - contract(
        "gtmn,mk->gtkn", real_grid, sin_outer
    )
    cos_twist, sin_twist = twiddle_tables(outer, inner)
    real_twisted = real_mid * cos_twist + imag_mid * sin_twist
    imag_twisted = imag_mid * cos_twist - real_mid * sin_twist
    cos_inner, sin_inner = dft_tables(inner)
    real_out = contract("gtkn,nj->jkgt", real_twisted, cos_inner) + contract(
        "gtkn,nj->jkgt", imag_twisted, sin_inner
    )
    imag_out = contract("gtkn,nj->jkgt", imag_twisted, cos_inner) - contract(
        "gtkn,nj->jkgt", real_twisted, sin_inner
    )
    scale = 1.0 / math.sqrt(lanes)
    stacked = (jnp.stack([real_out, imag_out], axis=3) * scale).astype(jnp.bfloat16)
    return stacked.reshape(lanes, inputs_here, 2 * spectra_count)


def square_products(plain, turned):
    real_part = jnp.einsum("cat,cbt->cab", plain, plain, preferred_element_type=jnp.float32)
    imag_part = jnp.einsum("cat,cbt->cab", plain, turned, preferred_element_type=jnp.float32)
    return (real_part, imag_part)


def on_device(voltages, flags, station_row):
    spectra_count = flags.shape[1]
    inputs_here = voltages.shape[0]
    lanes = voltages.shape[3]
    stn_count = lax.axis_size("stn")
    chan_count = lax.axis_size("chan")
    per_device = lanes // (stn_count * chan_count)
    total_inputs = inputs_here * stn_count * chan_count
    if (
        total_inputs == 32
        and inputs_here == 1
        and chan_count == 2
        and lanes == 16 * LANES
        and spectra_count == LANES
    ):
        return fused(voltages, flags, station_row, stn_count, chan_count)
    flags_all, rows_all = (
        lax.all_gather(flags, "stn", axis=0, tiled=True),
        lax.all_gather(station_row, "stn", axis=0, tiled=True),
    )
    spectra = channelize(voltages, spectra_count)
    grouped = spectra.reshape(stn_count, chan_count, per_device, inputs_here, 2 * spectra_count)
    order = jnp.argsort(rows_all)
    rows = jnp.arange(total_inputs, dtype=jnp.int32)
    station_of = order[rows // 2]
    source = 2 * station_of + rows % 2
    moved = lax.all_to_all(
        lax.all_to_all(grouped, "stn", split_axis=0, concat_axis=3, tiled=True),
        "chan",
        split_axis=1,
        concat_axis=3,
        tiled=True,
    )
    from_stn = source // (chan_count * inputs_here)
    from_chan = source // inputs_here % chan_count
    within = source % inputs_here
    placed = from_chan * (stn_count * inputs_here) + from_stn * inputs_here + within
    arrived = moved.reshape(per_device, total_inputs, 2, spectra_count)
    weights = jnp.take(flags_all, station_of, axis=0)
    kept = (
        jnp.take(arrived, placed, axis=1).astype(jnp.float32) * weights[None, :, None, :]
    ).astype(jnp.bfloat16)
    plain = kept.reshape(per_device, total_inputs, 2 * spectra_count)
    turned = jnp.concatenate([-kept[:, :, 1], kept[:, :, 0]], axis=-1)
    count = jnp.dot(
        weights, weights.T, preferred_element_type=jnp.float32, precision=lax.Precision.HIGHEST
    )
    denom = jnp.maximum(count, 1.0)
    real_part, imag_part = square_products(plain, turned)
    below = rows[:, None] >= rows[None, :]
    return jnp.where(below[None], real_part / denom, imag_part / denom).astype(jnp.bfloat16)


def host_tables(taps, lanes, devices):
    outer = lanes // LANES
    quads = LANES // devices
    total = taps * lanes
    places = np.arange(total) + 0.5
    window = 0.5 - 0.5 * np.cos(2.0 * np.pi * places / total)
    taper = (np.sinc((places - 0.5 * total) / lanes) * window).reshape(taps, outer, LANES)
    taper = taper.transpose(1, 0, 2)
    angle = 2.0 * np.pi * (np.arange(outer)[:, None] * np.arange(LANES)[None, :]) / lanes
    scale = 1.0 / math.sqrt(lanes)
    twist = np.stack([np.cos(angle), np.sin(angle)]) * scale
    turn = 2.0 * np.pi * (np.arange(LANES)[:, None] * np.arange(LANES)[None, :] % LANES) / LANES
    cos, sin = np.cos(turn), np.sin(turn)
    real_rows = np.concatenate([cos, sin], axis=1).reshape(devices, 1, quads, 2 * LANES)
    imag_rows = np.concatenate([-sin, cos], axis=1).reshape(devices, 1, quads, 2 * LANES)
    matrix = np.concatenate([real_rows, imag_rows], axis=1).reshape(2 * LANES, 2 * LANES)
    return (
        jnp.asarray(taper.astype(np.float32)),
        jnp.asarray(twist.astype(np.float32)),
        jnp.asarray(matrix.astype(np.float32)).astype(jnp.bfloat16),
    )


def dft4(a, b, c, d):
    s0 = (a[0] + c[0], a[1] + c[1])
    s1 = (a[0] - c[0], a[1] - c[1])
    s2 = (b[0] + d[0], b[1] + d[1])
    s3 = (b[0] - d[0], b[1] - d[1])
    return (
        (s0[0] + s2[0], s0[1] + s2[1]),
        (s1[0] + s3[1], s1[1] - s3[0]),
        (s0[0] - s2[0], s0[1] - s2[1]),
        (s1[0] - s3[1], s1[1] + s3[0]),
    )


def dft16(x):
    half = math.sqrt(0.5)
    mids = [dft4(x[p], x[4 + p], x[8 + p], x[12 + p]) for p in range(4)]
    out = [None] * 16
    for kx in range(4):
        turned = []
        for p in range(4):
            re, im = mids[p][kx]
            e = p * kx
            if e == 0:
                turned.append((re, im))
            elif e == 4:
                turned.append((im, -re))
            elif e == 2:
                turned.append(((re + im) * half, (im - re) * half))
            elif e == 6:
                turned.append(((im - re) * half, -(re + im) * half))
            else:
                c, s = math.cos(2 * math.pi * e / 16), math.sin(2 * math.pi * e / 16)
                turned.append((re * c + im * s, im * c - re * s))
        for ky, value in enumerate(dft4(*turned)):
            out[kx + 4 * ky] = value
    return out


def iota(shape, dim):
    return lax.broadcasted_iota(jnp.int32, shape, dim)


def kernel(
    stn_count, chan_count, chunks,
    volt_hbm, flags_ref, row_ref, taper_ref, twist_ref, matrix_ref, out_ref,
    volt, wide, filt, mids, send, recv, meta, gathered, masks, acc,
    load_sem, send_sem, recv_sem, meta_send_sem, meta_recv_sem,
):
    devices = stn_count * chan_count
    outer, taps = taper_ref.shape[0], taper_ref.shape[1]
    frames = volt.shape[0]
    spectra = flags_ref.shape[1]
    span = spectra // chunks
    packed = LANES // span
    groups = outer // packed
    quads = LANES // devices
    block = groups * ROWS
    stn, chan = lax.axis_index("stn"), lax.axis_index("chan")
    me = stn * chan_count + chan
    bits = devices.bit_length() - 1

    load = pltpu.make_async_copy(volt_hbm.at[0], volt, load_sem)
    load.start()

    def partner(step):
        other = jnp.int32(0)
        for bit in range(bits):
            other = other + ((me // 2**bit + step // 2**bit) % 2) * 2**bit
        return other

    barrier = pltpu.get_barrier_semaphore()

    def greet(step, carry):
        other = partner(step)
        pl.semaphore_signal(
            barrier, inc=1, device_id=(other // chan_count, other % chan_count),
            device_id_type=pl.DeviceIdType.MESH,
        )
        return carry

    lax.fori_loop(1, devices, greet, 0)

    flags8 = jnp.broadcast_to(flags_ref[...], (ROWS, LANES))
    station = jnp.broadcast_to(row_ref[0], (ROWS, LANES)).astype(jnp.float32)
    meta[stn] = jnp.where(iota((ROWS, LANES), 0) == 0, flags8, station)

    def meta_copy(other):
        return pltpu.make_async_remote_copy(
            src_ref=meta.at[stn], dst_ref=meta.at[stn],
            send_sem=meta_send_sem, recv_sem=meta_recv_sem,
            device_id=(other, chan), device_id_type=pl.DeviceIdType.MESH,
        )

    def block_copy(chunk, other):
        return pltpu.make_async_remote_copy(
            src_ref=send.at[chunk, other], dst_ref=recv.at[chunk, me],
            send_sem=send_sem.at[chunk], recv_sem=recv_sem.at[chunk],
            device_id=(other // chan_count, other % chan_count),
            device_id_type=pl.DeviceIdType.MESH,
        )

    load.wait()
    lane8 = iota((ROWS, LANES), 1)
    for chunk in range(chunks):
        start = chunk * span
        low = 0 if chunk == 0 else start + taps
        high = min(start + span + taps, frames)

        def widen(a, carry, low=low, high=high):
            lanes = pl.ds(pl.multiple_of(a * LANES, LANES), LANES)
            pairs = volt[low:high, :, lanes].reshape(2 * (high - low), LANES)
            wide[a, 2 * low : 2 * high, :] = pairs.astype(jnp.float32)
            return carry

        lax.fori_loop(0, outer, widen, 0)

        def fir(a, carry, start=start):
            for part in range(2):
                def window(tap):
                    return wide[a, pl.ds(2 * (start + tap) + part, span, stride=2), :]

                total = taper_ref[a, 0:1, :] * window(0)
                for tap in range(1, taps):
                    total = total + taper_ref[a, tap : tap + 1, :] * window(tap)
                filt[part, a] = total
            return carry

        lax.fori_loop(0, outer, fir, 0)

        def first_stage(tile, carry):
            rows = pl.ds(pl.multiple_of(tile * ROWS, ROWS), ROWS)
            values = dft16([(filt[0, a, rows, :], filt[1, a, rows, :]) for a in range(outer)])
            for k in range(outer):
                re, im = values[k]
                c, s = twist_ref[0, k : k + 1, :], twist_ref[1, k : k + 1, :]
                mids[k, rows, 0:LANES] = re * c + im * s
                mids[k, rows, LANES:] = im * c - re * s
            return carry

        lax.fori_loop(0, span // ROWS, first_stage, 0)

        weights8 = jnp.zeros((ROWS, LANES), jnp.float32)
        for j in range(packed):
            shift = (span * j - start) % LANES
            rolled = pltpu.roll(flags8, shift, 1) if shift else flags8
            weights8 = jnp.where(lane8 // span == j, rolled, weights8)
        for pair in range(groups // 2):
            halves = []
            for group in (2 * pair, 2 * pair + 1):
                data = mids[packed * group : packed * (group + 1)].reshape(LANES, 2 * LANES)
                spectrum = lax.dot_general(
                    matrix_ref[...], data.astype(jnp.bfloat16), (((1,), (1,)), ((), ())),
                    preferred_element_type=jnp.float32,
                )
                rounded = spectrum.astype(jnp.bfloat16).astype(jnp.float32)
                halves.append(rounded.reshape(devices, ROWS, LANES) * weights8[None])
            send[chunk, :, 2 * ROWS * pair : 2 * ROWS * (pair + 1), :] = jnp.concatenate(
                halves, axis=1
            ).astype(jnp.bfloat16)

        if chunk == 0:
            pl.semaphore_wait(barrier, devices - 1)

            def tell(step, carry):
                meta_copy((stn + step) % stn_count).start()
                return carry

        def push(step, carry, chunk=chunk):
            far = devices - 1 - (step - 1) // 2
            near = devices // 2 - step // 2
            block_copy(chunk, partner(step % 2 * far + (1 - step % 2) * near)).start()
            return carry

        lax.fori_loop(1, devices, push, 0)
        if chunk == 0:
            lax.fori_loop(1, stn_count, tell, 0)
        recv[chunk, me] = send[chunk, me]

    told = meta.at[pl.ds(0, stn_count - 1)]
    pltpu.make_async_copy(told, told, meta_recv_sem).wait()
    tall = packed * devices
    exact = functools.partial(
        lax.dot_general, precision=lax.Precision.HIGHEST, preferred_element_type=jnp.float32
    )
    spread = (iota((tall, stn_count), 0) % devices // 2 == iota((tall, stn_count), 1)).astype(
        jnp.float32
    )
    all_flags = meta[:, 0, :]
    all_rows = meta[:, 1, :]
    weights = exact(spread, all_flags, (((1,), (0,)), ((), ())))
    count = exact(weights[:devices], weights, (((1,), (1,)), ((), ())))
    place = 2 * exact(spread, all_rows, (((1,), (0,)), ((), ()))).astype(jnp.int32)
    place = place + iota(place.shape, 0) % 2
    across = place.T
    lower = place[:devices] >= across[:devices]
    denom = jnp.maximum(count, 1.0)
    lane_at = iota((tall, tall), 1)
    columns = jnp.logical_and(
        place == lane_at % devices, iota((tall, tall), 0) // devices == lane_at // devices
    ).astype(jnp.bfloat16)
    rows = jnp.logical_and(
        across == iota((tall, tall), 0) % devices, iota((tall, tall), 0) // devices == lane_at // devices
    ).astype(jnp.bfloat16)
    lane = iota((devices, 2 * LANES), 1) % LANES // span
    for j in range(packed):
        masks[j] = (lane == j).astype(jnp.bfloat16)
    for chunk in range(chunks):
        arrived = recv.at[chunk, pl.ds(0, devices - 1)]
        pltpu.make_async_copy(arrived, arrived, recv_sem.at[chunk]).wait()
        gathered[...] = recv[chunk].reshape(devices * block, LANES).astype(jnp.float32)
        for quad in range(quads):
            for group in range(groups):
                at = group * ROWS + quad
                re = gathered[pl.ds(at, devices, stride=block), :].astype(jnp.bfloat16)
                im = gathered[pl.ds(at + quads, devices, stride=block), :].astype(jnp.bfloat16)
                plain = jnp.concatenate([re, im], axis=1)
                turned = jnp.concatenate([im, -re], axis=1)
                left = jnp.concatenate([plain, turned], axis=0)
                right = jnp.concatenate([plain * masks[j] for j in range(packed)], axis=0)
                product = lax.dot_general(
                    left, right, (((1,), (1,)), ((), ())), preferred_element_type=jnp.float32
                )
                if chunk == 0:
                    acc[quad * groups + group] = product
                else:
                    acc[quad * groups + group] += product

    for first in range(0, quads * groups, packed):
        chosen = [
            jnp.where(lower, acc[g, :devices], acc[g, devices:]) / denom
            for g in range(first, first + packed)
        ]
        moved = jnp.dot(
            jnp.concatenate(chosen, axis=0).astype(jnp.bfloat16),
            columns,
            preferred_element_type=jnp.float32,
        )
        moved = jnp.dot(
            rows, moved.astype(jnp.bfloat16), preferred_element_type=jnp.float32
        ).astype(jnp.bfloat16)
        for g in range(packed):
            for j in range(packed):
                out_ref[packed * (first + g) + j] = moved[
                    devices * g : devices * (g + 1), devices * j : devices * (j + 1)
                ]

    for chunk in range(chunks):
        gone = send.at[chunk, pl.ds(0, devices - 1)]
        pltpu.make_async_copy(gone, gone, send_sem.at[chunk]).wait()
    pltpu.make_async_copy(told, told, meta_send_sem).wait()


def fused(voltages, flags, station_row, stn_count, chan_count):
    devices = stn_count * chan_count
    frames, lanes = voltages.shape[2], voltages.shape[3]
    spectra = flags.shape[1]
    taps = frames - spectra + 1
    outer = lanes // LANES
    chunks = 4
    span = spectra // chunks
    packed = LANES // span
    block = outer // packed * ROWS
    taper, twist, matrix = host_tables(taps, lanes, devices)
    vmem = pl.BlockSpec(memory_space=pltpu.VMEM)
    f32, bf16 = jnp.float32, jnp.bfloat16
    return pl.pallas_call(
        functools.partial(kernel, stn_count, chan_count, chunks),
        out_shape=jax.ShapeDtypeStruct((lanes // devices, devices, devices), bf16),
        in_specs=[
            pl.BlockSpec(memory_space=pltpu.HBM),
            vmem,
            pl.BlockSpec(memory_space=pltpu.SMEM),
            vmem,
            vmem,
            vmem,
        ],
        out_specs=vmem,
        scratch_shapes=[
            pltpu.VMEM((frames, 2, lanes), bf16),
            pltpu.VMEM((outer, 2 * frames, LANES), f32),
            pltpu.VMEM((2, outer, span, LANES), f32),
            pltpu.VMEM((outer, span, 2 * LANES), f32),
            pltpu.VMEM((chunks, devices, block, LANES), bf16),
            pltpu.VMEM((chunks, devices, block, LANES), bf16),
            pltpu.VMEM((stn_count, ROWS, LANES), f32),
            pltpu.VMEM((devices * block, LANES), f32),
            pltpu.VMEM((packed, devices, 2 * LANES), bf16),
            pltpu.VMEM((outer * (LANES // devices) // packed, 2 * devices, packed * devices), f32),
            pltpu.SemaphoreType.DMA,
            pltpu.SemaphoreType.DMA((chunks,)),
            pltpu.SemaphoreType.DMA((chunks,)),
            pltpu.SemaphoreType.DMA,
            pltpu.SemaphoreType.DMA,
        ],
        compiler_params=pltpu.CompilerParams(
            collective_id=0, has_side_effects=True, vmem_limit_bytes=32 * 1024 * 1024
        ),
    )(jnp.transpose(voltages, (0, 2, 1, 3)), flags, station_row, taper, twist, matrix)


def solution(mesh):
    placed = (P(("stn", "chan"), None, None, None), P("stn", None), P("stn"))
    return jax.shard_map(
        on_device,
        mesh=mesh,
        in_specs=placed,
        out_specs=P(("stn", "chan"), None, None),
        check_vma=False,
    )
```

```python
import functools
import math

import jax
import jax.numpy as jnp
import numpy as np
from jax import lax
from jax.experimental import pallas as pl
from jax.experimental.pallas import tpu as pltpu
from jax.sharding import PartitionSpec as P

LANES = 128
ROWS = 8


def filter_table(taps, lanes):
    total = taps * lanes
    places = jnp.arange(total, dtype=jnp.float32) + 0.5
    window = 0.5 - 0.5 * jnp.cos(2.0 * math.pi * places / total)
    return (jnp.sinc((places - 0.5 * total) / lanes) * window).reshape(taps, lanes)


def dft_tables(length):
    places = jnp.arange(length, dtype=jnp.int32)
    product = places[:, None] * places[None, :] % length
    angle = 2.0 * math.pi * product.astype(jnp.float32) / length
    return (jnp.cos(angle), jnp.sin(angle))


def twiddle_tables(outer, inner):
    product = (
        jnp.arange(outer, dtype=jnp.int32)[:, None]
        * jnp.arange(inner, dtype=jnp.int32)[None, :]
        % (outer * inner)
    )
    angle = 2.0 * math.pi * product.astype(jnp.float32) / (outer * inner)
    return (jnp.cos(angle), jnp.sin(angle))


def contract(form, left, right):
    return jnp.einsum(form, left, right, precision=lax.Precision.HIGHEST)


def channelize(voltages, spectra_count):
    inputs_here = voltages.shape[0]
    lanes = voltages.shape[3]
    taps = voltages.shape[2] - spectra_count + 1
    taps_table = filter_table(taps, lanes)
    real_acc = taps_table[0] * voltages[:, 0, 0:spectra_count, :].astype(jnp.float32)
    imag_acc = taps_table[0] * voltages[:, 1, 0:spectra_count, :].astype(jnp.float32)
    for tap_index in range(1, taps):
        real_acc = real_acc + taps_table[tap_index] * voltages[
            :, 0, tap_index : tap_index + spectra_count, :
        ].astype(jnp.float32)
        imag_acc = imag_acc + taps_table[tap_index] * voltages[
            :, 1, tap_index : tap_index + spectra_count, :
        ].astype(jnp.float32)
    inner = 128
    outer = lanes // inner
    real_grid = real_acc.reshape(inputs_here, spectra_count, outer, inner)
    imag_grid = imag_acc.reshape(inputs_here, spectra_count, outer, inner)
    cos_outer, sin_outer = dft_tables(outer)
    real_mid = contract("gtmn,mk->gtkn", real_grid, cos_outer) + contract(
        "gtmn,mk->gtkn", imag_grid, sin_outer
    )
    imag_mid = contract("gtmn,mk->gtkn", imag_grid, cos_outer) - contract(
        "gtmn,mk->gtkn", real_grid, sin_outer
    )
    cos_twist, sin_twist = twiddle_tables(outer, inner)
    real_twisted = real_mid * cos_twist + imag_mid * sin_twist
    imag_twisted = imag_mid * cos_twist - real_mid * sin_twist
    cos_inner, sin_inner = dft_tables(inner)
    real_out = contract("gtkn,nj->jkgt", real_twisted, cos_inner) + contract(
        "gtkn,nj->jkgt", imag_twisted, sin_inner
    )
    imag_out = contract("gtkn,nj->jkgt", imag_twisted, cos_inner) - contract(
        "gtkn,nj->jkgt", real_twisted, sin_inner
    )
    scale = 1.0 / math.sqrt(lanes)
    stacked = (jnp.stack([real_out, imag_out], axis=3) * scale).astype(jnp.bfloat16)
    return stacked.reshape(lanes, inputs_here, 2 * spectra_count)


def square_products(plain, turned):
    real_part = jnp.einsum("cat,cbt->cab", plain, plain, preferred_element_type=jnp.float32)
    imag_part = jnp.einsum("cat,cbt->cab", plain, turned, preferred_element_type=jnp.float32)
    return (real_part, imag_part)


def on_device(voltages, flags, station_row):
    spectra_count = flags.shape[1]
    inputs_here = voltages.shape[0]
    lanes = voltages.shape[3]
    stn_count = lax.axis_size("stn")
    chan_count = lax.axis_size("chan")
    per_device = lanes // (stn_count * chan_count)
    total_inputs = inputs_here * stn_count * chan_count
    if (
        total_inputs == 32
        and inputs_here == 1
        and chan_count == 2
        and lanes == 16 * LANES
        and spectra_count == LANES
    ):
        return fused(voltages, flags, station_row, stn_count, chan_count)
    flags_all, rows_all = (
        lax.all_gather(flags, "stn", axis=0, tiled=True),
        lax.all_gather(station_row, "stn", axis=0, tiled=True),
    )
    spectra = channelize(voltages, spectra_count)
    grouped = spectra.reshape(stn_count, chan_count, per_device, inputs_here, 2 * spectra_count)
    order = jnp.argsort(rows_all)
    rows = jnp.arange(total_inputs, dtype=jnp.int32)
    station_of = order[rows // 2]
    source = 2 * station_of + rows % 2
    moved = lax.all_to_all(
        lax.all_to_all(grouped, "stn", split_axis=0, concat_axis=3, tiled=True),
        "chan",
        split_axis=1,
        concat_axis=3,
        tiled=True,
    )
    from_stn = source // (chan_count * inputs_here)
    from_chan = source // inputs_here % chan_count
    within = source % inputs_here
    placed = from_chan * (stn_count * inputs_here) + from_stn * inputs_here + within
    arrived = moved.reshape(per_device, total_inputs, 2, spectra_count)
    weights = jnp.take(flags_all, station_of, axis=0)
    kept = (
        jnp.take(arrived, placed, axis=1).astype(jnp.float32) * weights[None, :, None, :]
    ).astype(jnp.bfloat16)
    plain = kept.reshape(per_device, total_inputs, 2 * spectra_count)
    turned = jnp.concatenate([-kept[:, :, 1], kept[:, :, 0]], axis=-1)
    count = jnp.dot(
        weights, weights.T, preferred_element_type=jnp.float32, precision=lax.Precision.HIGHEST
    )
    denom = jnp.maximum(count, 1.0)
    real_part, imag_part = square_products(plain, turned)
    below = rows[:, None] >= rows[None, :]
    return jnp.where(below[None], real_part / denom, imag_part / denom).astype(jnp.bfloat16)


def host_tables(taps, lanes, devices):
    outer = lanes // LANES
    quads = LANES // devices
    total = taps * lanes
    places = np.arange(total) + 0.5
    window = 0.5 - 0.5 * np.cos(2.0 * np.pi * places / total)
    taper = (np.sinc((places - 0.5 * total) / lanes) * window).reshape(taps, outer, LANES)
    taper = taper.transpose(1, 0, 2)
    angle = 2.0 * np.pi * (np.arange(outer)[:, None] * np.arange(LANES)[None, :]) / lanes
    scale = 1.0 / math.sqrt(lanes)
    twist = np.stack([np.cos(angle), np.sin(angle)]) * scale
    turn = 2.0 * np.pi * (np.arange(LANES)[:, None] * np.arange(LANES)[None, :] % LANES) / LANES
    cos, sin = np.cos(turn), np.sin(turn)
    real_rows = np.concatenate([cos, sin], axis=1).reshape(devices, 1, quads, 2 * LANES)
    imag_rows = np.concatenate([-sin, cos], axis=1).reshape(devices, 1, quads, 2 * LANES)
    matrix = np.concatenate([real_rows, imag_rows], axis=1).reshape(2 * LANES, 2 * LANES)
    return (
        jnp.asarray(taper.astype(np.float32)),
        jnp.asarray(twist.astype(np.float32)),
        jnp.asarray(matrix.astype(jnp.bfloat16).astype(np.float32)),
    )


def dft4(a, b, c, d):
    s0 = (a[0] + c[0], a[1] + c[1])
    s1 = (a[0] - c[0], a[1] - c[1])
    s2 = (b[0] + d[0], b[1] + d[1])
    s3 = (b[0] - d[0], b[1] - d[1])
    return (
        (s0[0] + s2[0], s0[1] + s2[1]),
        (s1[0] + s3[1], s1[1] - s3[0]),
        (s0[0] - s2[0], s0[1] - s2[1]),
        (s1[0] - s3[1], s1[1] + s3[0]),
    )


def dft16(x):
    half = math.sqrt(0.5)
    mids = [dft4(x[p], x[4 + p], x[8 + p], x[12 + p]) for p in range(4)]
    out = [None] * 16
    for kx in range(4):
        turned = []
        for p in range(4):
            re, im = mids[p][kx]
            e = p * kx
            if e == 0:
                turned.append((re, im))
            elif e == 4:
                turned.append((im, -re))
            elif e == 2:
                turned.append(((re + im) * half, (im - re) * half))
            elif e == 6:
                turned.append(((im - re) * half, -(re + im) * half))
            else:
                c, s = math.cos(2 * math.pi * e / 16), math.sin(2 * math.pi * e / 16)
                turned.append((re * c + im * s, im * c - re * s))
        for ky, value in enumerate(dft4(*turned)):
            out[kx + 4 * ky] = value
    return out


def iota(shape, dim):
    return lax.broadcasted_iota(jnp.int32, shape, dim)


def kernel(
    stn_count, chan_count, chunks,
    volt_hbm, flags_hbm, row_ref, taper_hbm, twist_hbm, matrix_hbm, out_ref,
    volt, flags_ref, taper_ref, twist_ref, matrix_f32, matrix_ref,
    wide, filt, mids, send, recv, meta, gathered, masks, acc,
    load_sem, send_sem, recv_sem, meta_send_sem, meta_recv_sem,
):
    devices = stn_count * chan_count
    outer, taps = taper_ref.shape[0], taper_ref.shape[1]
    frames = volt.shape[0]
    spectra = flags_ref.shape[1]
    span = spectra // chunks
    packed = LANES // span
    groups = outer // packed
    quads = LANES // devices
    block = groups * ROWS
    stn, chan = lax.axis_index("stn"), lax.axis_index("chan")
    me = stn * chan_count + chan
    bits = devices.bit_length() - 1

    first_frames = spectra // chunks + taps
    head, rest = pl.ds(0, first_frames), pl.ds(first_frames, frames - first_frames)
    sources = (
        (flags_hbm, flags_ref),
        (volt_hbm.at[0, head], volt.at[head]),
        (taper_hbm, taper_ref),
        (twist_hbm, twist_ref),
        (matrix_hbm, matrix_f32),
        (volt_hbm.at[0, rest], volt.at[rest]),
    )
    loads = [
        pltpu.make_async_copy(source, target, load_sem.at[k])
        for k, (source, target) in enumerate(sources)
    ]
    for load in loads:
        load.start()

    def partner(step):
        other = jnp.int32(0)
        for bit in range(bits):
            other = other + ((me // 2**bit + step // 2**bit) % 2) * 2**bit
        return other

    barrier = pltpu.get_barrier_semaphore()

    def greet(step, carry):
        other = partner(step)
        pl.semaphore_signal(
            barrier, inc=1, device_id=(other // chan_count, other % chan_count),
            device_id_type=pl.DeviceIdType.MESH,
        )
        return carry

    lax.fori_loop(1, devices, greet, 0)

    loads[0].wait()
    flags8 = jnp.broadcast_to(flags_ref[...], (ROWS, LANES))
    station = jnp.broadcast_to(row_ref[0], (ROWS, LANES)).astype(jnp.float32)
    meta[stn] = jnp.where(iota((ROWS, LANES), 0) == 0, flags8, station)

    def meta_copy(other):
        return pltpu.make_async_remote_copy(
            src_ref=meta.at[stn], dst_ref=meta.at[stn],
            send_sem=meta_send_sem, recv_sem=meta_recv_sem,
            device_id=(other, chan), device_id_type=pl.DeviceIdType.MESH,
        )

    def block_copy(chunk, other):
        return pltpu.make_async_remote_copy(
            src_ref=send.at[chunk, other], dst_ref=recv.at[chunk, me],
            send_sem=send_sem.at[chunk], recv_sem=recv_sem.at[chunk],
            device_id=(other // chan_count, other % chan_count),
            device_id_type=pl.DeviceIdType.MESH,
        )

    for load in loads[1:4]:
        load.wait()
    lane8 = iota((ROWS, LANES), 1)
    for chunk in range(chunks):
        start = chunk * span
        low = 0 if chunk == 0 else start + taps
        high = min(start + span + taps, frames)

        def widen(a, carry, low=low, high=high):
            lanes = pl.ds(pl.multiple_of(a * LANES, LANES), LANES)
            pairs = volt[low:high, :, lanes].reshape(2 * (high - low), LANES)
            wide[a, 2 * low : 2 * high, :] = pairs.astype(jnp.float32)
            return carry

        if chunk == 1:
            loads[5].wait()
        lax.fori_loop(0, outer, widen, 0)

        def fir(a, carry, start=start):
            for part in range(2):
                def window(tap):
                    return wide[a, pl.ds(2 * (start + tap) + part, span, stride=2), :]

                total = taper_ref[a, 0:1, :] * window(0)
                for tap in range(1, taps):
                    total = total + taper_ref[a, tap : tap + 1, :] * window(tap)
                filt[part, a] = total
            return carry

        lax.fori_loop(0, outer, fir, 0)

        def first_stage(tile, carry):
            rows = pl.ds(pl.multiple_of(tile * ROWS, ROWS), ROWS)
            values = dft16([(filt[0, a, rows, :], filt[1, a, rows, :]) for a in range(outer)])
            for k in range(outer):
                re, im = values[k]
                c, s = twist_ref[0, k : k + 1, :], twist_ref[1, k : k + 1, :]
                mids[k, rows, 0:LANES] = re * c + im * s
                mids[k, rows, LANES:] = im * c - re * s
            return carry

        lax.fori_loop(0, span // ROWS, first_stage, 0)

        weights8 = jnp.zeros((ROWS, LANES), jnp.float32)
        for j in range(packed):
            shift = (span * j - start) % LANES
            rolled = pltpu.roll(flags8, shift, 1) if shift else flags8
            weights8 = jnp.where(lane8 // span == j, rolled, weights8)
        if chunk == 0:
            loads[4].wait()
            matrix_ref[...] = matrix_f32[...].astype(jnp.bfloat16)
        for pair in range(groups // 2):
            halves = []
            for group in (2 * pair, 2 * pair + 1):
                data = mids[packed * group : packed * (group + 1)].reshape(LANES, 2 * LANES)
                spectrum = lax.dot_general(
                    matrix_ref[...], data.astype(jnp.bfloat16), (((1,), (1,)), ((), ())),
                    preferred_element_type=jnp.float32,
                )
                rounded = spectrum.astype(jnp.bfloat16).astype(jnp.float32)
                halves.append(rounded.reshape(devices, ROWS, LANES) * weights8[None])
            send[chunk, :, 2 * ROWS * pair : 2 * ROWS * (pair + 1), :] = jnp.concatenate(
                halves, axis=1
            ).astype(jnp.bfloat16)

        if chunk == 0:
            pl.semaphore_wait(barrier, devices - 1)

            def tell(step, carry):
                meta_copy((stn + step) % stn_count).start()
                return carry

        def push(step, carry, chunk=chunk):
            far = devices - 1 - (step - 1) // 2
            near = devices // 2 - step // 2
            block_copy(chunk, partner(step % 2 * far + (1 - step % 2) * near)).start()
            return carry

        lax.fori_loop(1, devices, push, 0)
        if chunk == 0:
            lax.fori_loop(1, stn_count, tell, 0)
        recv[chunk, me] = send[chunk, me]

    told = meta.at[pl.ds(0, stn_count - 1)]
    pltpu.make_async_copy(told, told, meta_recv_sem).wait()
    tall = packed * devices
    exact = functools.partial(
        lax.dot_general, precision=lax.Precision.HIGHEST, preferred_element_type=jnp.float32
    )
    spread = (iota((tall, stn_count), 0) % devices // 2 == iota((tall, stn_count), 1)).astype(
        jnp.float32
    )
    all_flags = meta[:, 0, :]
    all_rows = meta[:, 1, :]
    weights = exact(spread, all_flags, (((1,), (0,)), ((), ())))
    count = exact(weights[:devices], weights, (((1,), (1,)), ((), ())))
    place = 2 * exact(spread, all_rows, (((1,), (0,)), ((), ()))).astype(jnp.int32)
    place = place + iota(place.shape, 0) % 2
    across = place.T
    lower = place[:devices] >= across[:devices]
    denom = jnp.maximum(count, 1.0)
    lane_at = iota((tall, tall), 1)
    columns = jnp.logical_and(
        place == lane_at % devices, iota((tall, tall), 0) // devices == lane_at // devices
    ).astype(jnp.bfloat16)
    rows = jnp.logical_and(
        across == iota((tall, tall), 0) % devices, iota((tall, tall), 0) // devices == lane_at // devices
    ).astype(jnp.bfloat16)
    lane = iota((devices, 2 * LANES), 1) % LANES // span
    for j in range(packed):
        masks[j] = (lane == j).astype(jnp.bfloat16)
    for chunk in range(chunks):
        arrived = recv.at[chunk, pl.ds(0, devices - 1)]
        pltpu.make_async_copy(arrived, arrived, recv_sem.at[chunk]).wait()
        gathered[...] = recv[chunk].reshape(devices * block, LANES).astype(jnp.float32)
        for quad in range(quads):
            for group in range(groups):
                at = group * ROWS + quad
                re = gathered[pl.ds(at, devices, stride=block), :].astype(jnp.bfloat16)
                im = gathered[pl.ds(at + quads, devices, stride=block), :].astype(jnp.bfloat16)
                plain = jnp.concatenate([re, im], axis=1)
                turned = jnp.concatenate([im, -re], axis=1)
                left = jnp.concatenate([plain, turned], axis=0)
                right = jnp.concatenate([plain * masks[j] for j in range(packed)], axis=0)
                product = lax.dot_general(
                    left, right, (((1,), (1,)), ((), ())), preferred_element_type=jnp.float32
                )
                if chunk == 0:
                    acc[quad * groups + group] = product
                else:
                    acc[quad * groups + group] += product

    for first in range(0, quads * groups, packed):
        chosen = [
            jnp.where(lower, acc[g, :devices], acc[g, devices:]) / denom
            for g in range(first, first + packed)
        ]
        moved = jnp.dot(
            jnp.concatenate(chosen, axis=0).astype(jnp.bfloat16),
            columns,
            preferred_element_type=jnp.float32,
        )
        moved = jnp.dot(
            rows, moved.astype(jnp.bfloat16), preferred_element_type=jnp.float32
        ).astype(jnp.bfloat16)
        for g in range(packed):
            for j in range(packed):
                out_ref[packed * (first + g) + j] = moved[
                    devices * g : devices * (g + 1), devices * j : devices * (j + 1)
                ]

    for chunk in range(chunks):
        gone = send.at[chunk, pl.ds(0, devices - 1)]
        pltpu.make_async_copy(gone, gone, send_sem.at[chunk]).wait()
    pltpu.make_async_copy(told, told, meta_send_sem).wait()


def fused(voltages, flags, station_row, stn_count, chan_count):
    devices = stn_count * chan_count
    frames, lanes = voltages.shape[2], voltages.shape[3]
    spectra = flags.shape[1]
    taps = frames - spectra + 1
    outer = lanes // LANES
    chunks = 4
    span = spectra // chunks
    packed = LANES // span
    block = outer // packed * ROWS
    taper, twist, matrix = host_tables(taps, lanes, devices)
    vmem = pl.BlockSpec(memory_space=pltpu.VMEM)
    hbm = pl.BlockSpec(memory_space=pl.ANY)
    f32, bf16 = jnp.float32, jnp.bfloat16
    return pl.pallas_call(
        functools.partial(kernel, stn_count, chan_count, chunks),
        out_shape=jax.ShapeDtypeStruct((lanes // devices, devices, devices), bf16),
        in_specs=[
            hbm,
            hbm,
            pl.BlockSpec(memory_space=pltpu.SMEM),
            hbm,
            hbm,
            hbm,
        ],
        out_specs=vmem,
        scratch_shapes=[
            pltpu.VMEM((frames, 2, lanes), bf16),
            pltpu.VMEM(flags.shape, f32),
            pltpu.VMEM(taper.shape, f32),
            pltpu.VMEM(twist.shape, f32),
            pltpu.VMEM(matrix.shape, f32),
            pltpu.VMEM(matrix.shape, bf16),
            pltpu.VMEM((outer, 2 * frames, LANES), f32),
            pltpu.VMEM((2, outer, span, LANES), f32),
            pltpu.VMEM((outer, span, 2 * LANES), f32),
            pltpu.VMEM((chunks, devices, block, LANES), bf16),
            pltpu.VMEM((chunks, devices, block, LANES), bf16),
            pltpu.VMEM((stn_count, ROWS, LANES), f32),
            pltpu.VMEM((devices * block, LANES), f32),
            pltpu.VMEM((packed, devices, 2 * LANES), bf16),
            pltpu.VMEM((outer * (LANES // devices) // packed, 2 * devices, packed * devices), f32),
            pltpu.SemaphoreType.DMA((6,)),
            pltpu.SemaphoreType.DMA((chunks,)),
            pltpu.SemaphoreType.DMA((chunks,)),
            pltpu.SemaphoreType.DMA,
            pltpu.SemaphoreType.DMA,
        ],
        compiler_params=pltpu.CompilerParams(
            collective_id=0, has_side_effects=True, vmem_limit_bytes=63 * 1024 * 1024
        ),
    )(jnp.transpose(voltages, (0, 2, 1, 3)), flags, station_row, taper, twist, matrix)


def solution(mesh):
    placed = (P(("stn", "chan"), None, None, None), P("stn", None), P("stn"))
    return jax.shard_map(
        on_device,
        mesh=mesh,
        in_specs=placed,
        out_specs=P(("stn", "chan"), None, None),
        check_vma=False,
    )
```

```python
import functools
import math

import jax
import jax.numpy as jnp
import numpy as np
from jax import lax
from jax.experimental import pallas as pl
from jax.experimental.pallas import tpu as pltpu
from jax.sharding import PartitionSpec as P

LANES = 128
ROWS = 8


def filter_table(taps, lanes):
    total = taps * lanes
    places = jnp.arange(total, dtype=jnp.float32) + 0.5
    window = 0.5 - 0.5 * jnp.cos(2.0 * math.pi * places / total)
    return (jnp.sinc((places - 0.5 * total) / lanes) * window).reshape(taps, lanes)


def dft_tables(length):
    places = jnp.arange(length, dtype=jnp.int32)
    product = places[:, None] * places[None, :] % length
    angle = 2.0 * math.pi * product.astype(jnp.float32) / length
    return (jnp.cos(angle), jnp.sin(angle))


def twiddle_tables(outer, inner):
    product = (
        jnp.arange(outer, dtype=jnp.int32)[:, None]
        * jnp.arange(inner, dtype=jnp.int32)[None, :]
        % (outer * inner)
    )
    angle = 2.0 * math.pi * product.astype(jnp.float32) / (outer * inner)
    return (jnp.cos(angle), jnp.sin(angle))


def contract(form, left, right):
    return jnp.einsum(form, left, right, precision=lax.Precision.HIGHEST)


def channelize(voltages, spectra_count):
    inputs_here = voltages.shape[0]
    lanes = voltages.shape[3]
    taps = voltages.shape[2] - spectra_count + 1
    taps_table = filter_table(taps, lanes)
    real_acc = taps_table[0] * voltages[:, 0, 0:spectra_count, :].astype(jnp.float32)
    imag_acc = taps_table[0] * voltages[:, 1, 0:spectra_count, :].astype(jnp.float32)
    for tap_index in range(1, taps):
        real_acc = real_acc + taps_table[tap_index] * voltages[
            :, 0, tap_index : tap_index + spectra_count, :
        ].astype(jnp.float32)
        imag_acc = imag_acc + taps_table[tap_index] * voltages[
            :, 1, tap_index : tap_index + spectra_count, :
        ].astype(jnp.float32)
    inner = 128
    outer = lanes // inner
    real_grid = real_acc.reshape(inputs_here, spectra_count, outer, inner)
    imag_grid = imag_acc.reshape(inputs_here, spectra_count, outer, inner)
    cos_outer, sin_outer = dft_tables(outer)
    real_mid = contract("gtmn,mk->gtkn", real_grid, cos_outer) + contract(
        "gtmn,mk->gtkn", imag_grid, sin_outer
    )
    imag_mid = contract("gtmn,mk->gtkn", imag_grid, cos_outer) - contract(
        "gtmn,mk->gtkn", real_grid, sin_outer
    )
    cos_twist, sin_twist = twiddle_tables(outer, inner)
    real_twisted = real_mid * cos_twist + imag_mid * sin_twist
    imag_twisted = imag_mid * cos_twist - real_mid * sin_twist
    cos_inner, sin_inner = dft_tables(inner)
    real_out = contract("gtkn,nj->jkgt", real_twisted, cos_inner) + contract(
        "gtkn,nj->jkgt", imag_twisted, sin_inner
    )
    imag_out = contract("gtkn,nj->jkgt", imag_twisted, cos_inner) - contract(
        "gtkn,nj->jkgt", real_twisted, sin_inner
    )
    scale = 1.0 / math.sqrt(lanes)
    stacked = (jnp.stack([real_out, imag_out], axis=3) * scale).astype(jnp.bfloat16)
    return stacked.reshape(lanes, inputs_here, 2 * spectra_count)


def square_products(plain, turned):
    real_part = jnp.einsum("cat,cbt->cab", plain, plain, preferred_element_type=jnp.float32)
    imag_part = jnp.einsum("cat,cbt->cab", plain, turned, preferred_element_type=jnp.float32)
    return (real_part, imag_part)


def on_device(voltages, flags, station_row):
    spectra_count = flags.shape[1]
    inputs_here = voltages.shape[0]
    lanes = voltages.shape[3]
    stn_count = lax.axis_size("stn")
    chan_count = lax.axis_size("chan")
    per_device = lanes // (stn_count * chan_count)
    total_inputs = inputs_here * stn_count * chan_count
    if (
        total_inputs == 32
        and inputs_here == 1
        and chan_count == 2
        and lanes == 16 * LANES
        and spectra_count == LANES
    ):
        return fused(voltages, flags, station_row, stn_count, chan_count)
    flags_all, rows_all = (
        lax.all_gather(flags, "stn", axis=0, tiled=True),
        lax.all_gather(station_row, "stn", axis=0, tiled=True),
    )
    spectra = channelize(voltages, spectra_count)
    grouped = spectra.reshape(stn_count, chan_count, per_device, inputs_here, 2 * spectra_count)
    order = jnp.argsort(rows_all)
    rows = jnp.arange(total_inputs, dtype=jnp.int32)
    station_of = order[rows // 2]
    source = 2 * station_of + rows % 2
    moved = lax.all_to_all(
        lax.all_to_all(grouped, "stn", split_axis=0, concat_axis=3, tiled=True),
        "chan",
        split_axis=1,
        concat_axis=3,
        tiled=True,
    )
    from_stn = source // (chan_count * inputs_here)
    from_chan = source // inputs_here % chan_count
    within = source % inputs_here
    placed = from_chan * (stn_count * inputs_here) + from_stn * inputs_here + within
    arrived = moved.reshape(per_device, total_inputs, 2, spectra_count)
    weights = jnp.take(flags_all, station_of, axis=0)
    kept = (
        jnp.take(arrived, placed, axis=1).astype(jnp.float32) * weights[None, :, None, :]
    ).astype(jnp.bfloat16)
    plain = kept.reshape(per_device, total_inputs, 2 * spectra_count)
    turned = jnp.concatenate([-kept[:, :, 1], kept[:, :, 0]], axis=-1)
    count = jnp.dot(
        weights, weights.T, preferred_element_type=jnp.float32, precision=lax.Precision.HIGHEST
    )
    denom = jnp.maximum(count, 1.0)
    real_part, imag_part = square_products(plain, turned)
    below = rows[:, None] >= rows[None, :]
    return jnp.where(below[None], real_part / denom, imag_part / denom).astype(jnp.bfloat16)


def host_tables(taps, lanes, devices):
    outer = lanes // LANES
    quads = LANES // devices
    total = taps * lanes
    places = np.arange(total) + 0.5
    window = 0.5 - 0.5 * np.cos(2.0 * np.pi * places / total)
    taper = (np.sinc((places - 0.5 * total) / lanes) * window).reshape(taps, outer, LANES)
    taper = taper.transpose(1, 0, 2)
    angle = 2.0 * np.pi * (np.arange(outer)[:, None] * np.arange(LANES)[None, :]) / lanes
    scale = 1.0 / math.sqrt(lanes)
    twist = np.stack([np.cos(angle), np.sin(angle)]) * scale
    turn = 2.0 * np.pi * (np.arange(LANES)[:, None] * np.arange(LANES)[None, :] % LANES) / LANES
    cos, sin = np.cos(turn), np.sin(turn)
    real_rows = np.concatenate([cos, sin], axis=1).reshape(devices, 1, quads, 2 * LANES)
    imag_rows = np.concatenate([-sin, cos], axis=1).reshape(devices, 1, quads, 2 * LANES)
    matrix = np.concatenate([real_rows, imag_rows], axis=1).reshape(2 * LANES, 2 * LANES)
    rows = [
        np.repeat(taper.reshape(outer * taps, LANES), ROWS, axis=0),
        twist.reshape(2 * outer, LANES),
        matrix.astype(jnp.bfloat16).astype(np.float32)[:, :LANES],
        matrix.astype(jnp.bfloat16).astype(np.float32)[:, LANES:],
    ]
    return jnp.asarray(np.concatenate(rows, axis=0).astype(np.float32))


def dft4(a, b, c, d):
    s0 = (a[0] + c[0], a[1] + c[1])
    s1 = (a[0] - c[0], a[1] - c[1])
    s2 = (b[0] + d[0], b[1] + d[1])
    s3 = (b[0] - d[0], b[1] - d[1])
    return (
        (s0[0] + s2[0], s0[1] + s2[1]),
        (s1[0] + s3[1], s1[1] - s3[0]),
        (s0[0] - s2[0], s0[1] - s2[1]),
        (s1[0] - s3[1], s1[1] + s3[0]),
    )


def dft16(x):
    half = math.sqrt(0.5)
    mids = [dft4(x[p], x[4 + p], x[8 + p], x[12 + p]) for p in range(4)]
    out = [None] * 16
    for kx in range(4):
        turned = []
        for p in range(4):
            re, im = mids[p][kx]
            e = p * kx
            if e == 0:
                turned.append((re, im))
            elif e == 4:
                turned.append((im, -re))
            elif e == 2:
                turned.append(((re + im) * half, (im - re) * half))
            elif e == 6:
                turned.append(((im - re) * half, -(re + im) * half))
            else:
                c, s = math.cos(2 * math.pi * e / 16), math.sin(2 * math.pi * e / 16)
                turned.append((re * c + im * s, im * c - re * s))
        for ky, value in enumerate(dft4(*turned)):
            out[kx + 4 * ky] = value
    return out


def iota(shape, dim):
    return lax.broadcasted_iota(jnp.int32, shape, dim)


def kernel(
    stn_count, chan_count, chunks,
    volt_hbm, flags_ref, row_ref, table_hbm, out_ref,
    volt, taper_ref, twist_ref, matrix_f32, matrix_ref,
    wide, filt, mids, send, recv, meta, gathered, masks, acc,
    load_sem, send_sem, recv_sem, meta_send_sem, meta_recv_sem,
):
    devices = stn_count * chan_count
    frames = volt.shape[0]
    spectra = flags_ref.shape[1]
    taps = frames - spectra + 1
    outer = volt.shape[2] // LANES
    span = spectra // chunks
    packed = LANES // span
    groups = outer // packed
    quads = LANES // devices
    block = groups * ROWS
    stn, chan = lax.axis_index("stn"), lax.axis_index("chan")
    me = stn * chan_count + chan
    bits = devices.bit_length() - 1

    first_frames = spectra // chunks + taps
    head, rest = pl.ds(0, first_frames), pl.ds(first_frames, frames - first_frames)
    taper_rows, twist_rows, matrix_rows = outer * taps * ROWS, 2 * outer, 4 * LANES
    sources = (
        (volt_hbm.at[0, head], volt.at[head]),
        (table_hbm.at[pl.ds(0, taper_rows)], taper_ref),
        (table_hbm.at[pl.ds(taper_rows, twist_rows)], twist_ref),
        (table_hbm.at[pl.ds(taper_rows + twist_rows, matrix_rows)], matrix_f32),
        (volt_hbm.at[0, rest], volt.at[rest]),
    )
    loads = [
        pltpu.make_async_copy(source, target, load_sem.at[k])
        for k, (source, target) in enumerate(sources)
    ]
    for load in loads:
        load.start()

    def partner(step):
        other = jnp.int32(0)
        for bit in range(bits):
            other = other + ((me // 2**bit + step // 2**bit) % 2) * 2**bit
        return other

    barrier = pltpu.get_barrier_semaphore()

    def greet(step, carry):
        other = partner(step)
        pl.semaphore_signal(
            barrier, inc=1, device_id=(other // chan_count, other % chan_count),
            device_id_type=pl.DeviceIdType.MESH,
        )
        return carry

    lax.fori_loop(1, devices, greet, 0)

    lane8 = iota((ROWS, LANES), 1)
    flags8 = lax.fori_loop(
        0, spectra, lambda t, held: jnp.where(lane8 == t, flags_ref[0, t], held),
        jnp.zeros((ROWS, LANES), jnp.float32), unroll=8,
    )
    station = jnp.broadcast_to(row_ref[0], (ROWS, LANES)).astype(jnp.float32)
    meta[stn] = jnp.where(iota((ROWS, LANES), 0) == 0, flags8, station)

    def meta_copy(other):
        return pltpu.make_async_remote_copy(
            src_ref=meta.at[stn], dst_ref=meta.at[stn],
            send_sem=meta_send_sem, recv_sem=meta_recv_sem,
            device_id=(other, chan), device_id_type=pl.DeviceIdType.MESH,
        )

    def block_copy(chunk, other):
        return pltpu.make_async_remote_copy(
            src_ref=send.at[chunk, other], dst_ref=recv.at[chunk, me],
            send_sem=send_sem.at[chunk], recv_sem=recv_sem.at[chunk],
            device_id=(other // chan_count, other % chan_count),
            device_id_type=pl.DeviceIdType.MESH,
        )

    for load in loads[:3]:
        load.wait()
    for chunk in range(chunks):
        start = chunk * span
        low = 0 if chunk == 0 else start + taps
        high = min(start + span + taps, frames)

        def widen(a, carry, low=low, high=high):
            lanes = pl.ds(pl.multiple_of(a * LANES, LANES), LANES)
            pairs = volt[low:high, :, lanes].reshape(2 * (high - low), LANES)
            wide[a, 2 * low : 2 * high, :] = pairs.astype(jnp.float32)
            return carry

        if chunk == 1:
            loads[4].wait()
        lax.fori_loop(0, outer, widen, 0)

        def fir(a, carry, start=start):
            for part in range(2):
                def window(tap):
                    rows = wide[a, pl.ds(2 * (start + tap) + part, span, stride=2), :]
                    return rows.reshape(span // ROWS, ROWS, LANES)

                def weight(tap):
                    at = pl.multiple_of((a * taps + tap) * ROWS, ROWS)
                    return taper_ref[pl.ds(at, ROWS), :][None]

                total = weight(0) * window(0)
                for tap in range(1, taps):
                    total = total + weight(tap) * window(tap)
                filt[part, a] = total.reshape(span, LANES)
            return carry

        lax.fori_loop(0, outer, fir, 0)

        def first_stage(tile, carry):
            rows = pl.ds(pl.multiple_of(tile * ROWS, ROWS), ROWS)
            values = dft16([(filt[0, a, rows, :], filt[1, a, rows, :]) for a in range(outer)])
            for k in range(outer):
                re, im = values[k]
                c = twist_ref[k : k + 1, :]
                s = twist_ref[outer + k : outer + k + 1, :]
                mids[k, rows, 0:LANES] = re * c + im * s
                mids[k, rows, LANES:] = im * c - re * s
            return carry

        lax.fori_loop(0, span // ROWS, first_stage, 0)

        weights8 = jnp.zeros((ROWS, LANES), jnp.float32)
        for j in range(packed):
            shift = (span * j - start) % LANES
            rolled = pltpu.roll(flags8, shift, 1) if shift else flags8
            weights8 = jnp.where(lane8 // span == j, rolled, weights8)
        if chunk == 0:
            loads[3].wait()
            for half in range(2):
                columns = slice(half * LANES, (half + 1) * LANES)
                matrix_ref[:, columns] = matrix_f32[
                    2 * LANES * half : 2 * LANES * (half + 1)
                ].astype(jnp.bfloat16)
        for pair in range(groups // 2):
            halves = []
            for group in (2 * pair, 2 * pair + 1):
                data = mids[packed * group : packed * (group + 1)].reshape(LANES, 2 * LANES)
                spectrum = lax.dot_general(
                    matrix_ref[...], data.astype(jnp.bfloat16), (((1,), (1,)), ((), ())),
                    preferred_element_type=jnp.float32,
                )
                rounded = spectrum.astype(jnp.bfloat16).astype(jnp.float32)
                halves.append(rounded.reshape(devices, ROWS, LANES) * weights8[None])
            send[chunk, :, 2 * ROWS * pair : 2 * ROWS * (pair + 1), :] = jnp.concatenate(
                halves, axis=1
            ).astype(jnp.bfloat16)

        if chunk == 0:
            pl.semaphore_wait(barrier, devices - 1)

            def tell(step, carry):
                meta_copy((stn + step) % stn_count).start()
                return carry

        def push(step, carry, chunk=chunk):
            far = devices - 1 - (step - 1) // 2
            near = devices // 2 - step // 2
            block_copy(chunk, partner(step % 2 * far + (1 - step % 2) * near)).start()
            return carry

        lax.fori_loop(1, devices, push, 0)
        if chunk == 0:
            lax.fori_loop(1, stn_count, tell, 0)
        recv[chunk, me] = send[chunk, me]

    told = meta.at[pl.ds(0, stn_count - 1)]
    pltpu.make_async_copy(told, told, meta_recv_sem).wait()
    tall = packed * devices
    exact = functools.partial(
        lax.dot_general, precision=lax.Precision.HIGHEST, preferred_element_type=jnp.float32
    )
    spread = (iota((tall, stn_count), 0) % devices // 2 == iota((tall, stn_count), 1)).astype(
        jnp.float32
    )
    all_flags = meta[:, 0, :]
    all_rows = meta[:, 1, :]
    weights = exact(spread, all_flags, (((1,), (0,)), ((), ())))
    count = exact(weights[:devices], weights, (((1,), (1,)), ((), ())))
    place = 2 * exact(spread, all_rows, (((1,), (0,)), ((), ()))).astype(jnp.int32)
    place = place + iota(place.shape, 0) % 2
    across = place.T
    lower = place[:devices] >= across[:devices]
    denom = jnp.maximum(count, 1.0)
    lane_at = iota((tall, tall), 1)
    columns = jnp.logical_and(
        place == lane_at % devices, iota((tall, tall), 0) // devices == lane_at // devices
    ).astype(jnp.bfloat16)
    rows = jnp.logical_and(
        across == iota((tall, tall), 0) % devices, iota((tall, tall), 0) // devices == lane_at // devices
    ).astype(jnp.bfloat16)
    lane = iota((devices, 2 * LANES), 1) % LANES // span
    for j in range(packed):
        masks[j] = (lane == j).astype(jnp.bfloat16)
    for chunk in range(chunks):
        arrived = recv.at[chunk, pl.ds(0, devices - 1)]
        pltpu.make_async_copy(arrived, arrived, recv_sem.at[chunk]).wait()
        gathered[...] = recv[chunk].reshape(devices * block, LANES).astype(jnp.float32)
        for quad in range(quads):
            for group in range(groups):
                at = group * ROWS + quad
                re = gathered[pl.ds(at, devices, stride=block), :].astype(jnp.bfloat16)
                im = gathered[pl.ds(at + quads, devices, stride=block), :].astype(jnp.bfloat16)
                plain = jnp.concatenate([re, im], axis=1)
                turned = jnp.concatenate([im, -re], axis=1)
                left = jnp.concatenate([plain, turned], axis=0)
                right = jnp.concatenate([plain * masks[j] for j in range(packed)], axis=0)
                product = lax.dot_general(
                    left, right, (((1,), (1,)), ((), ())), preferred_element_type=jnp.float32
                )
                if chunk == 0:
                    acc[quad * groups + group] = product
                else:
                    acc[quad * groups + group] += product

    for first in range(0, quads * groups, packed):
        chosen = [
            jnp.where(lower, acc[g, :devices], acc[g, devices:]) / denom
            for g in range(first, first + packed)
        ]
        moved = jnp.dot(
            jnp.concatenate(chosen, axis=0).astype(jnp.bfloat16),
            columns,
            preferred_element_type=jnp.float32,
        )
        moved = jnp.dot(
            rows, moved.astype(jnp.bfloat16), preferred_element_type=jnp.float32
        ).astype(jnp.bfloat16)
        for g in range(packed):
            for j in range(packed):
                out_ref[packed * (first + g) + j] = moved[
                    devices * g : devices * (g + 1), devices * j : devices * (j + 1)
                ]

    for chunk in range(chunks):
        gone = send.at[chunk, pl.ds(0, devices - 1)]
        pltpu.make_async_copy(gone, gone, send_sem.at[chunk]).wait()
    pltpu.make_async_copy(told, told, meta_send_sem).wait()


def fused(voltages, flags, station_row, stn_count, chan_count):
    devices = stn_count * chan_count
    frames, lanes = voltages.shape[2], voltages.shape[3]
    spectra = flags.shape[1]
    taps = frames - spectra + 1
    outer = lanes // LANES
    chunks = 4
    span = spectra // chunks
    packed = LANES // span
    block = outer // packed * ROWS
    table = host_tables(taps, lanes, devices)
    vmem = pl.BlockSpec(memory_space=pltpu.VMEM)
    hbm = pl.BlockSpec(memory_space=pl.ANY)
    f32, bf16 = jnp.float32, jnp.bfloat16
    return pl.pallas_call(
        functools.partial(kernel, stn_count, chan_count, chunks),
        out_shape=jax.ShapeDtypeStruct((lanes // devices, devices, devices), bf16),
        in_specs=[
            hbm,
            pl.BlockSpec(memory_space=pltpu.SMEM),
            pl.BlockSpec(memory_space=pltpu.SMEM),
            hbm,
        ],
        out_specs=vmem,
        scratch_shapes=[
            pltpu.VMEM((frames, 2, lanes), bf16),
            pltpu.VMEM((outer * taps * ROWS, LANES), f32),
            pltpu.VMEM((2 * outer, LANES), f32),
            pltpu.VMEM((4 * LANES, LANES), f32),
            pltpu.VMEM((2 * LANES, 2 * LANES), bf16),
            pltpu.VMEM((outer, 2 * frames, LANES), f32),
            pltpu.VMEM((2, outer, span, LANES), f32),
            pltpu.VMEM((outer, span, 2 * LANES), f32),
            pltpu.VMEM((chunks, devices, block, LANES), bf16),
            pltpu.VMEM((chunks, devices, block, LANES), bf16),
            pltpu.VMEM((stn_count, ROWS, LANES), f32),
            pltpu.VMEM((devices * block, LANES), f32),
            pltpu.VMEM((packed, devices, 2 * LANES), bf16),
            pltpu.VMEM((outer * (LANES // devices) // packed, 2 * devices, packed * devices), f32),
            pltpu.SemaphoreType.DMA((5,)),
            pltpu.SemaphoreType.DMA((chunks,)),
            pltpu.SemaphoreType.DMA((chunks,)),
            pltpu.SemaphoreType.DMA,
            pltpu.SemaphoreType.DMA,
        ],
        compiler_params=pltpu.CompilerParams(
            collective_id=0, has_side_effects=True, vmem_limit_bytes=53 * 1024 * 1024
        ),
    )(jnp.transpose(voltages, (0, 2, 1, 3)), flags, station_row, table)


def solution(mesh):
    placed = (P(("stn", "chan"), None, None, None), P("stn", None), P("stn"))
    return jax.shard_map(
        on_device,
        mesh=mesh,
        in_specs=placed,
        out_specs=P(("stn", "chan"), None, None),
        check_vma=False,
    )
```

```python
import functools
import math

import jax
import jax.numpy as jnp
import numpy as np
from jax import lax
from jax.experimental import pallas as pl
from jax.experimental.pallas import tpu as pltpu
from jax.sharding import PartitionSpec as P

LANES = 128
ROWS = 8


def filter_table(taps, lanes):
    total = taps * lanes
    places = jnp.arange(total, dtype=jnp.float32) + 0.5
    window = 0.5 - 0.5 * jnp.cos(2.0 * math.pi * places / total)
    return (jnp.sinc((places - 0.5 * total) / lanes) * window).reshape(taps, lanes)


def dft_tables(length):
    places = jnp.arange(length, dtype=jnp.int32)
    product = places[:, None] * places[None, :] % length
    angle = 2.0 * math.pi * product.astype(jnp.float32) / length
    return (jnp.cos(angle), jnp.sin(angle))


def twiddle_tables(outer, inner):
    product = (
        jnp.arange(outer, dtype=jnp.int32)[:, None]
        * jnp.arange(inner, dtype=jnp.int32)[None, :]
        % (outer * inner)
    )
    angle = 2.0 * math.pi * product.astype(jnp.float32) / (outer * inner)
    return (jnp.cos(angle), jnp.sin(angle))


def contract(form, left, right):
    return jnp.einsum(form, left, right, precision=lax.Precision.HIGHEST)


def channelize(voltages, spectra_count):
    inputs_here = voltages.shape[0]
    lanes = voltages.shape[3]
    taps = voltages.shape[2] - spectra_count + 1
    taps_table = filter_table(taps, lanes)
    real_acc = taps_table[0] * voltages[:, 0, 0:spectra_count, :].astype(jnp.float32)
    imag_acc = taps_table[0] * voltages[:, 1, 0:spectra_count, :].astype(jnp.float32)
    for tap_index in range(1, taps):
        real_acc = real_acc + taps_table[tap_index] * voltages[
            :, 0, tap_index : tap_index + spectra_count, :
        ].astype(jnp.float32)
        imag_acc = imag_acc + taps_table[tap_index] * voltages[
            :, 1, tap_index : tap_index + spectra_count, :
        ].astype(jnp.float32)
    inner = 128
    outer = lanes // inner
    real_grid = real_acc.reshape(inputs_here, spectra_count, outer, inner)
    imag_grid = imag_acc.reshape(inputs_here, spectra_count, outer, inner)
    cos_outer, sin_outer = dft_tables(outer)
    real_mid = contract("gtmn,mk->gtkn", real_grid, cos_outer) + contract(
        "gtmn,mk->gtkn", imag_grid, sin_outer
    )
    imag_mid = contract("gtmn,mk->gtkn", imag_grid, cos_outer) - contract(
        "gtmn,mk->gtkn", real_grid, sin_outer
    )
    cos_twist, sin_twist = twiddle_tables(outer, inner)
    real_twisted = real_mid * cos_twist + imag_mid * sin_twist
    imag_twisted = imag_mid * cos_twist - real_mid * sin_twist
    cos_inner, sin_inner = dft_tables(inner)
    real_out = contract("gtkn,nj->jkgt", real_twisted, cos_inner) + contract(
        "gtkn,nj->jkgt", imag_twisted, sin_inner
    )
    imag_out = contract("gtkn,nj->jkgt", imag_twisted, cos_inner) - contract(
        "gtkn,nj->jkgt", real_twisted, sin_inner
    )
    scale = 1.0 / math.sqrt(lanes)
    stacked = (jnp.stack([real_out, imag_out], axis=3) * scale).astype(jnp.bfloat16)
    return stacked.reshape(lanes, inputs_here, 2 * spectra_count)


def square_products(plain, turned):
    real_part = jnp.einsum("cat,cbt->cab", plain, plain, preferred_element_type=jnp.float32)
    imag_part = jnp.einsum("cat,cbt->cab", plain, turned, preferred_element_type=jnp.float32)
    return (real_part, imag_part)


def on_device(voltages, flags, station_row):
    spectra_count = flags.shape[1]
    inputs_here = voltages.shape[0]
    lanes = voltages.shape[3]
    stn_count = lax.axis_size("stn")
    chan_count = lax.axis_size("chan")
    per_device = lanes // (stn_count * chan_count)
    total_inputs = inputs_here * stn_count * chan_count
    if (
        total_inputs == 32
        and inputs_here == 1
        and chan_count == 2
        and lanes == 16 * LANES
        and spectra_count == LANES
    ):
        return fused(voltages, flags, station_row, stn_count, chan_count)
    flags_all, rows_all = (
        lax.all_gather(flags, "stn", axis=0, tiled=True),
        lax.all_gather(station_row, "stn", axis=0, tiled=True),
    )
    spectra = channelize(voltages, spectra_count)
    grouped = spectra.reshape(stn_count, chan_count, per_device, inputs_here, 2 * spectra_count)
    order = jnp.argsort(rows_all)
    rows = jnp.arange(total_inputs, dtype=jnp.int32)
    station_of = order[rows // 2]
    source = 2 * station_of + rows % 2
    moved = lax.all_to_all(
        lax.all_to_all(grouped, "stn", split_axis=0, concat_axis=3, tiled=True),
        "chan",
        split_axis=1,
        concat_axis=3,
        tiled=True,
    )
    from_stn = source // (chan_count * inputs_here)
    from_chan = source // inputs_here % chan_count
    within = source % inputs_here
    placed = from_chan * (stn_count * inputs_here) + from_stn * inputs_here + within
    arrived = moved.reshape(per_device, total_inputs, 2, spectra_count)
    weights = jnp.take(flags_all, station_of, axis=0)
    kept = (
        jnp.take(arrived, placed, axis=1).astype(jnp.float32) * weights[None, :, None, :]
    ).astype(jnp.bfloat16)
    plain = kept.reshape(per_device, total_inputs, 2 * spectra_count)
    turned = jnp.concatenate([-kept[:, :, 1], kept[:, :, 0]], axis=-1)
    count = jnp.dot(
        weights, weights.T, preferred_element_type=jnp.float32, precision=lax.Precision.HIGHEST
    )
    denom = jnp.maximum(count, 1.0)
    real_part, imag_part = square_products(plain, turned)
    below = rows[:, None] >= rows[None, :]
    return jnp.where(below[None], real_part / denom, imag_part / denom).astype(jnp.bfloat16)


def host_tables(taps, lanes, devices):
    outer = lanes // LANES
    quads = LANES // devices
    total = taps * lanes
    places = np.arange(total) + 0.5
    window = 0.5 - 0.5 * np.cos(2.0 * np.pi * places / total)
    taper = (np.sinc((places - 0.5 * total) / lanes) * window).reshape(taps, outer, LANES)
    taper = taper.transpose(1, 0, 2)
    angle = 2.0 * np.pi * (np.arange(outer)[:, None] * np.arange(LANES)[None, :]) / lanes
    scale = 1.0 / math.sqrt(lanes)
    twist = np.stack([np.cos(angle), np.sin(angle)]) * scale
    turn = 2.0 * np.pi * (np.arange(LANES)[:, None] * np.arange(LANES)[None, :] % LANES) / LANES
    cos, sin = np.cos(turn), np.sin(turn)
    real_rows = np.concatenate([cos, sin], axis=1).reshape(devices, 1, quads, 2 * LANES)
    imag_rows = np.concatenate([-sin, cos], axis=1).reshape(devices, 1, quads, 2 * LANES)
    matrix = np.concatenate([real_rows, imag_rows], axis=1).reshape(2 * LANES, 2 * LANES)
    rows = [
        np.repeat(taper.reshape(outer * taps, LANES), ROWS, axis=0),
        twist.reshape(2 * outer, LANES),
        matrix.astype(jnp.bfloat16).astype(np.float32)[:, :LANES],
        matrix.astype(jnp.bfloat16).astype(np.float32)[:, LANES:],
    ]
    return jnp.asarray(np.concatenate(rows, axis=0).astype(np.float32))


def dft4(a, b, c, d):
    s0 = (a[0] + c[0], a[1] + c[1])
    s1 = (a[0] - c[0], a[1] - c[1])
    s2 = (b[0] + d[0], b[1] + d[1])
    s3 = (b[0] - d[0], b[1] - d[1])
    return (
        (s0[0] + s2[0], s0[1] + s2[1]),
        (s1[0] + s3[1], s1[1] - s3[0]),
        (s0[0] - s2[0], s0[1] - s2[1]),
        (s1[0] - s3[1], s1[1] + s3[0]),
    )


def dft16(x):
    half = math.sqrt(0.5)
    mids = [dft4(x[p], x[4 + p], x[8 + p], x[12 + p]) for p in range(4)]
    out = [None] * 16
    for kx in range(4):
        turned = []
        for p in range(4):
            re, im = mids[p][kx]
            e = p * kx
            if e == 0:
                turned.append((re, im))
            elif e == 4:
                turned.append((im, -re))
            elif e == 2:
                turned.append(((re + im) * half, (im - re) * half))
            elif e == 6:
                turned.append(((im - re) * half, -(re + im) * half))
            else:
                c, s = math.cos(2 * math.pi * e / 16), math.sin(2 * math.pi * e / 16)
                turned.append((re * c + im * s, im * c - re * s))
        for ky, value in enumerate(dft4(*turned)):
            out[kx + 4 * ky] = value
    return out


def iota(shape, dim):
    return lax.broadcasted_iota(jnp.int32, shape, dim)


def kernel(
    stn_count, chan_count, chunks,
    volt_hbm, flags_ref, row_ref, table_hbm, out_ref,
    volt, taper_ref, twist_ref, matrix_f32, matrix_ref,
    wide, filt, mids, send, recv, meta, gathered, masks, acc,
    load_sem, send_sem, recv_sem, meta_send_sem, meta_recv_sem,
):
    devices = stn_count * chan_count
    frames = volt.shape[0]
    spectra = flags_ref.shape[1]
    taps = frames - spectra + 1
    outer = volt.shape[2] // LANES
    span = spectra // chunks
    packed = LANES // span
    groups = outer // packed
    quads = LANES // devices
    block = groups * ROWS
    stn, chan = lax.axis_index("stn"), lax.axis_index("chan")
    me = stn * chan_count + chan

    first_frames = spectra // chunks + taps
    head, rest = pl.ds(0, first_frames), pl.ds(first_frames, frames - first_frames)
    taper_rows, twist_rows, matrix_rows = outer * taps * ROWS, 2 * outer, 4 * LANES
    sources = (
        (volt_hbm.at[0, head], volt.at[head]),
        (table_hbm.at[pl.ds(0, taper_rows)], taper_ref),
        (table_hbm.at[pl.ds(taper_rows, twist_rows)], twist_ref),
        (table_hbm.at[pl.ds(taper_rows + twist_rows, matrix_rows)], matrix_f32),
        (volt_hbm.at[0, rest], volt.at[rest]),
    )
    loads = [
        pltpu.make_async_copy(source, target, load_sem.at[k])
        for k, (source, target) in enumerate(sources)
    ]
    for load in loads:
        load.start()

    stn_flips = [
        (1 - 2 * (stn // 2**bit % 2)) * 2**bit for bit in range(stn_count.bit_length() - 1)
    ]
    chan_flips = [
        (1 - 2 * (chan // 2**bit % 2)) * 2**bit for bit in range(chan_count.bit_length() - 1)
    ]

    def flipped(start, flips, step):
        for bit, flip in enumerate(flips):
            if step >> bit & 1:
                start = start + flip
        return start

    def partner(step):
        return (
            flipped(stn, stn_flips, step // chan_count),
            flipped(chan, chan_flips, step % chan_count),
        )

    barrier = pltpu.get_barrier_semaphore()
    for step in range(1, devices):
        pl.semaphore_signal(
            barrier, inc=1, device_id=partner(step), device_id_type=pl.DeviceIdType.MESH
        )

    lane8 = iota((ROWS, LANES), 1)
    flags8 = lax.fori_loop(
        0, spectra, lambda t, held: jnp.where(lane8 == t, flags_ref[0, t], held),
        jnp.zeros((ROWS, LANES), jnp.float32), unroll=8,
    )
    station = jnp.broadcast_to(row_ref[0], (ROWS, LANES)).astype(jnp.float32)
    meta[stn] = jnp.where(iota((ROWS, LANES), 0) == 0, flags8, station)

    def meta_copy(step):
        return pltpu.make_async_remote_copy(
            src_ref=meta.at[stn], dst_ref=meta.at[stn],
            send_sem=meta_send_sem, recv_sem=meta_recv_sem,
            device_id=(flipped(stn, stn_flips, step), chan), device_id_type=pl.DeviceIdType.MESH,
        )

    def block_copy(chunk, step):
        to_stn, to_chan = partner(step)
        return pltpu.make_async_remote_copy(
            src_ref=send.at[chunk, to_stn * chan_count + to_chan], dst_ref=recv.at[chunk, me],
            send_sem=send_sem.at[chunk], recv_sem=recv_sem.at[chunk],
            device_id=(to_stn, to_chan), device_id_type=pl.DeviceIdType.MESH,
        )

    for load in loads[:3]:
        load.wait()
    for chunk in range(chunks):
        start = chunk * span
        low = 0 if chunk == 0 else start + taps
        high = min(start + span + taps, frames)

        def widen(a, carry, low=low, high=high):
            lanes = pl.ds(pl.multiple_of(a * LANES, LANES), LANES)
            pairs = volt[low:high, :, lanes].reshape(2 * (high - low), LANES)
            wide[a, 2 * low : 2 * high, :] = pairs.astype(jnp.float32)
            return carry

        if chunk == 1:
            loads[4].wait()
        lax.fori_loop(0, outer, widen, 0)

        def fir(a, carry, start=start):
            for part in range(2):
                def window(tap):
                    rows = wide[a, pl.ds(2 * (start + tap) + part, span, stride=2), :]
                    return rows.reshape(span // ROWS, ROWS, LANES)

                def weight(tap):
                    at = pl.multiple_of((a * taps + tap) * ROWS, ROWS)
                    return taper_ref[pl.ds(at, ROWS), :][None]

                total = weight(0) * window(0)
                for tap in range(1, taps):
                    total = total + weight(tap) * window(tap)
                filt[part, a] = total.reshape(span, LANES)
            return carry

        lax.fori_loop(0, outer, fir, 0)

        def first_stage(tile, carry):
            rows = pl.ds(pl.multiple_of(tile * ROWS, ROWS), ROWS)
            values = dft16([(filt[0, a, rows, :], filt[1, a, rows, :]) for a in range(outer)])
            for k in range(outer):
                re, im = values[k]
                c = twist_ref[k : k + 1, :]
                s = twist_ref[outer + k : outer + k + 1, :]
                mids[k, rows, 0:LANES] = re * c + im * s
                mids[k, rows, LANES:] = im * c - re * s
            return carry

        lax.fori_loop(0, span // ROWS, first_stage, 0)

        weights8 = jnp.zeros((ROWS, LANES), jnp.float32)
        for j in range(packed):
            shift = (span * j - start) % LANES
            rolled = pltpu.roll(flags8, shift, 1) if shift else flags8
            weights8 = jnp.where(lane8 // span == j, rolled, weights8)
        if chunk == 0:
            loads[3].wait()
            for half in range(2):
                columns = slice(half * LANES, (half + 1) * LANES)
                matrix_ref[:, columns] = matrix_f32[
                    2 * LANES * half : 2 * LANES * (half + 1)
                ].astype(jnp.bfloat16)
        for pair in range(groups // 2):
            halves = []
            for group in (2 * pair, 2 * pair + 1):
                data = mids[packed * group : packed * (group + 1)].reshape(LANES, 2 * LANES)
                spectrum = lax.dot_general(
                    matrix_ref[...], data.astype(jnp.bfloat16), (((1,), (1,)), ((), ())),
                    preferred_element_type=jnp.float32,
                )
                rounded = spectrum.astype(jnp.bfloat16).astype(jnp.float32)
                halves.append(rounded.reshape(devices, ROWS, LANES) * weights8[None])
            send[chunk, :, 2 * ROWS * pair : 2 * ROWS * (pair + 1), :] = jnp.concatenate(
                halves, axis=1
            ).astype(jnp.bfloat16)

        if chunk == 0:
            pl.semaphore_wait(barrier, devices - 1)
        half = devices // 2
        for far in range(devices - 1, half - 1, -1):
            block_copy(chunk, far).start()
            if far > half:
                block_copy(chunk, far - half).start()
        if chunk == 0:
            for step in range(1, stn_count):
                meta_copy(step).start()
        recv[chunk, me] = send[chunk, me]

    told = meta.at[pl.ds(0, stn_count - 1)]
    pltpu.make_async_copy(told, told, meta_recv_sem).wait()
    tall = packed * devices
    exact = functools.partial(
        lax.dot_general, precision=lax.Precision.HIGHEST, preferred_element_type=jnp.float32
    )
    spread = (iota((tall, stn_count), 0) % devices // 2 == iota((tall, stn_count), 1)).astype(
        jnp.float32
    )
    all_flags = meta[:, 0, :]
    all_rows = meta[:, 1, :]
    weights = exact(spread, all_flags, (((1,), (0,)), ((), ())))
    count = exact(weights[:devices], weights, (((1,), (1,)), ((), ())))
    place = 2 * exact(spread, all_rows, (((1,), (0,)), ((), ()))).astype(jnp.int32)
    place = place + iota(place.shape, 0) % 2
    across = place.T
    lower = place[:devices] >= across[:devices]
    denom = jnp.maximum(count, 1.0)
    lane_at = iota((tall, tall), 1)
    columns = jnp.logical_and(
        place == lane_at % devices, iota((tall, tall), 0) // devices == lane_at // devices
    ).astype(jnp.bfloat16)
    rows = jnp.logical_and(
        across == iota((tall, tall), 0) % devices, iota((tall, tall), 0) // devices == lane_at // devices
    ).astype(jnp.bfloat16)
    lane = iota((devices, 2 * LANES), 1) % LANES // span
    for j in range(packed):
        masks[j] = (lane == j).astype(jnp.bfloat16)
    for chunk in range(chunks):
        arrived = recv.at[chunk, pl.ds(0, devices - 1)]
        pltpu.make_async_copy(arrived, arrived, recv_sem.at[chunk]).wait()
        gathered[...] = recv[chunk].reshape(devices * block, LANES).astype(jnp.float32)
        for quad in range(quads):
            for group in range(groups):
                at = group * ROWS + quad
                re = gathered[pl.ds(at, devices, stride=block), :].astype(jnp.bfloat16)
                im = gathered[pl.ds(at + quads, devices, stride=block), :].astype(jnp.bfloat16)
                plain = jnp.concatenate([re, im], axis=1)
                turned = jnp.concatenate([im, -re], axis=1)
                left = jnp.concatenate([plain, turned], axis=0)
                right = jnp.concatenate([plain * masks[j] for j in range(packed)], axis=0)
                product = lax.dot_general(
                    left, right, (((1,), (1,)), ((), ())), preferred_element_type=jnp.float32
                )
                if chunk == 0:
                    acc[quad * groups + group] = product
                else:
                    acc[quad * groups + group] += product

    for first in range(0, quads * groups, packed):
        chosen = [
            jnp.where(lower, acc[g, :devices], acc[g, devices:]) / denom
            for g in range(first, first + packed)
        ]
        moved = jnp.dot(
            jnp.concatenate(chosen, axis=0).astype(jnp.bfloat16),
            columns,
            preferred_element_type=jnp.float32,
        )
        moved = jnp.dot(
            rows, moved.astype(jnp.bfloat16), preferred_element_type=jnp.float32
        ).astype(jnp.bfloat16)
        for g in range(packed):
            for j in range(packed):
                out_ref[packed * (first + g) + j] = moved[
                    devices * g : devices * (g + 1), devices * j : devices * (j + 1)
                ]

    for chunk in range(chunks):
        gone = send.at[chunk, pl.ds(0, devices - 1)]
        pltpu.make_async_copy(gone, gone, send_sem.at[chunk]).wait()
    pltpu.make_async_copy(told, told, meta_send_sem).wait()


def fused(voltages, flags, station_row, stn_count, chan_count):
    devices = stn_count * chan_count
    frames, lanes = voltages.shape[2], voltages.shape[3]
    spectra = flags.shape[1]
    taps = frames - spectra + 1
    outer = lanes // LANES
    chunks = 4
    span = spectra // chunks
    packed = LANES // span
    block = outer // packed * ROWS
    table = host_tables(taps, lanes, devices)
    vmem = pl.BlockSpec(memory_space=pltpu.VMEM)
    hbm = pl.BlockSpec(memory_space=pl.ANY)
    f32, bf16 = jnp.float32, jnp.bfloat16
    return pl.pallas_call(
        functools.partial(kernel, stn_count, chan_count, chunks),
        out_shape=jax.ShapeDtypeStruct((lanes // devices, devices, devices), bf16),
        in_specs=[
            hbm,
            pl.BlockSpec(memory_space=pltpu.SMEM),
            pl.BlockSpec(memory_space=pltpu.SMEM),
            hbm,
        ],
        out_specs=vmem,
        scratch_shapes=[
            pltpu.VMEM((frames, 2, lanes), bf16),
            pltpu.VMEM((outer * taps * ROWS, LANES), f32),
            pltpu.VMEM((2 * outer, LANES), f32),
            pltpu.VMEM((4 * LANES, LANES), f32),
            pltpu.VMEM((2 * LANES, 2 * LANES), bf16),
            pltpu.VMEM((outer, 2 * frames, LANES), f32),
            pltpu.VMEM((2, outer, span, LANES), f32),
            pltpu.VMEM((outer, span, 2 * LANES), f32),
            pltpu.VMEM((chunks, devices, block, LANES), bf16),
            pltpu.VMEM((chunks, devices, block, LANES), bf16),
            pltpu.VMEM((stn_count, ROWS, LANES), f32),
            pltpu.VMEM((devices * block, LANES), f32),
            pltpu.VMEM((packed, devices, 2 * LANES), bf16),
            pltpu.VMEM((outer * (LANES // devices) // packed, 2 * devices, packed * devices), f32),
            pltpu.SemaphoreType.DMA((5,)),
            pltpu.SemaphoreType.DMA((chunks,)),
            pltpu.SemaphoreType.DMA((chunks,)),
            pltpu.SemaphoreType.DMA,
            pltpu.SemaphoreType.DMA,
        ],
        compiler_params=pltpu.CompilerParams(
            collective_id=0, has_side_effects=True, vmem_limit_bytes=53 * 1024 * 1024
        ),
    )(jnp.transpose(voltages, (0, 2, 1, 3)), flags, station_row, table)


def solution(mesh):
    placed = (P(("stn", "chan"), None, None, None), P("stn", None), P("stn"))
    return jax.shard_map(
        on_device,
        mesh=mesh,
        in_specs=placed,
        out_specs=P(("stn", "chan"), None, None),
        check_vma=False,
    )
```

```python
import functools
import math

import jax
import jax.numpy as jnp
import numpy as np
from jax import lax
from jax.experimental import pallas as pl
from jax.experimental.pallas import tpu as pltpu
from jax.sharding import PartitionSpec as P

LANES = 128
ROWS = 8


def filter_table(taps, lanes):
    total = taps * lanes
    places = jnp.arange(total, dtype=jnp.float32) + 0.5
    window = 0.5 - 0.5 * jnp.cos(2.0 * math.pi * places / total)
    return (jnp.sinc((places - 0.5 * total) / lanes) * window).reshape(taps, lanes)


def dft_tables(length):
    places = jnp.arange(length, dtype=jnp.int32)
    product = places[:, None] * places[None, :] % length
    angle = 2.0 * math.pi * product.astype(jnp.float32) / length
    return (jnp.cos(angle), jnp.sin(angle))


def twiddle_tables(outer, inner):
    product = (
        jnp.arange(outer, dtype=jnp.int32)[:, None]
        * jnp.arange(inner, dtype=jnp.int32)[None, :]
        % (outer * inner)
    )
    angle = 2.0 * math.pi * product.astype(jnp.float32) / (outer * inner)
    return (jnp.cos(angle), jnp.sin(angle))


def contract(form, left, right):
    return jnp.einsum(form, left, right, precision=lax.Precision.HIGHEST)


def channelize(voltages, spectra_count):
    inputs_here = voltages.shape[0]
    lanes = voltages.shape[3]
    taps = voltages.shape[2] - spectra_count + 1
    taps_table = filter_table(taps, lanes)
    real_acc = taps_table[0] * voltages[:, 0, 0:spectra_count, :].astype(jnp.float32)
    imag_acc = taps_table[0] * voltages[:, 1, 0:spectra_count, :].astype(jnp.float32)
    for tap_index in range(1, taps):
        real_acc = real_acc + taps_table[tap_index] * voltages[
            :, 0, tap_index : tap_index + spectra_count, :
        ].astype(jnp.float32)
        imag_acc = imag_acc + taps_table[tap_index] * voltages[
            :, 1, tap_index : tap_index + spectra_count, :
        ].astype(jnp.float32)
    inner = 128
    outer = lanes // inner
    real_grid = real_acc.reshape(inputs_here, spectra_count, outer, inner)
    imag_grid = imag_acc.reshape(inputs_here, spectra_count, outer, inner)
    cos_outer, sin_outer = dft_tables(outer)
    real_mid = contract("gtmn,mk->gtkn", real_grid, cos_outer) + contract(
        "gtmn,mk->gtkn", imag_grid, sin_outer
    )
    imag_mid = contract("gtmn,mk->gtkn", imag_grid, cos_outer) - contract(
        "gtmn,mk->gtkn", real_grid, sin_outer
    )
    cos_twist, sin_twist = twiddle_tables(outer, inner)
    real_twisted = real_mid * cos_twist + imag_mid * sin_twist
    imag_twisted = imag_mid * cos_twist - real_mid * sin_twist
    cos_inner, sin_inner = dft_tables(inner)
    real_out = contract("gtkn,nj->jkgt", real_twisted, cos_inner) + contract(
        "gtkn,nj->jkgt", imag_twisted, sin_inner
    )
    imag_out = contract("gtkn,nj->jkgt", imag_twisted, cos_inner) - contract(
        "gtkn,nj->jkgt", real_twisted, sin_inner
    )
    scale = 1.0 / math.sqrt(lanes)
    stacked = (jnp.stack([real_out, imag_out], axis=3) * scale).astype(jnp.bfloat16)
    return stacked.reshape(lanes, inputs_here, 2 * spectra_count)


def square_products(plain, turned):
    real_part = jnp.einsum("cat,cbt->cab", plain, plain, preferred_element_type=jnp.float32)
    imag_part = jnp.einsum("cat,cbt->cab", plain, turned, preferred_element_type=jnp.float32)
    return (real_part, imag_part)


def on_device(voltages, flags, station_row):
    spectra_count = flags.shape[1]
    inputs_here = voltages.shape[0]
    lanes = voltages.shape[3]
    stn_count = lax.axis_size("stn")
    chan_count = lax.axis_size("chan")
    per_device = lanes // (stn_count * chan_count)
    total_inputs = inputs_here * stn_count * chan_count
    if (
        total_inputs == 32
        and inputs_here == 1
        and chan_count == 2
        and lanes == 16 * LANES
        and spectra_count == LANES
    ):
        return fused(voltages, flags, station_row, stn_count, chan_count)
    flags_all, rows_all = (
        lax.all_gather(flags, "stn", axis=0, tiled=True),
        lax.all_gather(station_row, "stn", axis=0, tiled=True),
    )
    spectra = channelize(voltages, spectra_count)
    grouped = spectra.reshape(stn_count, chan_count, per_device, inputs_here, 2 * spectra_count)
    order = jnp.argsort(rows_all)
    rows = jnp.arange(total_inputs, dtype=jnp.int32)
    station_of = order[rows // 2]
    source = 2 * station_of + rows % 2
    moved = lax.all_to_all(
        lax.all_to_all(grouped, "stn", split_axis=0, concat_axis=3, tiled=True),
        "chan",
        split_axis=1,
        concat_axis=3,
        tiled=True,
    )
    from_stn = source // (chan_count * inputs_here)
    from_chan = source // inputs_here % chan_count
    within = source % inputs_here
    placed = from_chan * (stn_count * inputs_here) + from_stn * inputs_here + within
    arrived = moved.reshape(per_device, total_inputs, 2, spectra_count)
    weights = jnp.take(flags_all, station_of, axis=0)
    kept = (
        jnp.take(arrived, placed, axis=1).astype(jnp.float32) * weights[None, :, None, :]
    ).astype(jnp.bfloat16)
    plain = kept.reshape(per_device, total_inputs, 2 * spectra_count)
    turned = jnp.concatenate([-kept[:, :, 1], kept[:, :, 0]], axis=-1)
    count = jnp.dot(
        weights, weights.T, preferred_element_type=jnp.float32, precision=lax.Precision.HIGHEST
    )
    denom = jnp.maximum(count, 1.0)
    real_part, imag_part = square_products(plain, turned)
    below = rows[:, None] >= rows[None, :]
    return jnp.where(below[None], real_part / denom, imag_part / denom).astype(jnp.bfloat16)


def host_tables(taps, lanes, devices):
    outer = lanes // LANES
    quads = LANES // devices
    total = taps * lanes
    places = np.arange(total) + 0.5
    window = 0.5 - 0.5 * np.cos(2.0 * np.pi * places / total)
    taper = (np.sinc((places - 0.5 * total) / lanes) * window).reshape(taps, outer, LANES)
    taper = taper.transpose(1, 0, 2)
    angle = 2.0 * np.pi * (np.arange(outer)[:, None] * np.arange(LANES)[None, :]) / lanes
    scale = 1.0 / math.sqrt(lanes)
    twist = np.stack([np.cos(angle), np.sin(angle)]) * scale
    turn = 2.0 * np.pi * (np.arange(LANES)[:, None] * np.arange(LANES)[None, :] % LANES) / LANES
    cos, sin = np.cos(turn), np.sin(turn)
    real_rows = np.concatenate([cos, sin], axis=1).reshape(devices, 1, quads, 2 * LANES)
    imag_rows = np.concatenate([-sin, cos], axis=1).reshape(devices, 1, quads, 2 * LANES)
    matrix = np.concatenate([real_rows, imag_rows], axis=1).reshape(2 * LANES, 2 * LANES)
    rows = [
        np.repeat(taper.reshape(outer * taps, LANES), ROWS, axis=0),
        twist.reshape(2 * outer, LANES),
        matrix.astype(jnp.bfloat16).astype(np.float32)[:, :LANES],
        matrix.astype(jnp.bfloat16).astype(np.float32)[:, LANES:],
    ]
    return jnp.asarray(np.concatenate(rows, axis=0).astype(np.float32))


def dft4(a, b, c, d):
    s0 = (a[0] + c[0], a[1] + c[1])
    s1 = (a[0] - c[0], a[1] - c[1])
    s2 = (b[0] + d[0], b[1] + d[1])
    s3 = (b[0] - d[0], b[1] - d[1])
    return (
        (s0[0] + s2[0], s0[1] + s2[1]),
        (s1[0] + s3[1], s1[1] - s3[0]),
        (s0[0] - s2[0], s0[1] - s2[1]),
        (s1[0] - s3[1], s1[1] + s3[0]),
    )


def dft16(x):
    half = math.sqrt(0.5)
    mids = [dft4(x[p], x[4 + p], x[8 + p], x[12 + p]) for p in range(4)]
    out = [None] * 16
    for kx in range(4):
        turned = []
        for p in range(4):
            re, im = mids[p][kx]
            e = p * kx
            if e == 0:
                turned.append((re, im))
            elif e == 4:
                turned.append((im, -re))
            elif e == 2:
                turned.append(((re + im) * half, (im - re) * half))
            elif e == 6:
                turned.append(((im - re) * half, -(re + im) * half))
            else:
                c, s = math.cos(2 * math.pi * e / 16), math.sin(2 * math.pi * e / 16)
                turned.append((re * c + im * s, im * c - re * s))
        for ky, value in enumerate(dft4(*turned)):
            out[kx + 4 * ky] = value
    return out


def iota(shape, dim):
    return lax.broadcasted_iota(jnp.int32, shape, dim)


def kernel(
    stn_count, chan_count, chunks,
    volt_hbm, flags_ref, row_ref, table_hbm, out_ref,
    volt, taper_ref, twist_ref, matrix_f32, matrix_ref,
    wide, filt, mids, send, recv, meta, gathered, masks, acc,
    load_sem, send_sem, recv_sem, meta_send_sem, meta_recv_sem,
):
    devices = stn_count * chan_count
    frames = volt.shape[0]
    spectra = flags_ref.shape[1]
    taps = frames - spectra + 1
    outer = volt.shape[2] // LANES
    span = spectra // chunks
    packed = LANES // span
    groups = outer // packed
    quads = LANES // devices
    block = groups * ROWS
    stn, chan = lax.axis_index("stn"), lax.axis_index("chan")
    me = stn * chan_count + chan

    first_frames = spectra // chunks + taps
    head, rest = pl.ds(0, first_frames), pl.ds(first_frames, frames - first_frames)
    taper_rows, twist_rows, matrix_rows = outer * taps * ROWS, 2 * outer, 4 * LANES
    sources = (
        (volt_hbm.at[0, head], volt.at[head]),
        (table_hbm.at[pl.ds(0, taper_rows)], taper_ref),
        (table_hbm.at[pl.ds(taper_rows, twist_rows)], twist_ref),
        (table_hbm.at[pl.ds(taper_rows + twist_rows, matrix_rows)], matrix_f32),
        (volt_hbm.at[0, rest], volt.at[rest]),
    )
    loads = [
        pltpu.make_async_copy(source, target, load_sem.at[k])
        for k, (source, target) in enumerate(sources)
    ]
    for load in loads:
        load.start()

    stn_flips = [
        (1 - 2 * (stn // 2**bit % 2)) * 2**bit for bit in range(stn_count.bit_length() - 1)
    ]
    chan_flips = [
        (1 - 2 * (chan // 2**bit % 2)) * 2**bit for bit in range(chan_count.bit_length() - 1)
    ]

    def flipped(start, flips, step):
        for bit, flip in enumerate(flips):
            if step >> bit & 1:
                start = start + flip
        return start

    def partner(step):
        return (
            flipped(stn, stn_flips, step // chan_count),
            flipped(chan, chan_flips, step % chan_count),
        )

    barrier = pltpu.get_barrier_semaphore()
    for step in range(1, devices):
        pl.semaphore_signal(
            barrier, inc=1, device_id=partner(step), device_id_type=pl.DeviceIdType.MESH
        )

    lane8 = iota((ROWS, LANES), 1)
    flags8 = lax.fori_loop(
        0, spectra, lambda t, held: jnp.where(lane8 == t, flags_ref[0, t], held),
        jnp.zeros((ROWS, LANES), jnp.float32), unroll=8,
    )
    station = jnp.broadcast_to(row_ref[0], (ROWS, LANES)).astype(jnp.float32)
    meta[stn] = jnp.where(iota((ROWS, LANES), 0) == 0, flags8, station)

    def meta_copy(step):
        return pltpu.make_async_remote_copy(
            src_ref=meta.at[stn], dst_ref=meta.at[stn],
            send_sem=meta_send_sem, recv_sem=meta_recv_sem,
            device_id=(flipped(stn, stn_flips, step), chan), device_id_type=pl.DeviceIdType.MESH,
        )

    def block_copy(chunk, step):
        to_stn, to_chan = partner(step)
        return pltpu.make_async_remote_copy(
            src_ref=send.at[chunk, to_stn * chan_count + to_chan], dst_ref=recv.at[chunk, me],
            send_sem=send_sem.at[chunk], recv_sem=recv_sem.at[chunk],
            device_id=(to_stn, to_chan), device_id_type=pl.DeviceIdType.MESH,
        )

    for load in loads[:3]:
        load.wait()
    for chunk in range(chunks):
        start = chunk * span
        low = 0 if chunk == 0 else start + taps
        high = min(start + span + taps, frames)

        def widen(a, carry, low=low, high=high):
            lanes = pl.ds(pl.multiple_of(a * LANES, LANES), LANES)
            pairs = volt[low:high, :, lanes].reshape(2 * (high - low), LANES)
            wide[a, 2 * low : 2 * high, :] = pairs.astype(jnp.float32)
            return carry

        if chunk == 1:
            loads[4].wait()
        lax.fori_loop(0, outer, widen, 0)

        def fir(a, carry, start=start):
            for part in range(2):
                def window(tap):
                    rows = wide[a, pl.ds(2 * (start + tap) + part, span, stride=2), :]
                    return rows.reshape(span // ROWS, ROWS, LANES)

                def weight(tap):
                    at = pl.multiple_of((a * taps + tap) * ROWS, ROWS)
                    return taper_ref[pl.ds(at, ROWS), :][None]

                total = weight(0) * window(0)
                for tap in range(1, taps):
                    total = total + weight(tap) * window(tap)
                filt[part, a] = total.reshape(span, LANES)
            return carry

        lax.fori_loop(0, outer, fir, 0)

        def first_stage(tile, carry):
            rows = pl.ds(pl.multiple_of(tile * ROWS, ROWS), ROWS)
            values = dft16([(filt[0, a, rows, :], filt[1, a, rows, :]) for a in range(outer)])
            for k in range(outer):
                re, im = values[k]
                c = twist_ref[k : k + 1, :]
                s = twist_ref[outer + k : outer + k + 1, :]
                mids[k, rows, 0:LANES] = re * c + im * s
                mids[k, rows, LANES:] = im * c - re * s
            return carry

        lax.fori_loop(0, span // ROWS, first_stage, 0)

        weights8 = jnp.zeros((ROWS, LANES), jnp.float32)
        for j in range(packed):
            shift = (span * j - start) % LANES
            rolled = pltpu.roll(flags8, shift, 1) if shift else flags8
            weights8 = jnp.where(lane8 // span == j, rolled, weights8)
        if chunk == 0:
            loads[3].wait()
            for half in range(2):
                columns = slice(half * LANES, (half + 1) * LANES)
                matrix_ref[:, columns] = matrix_f32[
                    2 * LANES * half : 2 * LANES * (half + 1)
                ].astype(jnp.bfloat16)
        for pair in range(groups // 2):
            halves = []
            for group in (2 * pair, 2 * pair + 1):
                data = mids[packed * group : packed * (group + 1)].reshape(LANES, 2 * LANES)
                spectrum = lax.dot_general(
                    matrix_ref[...], data.astype(jnp.bfloat16), (((1,), (1,)), ((), ())),
                    preferred_element_type=jnp.float32,
                )
                rounded = spectrum.astype(jnp.bfloat16).astype(jnp.float32)
                halves.append(rounded.reshape(devices, ROWS, LANES) * weights8[None])
            send[chunk, :, 2 * ROWS * pair : 2 * ROWS * (pair + 1), :] = jnp.concatenate(
                halves, axis=1
            ).astype(jnp.bfloat16)

        if chunk == 0:
            pl.semaphore_wait(barrier, devices - 1)
        half = devices // 2
        for far in range(devices - 1, half - 1, -1):
            block_copy(chunk, far).start()
            if far > half:
                block_copy(chunk, far - half).start()
        if chunk == 0:
            for step in range(1, stn_count):
                meta_copy(step).start()
        recv[chunk, me] = send[chunk, me]

    told = meta.at[pl.ds(0, stn_count - 1)]
    pltpu.make_async_copy(told, told, meta_recv_sem).wait()
    tall = packed * devices
    exact = functools.partial(
        lax.dot_general, precision=lax.Precision.HIGHEST, preferred_element_type=jnp.float32
    )
    spread = (iota((tall, stn_count), 0) % devices // 2 == iota((tall, stn_count), 1)).astype(
        jnp.float32
    )
    all_flags = meta[:, 0, :]
    all_rows = meta[:, 1, :]
    weights = exact(spread, all_flags, (((1,), (0,)), ((), ())))
    count = exact(weights[:devices], weights, (((1,), (1,)), ((), ())))
    place = 2 * exact(spread, all_rows, (((1,), (0,)), ((), ()))).astype(jnp.int32)
    place = place + iota(place.shape, 0) % 2
    across = place.T
    place = place[:, :tall]
    lower = place[:devices] >= across[:devices]
    denom = jnp.maximum(count, 1.0)
    lane_at = iota((tall, tall), 1)
    columns = jnp.logical_and(
        place == lane_at % devices, iota((tall, tall), 0) // devices == lane_at // devices
    ).astype(jnp.bfloat16)
    rows = jnp.logical_and(
        across[:tall] == iota((tall, tall), 0) % devices, iota((tall, tall), 0) // devices == lane_at // devices
    ).astype(jnp.bfloat16)
    lane = iota((devices, 2 * LANES), 1) % LANES // span
    for j in range(packed):
        masks[j] = (lane == j).astype(jnp.bfloat16)
    for chunk in range(chunks):
        arrived = recv.at[chunk, pl.ds(0, devices - 1)]
        pltpu.make_async_copy(arrived, arrived, recv_sem.at[chunk]).wait()
        gathered[...] = recv[chunk].reshape(devices * block, LANES).astype(jnp.float32)
        for quad in range(quads):
            for group in range(groups):
                at = group * ROWS + quad
                re = gathered[pl.ds(at, devices, stride=block), :].astype(jnp.bfloat16)
                im = gathered[pl.ds(at + quads, devices, stride=block), :].astype(jnp.bfloat16)
                plain = jnp.concatenate([re, im], axis=1)
                turned = jnp.concatenate([im, -re], axis=1)
                left = jnp.concatenate([plain, turned], axis=0)
                right = jnp.concatenate([plain * masks[j] for j in range(packed)], axis=0)
                product = lax.dot_general(
                    left, right, (((1,), (1,)), ((), ())), preferred_element_type=jnp.float32
                )
                if chunk == 0:
                    acc[quad * groups + group] = product
                else:
                    acc[quad * groups + group] += product

    for first in range(0, quads * groups, packed):
        chosen = [
            jnp.where(lower, acc[g, :devices], acc[g, devices:]) / denom
            for g in range(first, first + packed)
        ]
        moved = jnp.dot(
            jnp.concatenate(chosen, axis=0).astype(jnp.bfloat16),
            columns,
            preferred_element_type=jnp.float32,
        )
        moved = jnp.dot(
            rows, moved.astype(jnp.bfloat16), preferred_element_type=jnp.float32
        ).astype(jnp.bfloat16)
        for g in range(packed):
            for j in range(packed):
                out_ref[packed * (first + g) + j] = moved[
                    devices * g : devices * (g + 1), devices * j : devices * (j + 1)
                ]

    for chunk in range(chunks):
        gone = send.at[chunk, pl.ds(0, devices - 1)]
        pltpu.make_async_copy(gone, gone, send_sem.at[chunk]).wait()
    pltpu.make_async_copy(told, told, meta_send_sem).wait()


def fused(voltages, flags, station_row, stn_count, chan_count):
    devices = stn_count * chan_count
    frames, lanes = voltages.shape[2], voltages.shape[3]
    spectra = flags.shape[1]
    taps = frames - spectra + 1
    outer = lanes // LANES
    chunks = 2
    span = spectra // chunks
    packed = LANES // span
    block = outer // packed * ROWS
    table = host_tables(taps, lanes, devices)
    vmem = pl.BlockSpec(memory_space=pltpu.VMEM)
    hbm = pl.BlockSpec(memory_space=pl.ANY)
    f32, bf16 = jnp.float32, jnp.bfloat16
    return pl.pallas_call(
        functools.partial(kernel, stn_count, chan_count, chunks),
        out_shape=jax.ShapeDtypeStruct((lanes // devices, devices, devices), bf16),
        in_specs=[
            hbm,
            pl.BlockSpec(memory_space=pltpu.SMEM),
            pl.BlockSpec(memory_space=pltpu.SMEM),
            hbm,
        ],
        out_specs=vmem,
        scratch_shapes=[
            pltpu.VMEM((frames, 2, lanes), bf16),
            pltpu.VMEM((outer * taps * ROWS, LANES), f32),
            pltpu.VMEM((2 * outer, LANES), f32),
            pltpu.VMEM((4 * LANES, LANES), f32),
            pltpu.VMEM((2 * LANES, 2 * LANES), bf16),
            pltpu.VMEM((outer, 2 * frames, LANES), f32),
            pltpu.VMEM((2, outer, span, LANES), f32),
            pltpu.VMEM((outer, span, 2 * LANES), f32),
            pltpu.VMEM((chunks, devices, block, LANES), bf16),
            pltpu.VMEM((chunks, devices, block, LANES), bf16),
            pltpu.VMEM((stn_count, ROWS, LANES), f32),
            pltpu.VMEM((devices * block, LANES), f32),
            pltpu.VMEM((packed, devices, 2 * LANES), bf16),
            pltpu.VMEM((outer * (LANES // devices) // packed, 2 * devices, packed * devices), f32),
            pltpu.SemaphoreType.DMA((5,)),
            pltpu.SemaphoreType.DMA((chunks,)),
            pltpu.SemaphoreType.DMA((chunks,)),
            pltpu.SemaphoreType.DMA,
            pltpu.SemaphoreType.DMA,
        ],
        compiler_params=pltpu.CompilerParams(
            collective_id=0, has_side_effects=True, vmem_limit_bytes=53 * 1024 * 1024
        ),
    )(jnp.transpose(voltages, (0, 2, 1, 3)), flags, station_row, table)


def solution(mesh):
    placed = (P(("stn", "chan"), None, None, None), P("stn", None), P("stn"))
    return jax.shard_map(
        on_device,
        mesh=mesh,
        in_specs=placed,
        out_specs=P(("stn", "chan"), None, None),
        check_vma=False,
    )
```

```python
import functools
import math

import jax
import jax.numpy as jnp
import numpy as np
from jax import lax
from jax.experimental import pallas as pl
from jax.experimental.pallas import tpu as pltpu
from jax.sharding import PartitionSpec as P

LANES = 128
ROWS = 8


def filter_table(taps, lanes):
    total = taps * lanes
    places = jnp.arange(total, dtype=jnp.float32) + 0.5
    window = 0.5 - 0.5 * jnp.cos(2.0 * math.pi * places / total)
    return (jnp.sinc((places - 0.5 * total) / lanes) * window).reshape(taps, lanes)


def dft_tables(length):
    places = jnp.arange(length, dtype=jnp.int32)
    product = places[:, None] * places[None, :] % length
    angle = 2.0 * math.pi * product.astype(jnp.float32) / length
    return (jnp.cos(angle), jnp.sin(angle))


def twiddle_tables(outer, inner):
    product = (
        jnp.arange(outer, dtype=jnp.int32)[:, None]
        * jnp.arange(inner, dtype=jnp.int32)[None, :]
        % (outer * inner)
    )
    angle = 2.0 * math.pi * product.astype(jnp.float32) / (outer * inner)
    return (jnp.cos(angle), jnp.sin(angle))


def contract(form, left, right):
    return jnp.einsum(form, left, right, precision=lax.Precision.HIGHEST)


def channelize(voltages, spectra_count):
    inputs_here = voltages.shape[0]
    lanes = voltages.shape[3]
    taps = voltages.shape[2] - spectra_count + 1
    taps_table = filter_table(taps, lanes)
    real_acc = taps_table[0] * voltages[:, 0, 0:spectra_count, :].astype(jnp.float32)
    imag_acc = taps_table[0] * voltages[:, 1, 0:spectra_count, :].astype(jnp.float32)
    for tap_index in range(1, taps):
        real_acc = real_acc + taps_table[tap_index] * voltages[
            :, 0, tap_index : tap_index + spectra_count, :
        ].astype(jnp.float32)
        imag_acc = imag_acc + taps_table[tap_index] * voltages[
            :, 1, tap_index : tap_index + spectra_count, :
        ].astype(jnp.float32)
    inner = 128
    outer = lanes // inner
    real_grid = real_acc.reshape(inputs_here, spectra_count, outer, inner)
    imag_grid = imag_acc.reshape(inputs_here, spectra_count, outer, inner)
    cos_outer, sin_outer = dft_tables(outer)
    real_mid = contract("gtmn,mk->gtkn", real_grid, cos_outer) + contract(
        "gtmn,mk->gtkn", imag_grid, sin_outer
    )
    imag_mid = contract("gtmn,mk->gtkn", imag_grid, cos_outer) - contract(
        "gtmn,mk->gtkn", real_grid, sin_outer
    )
    cos_twist, sin_twist = twiddle_tables(outer, inner)
    real_twisted = real_mid * cos_twist + imag_mid * sin_twist
    imag_twisted = imag_mid * cos_twist - real_mid * sin_twist
    cos_inner, sin_inner = dft_tables(inner)
    real_out = contract("gtkn,nj->jkgt", real_twisted, cos_inner) + contract(
        "gtkn,nj->jkgt", imag_twisted, sin_inner
    )
    imag_out = contract("gtkn,nj->jkgt", imag_twisted, cos_inner) - contract(
        "gtkn,nj->jkgt", real_twisted, sin_inner
    )
    scale = 1.0 / math.sqrt(lanes)
    stacked = (jnp.stack([real_out, imag_out], axis=3) * scale).astype(jnp.bfloat16)
    return stacked.reshape(lanes, inputs_here, 2 * spectra_count)


def square_products(plain, turned):
    real_part = jnp.einsum("cat,cbt->cab", plain, plain, preferred_element_type=jnp.float32)
    imag_part = jnp.einsum("cat,cbt->cab", plain, turned, preferred_element_type=jnp.float32)
    return (real_part, imag_part)


def on_device(voltages, flags, station_row):
    spectra_count = flags.shape[1]
    inputs_here = voltages.shape[0]
    lanes = voltages.shape[3]
    stn_count = lax.axis_size("stn")
    chan_count = lax.axis_size("chan")
    per_device = lanes // (stn_count * chan_count)
    total_inputs = inputs_here * stn_count * chan_count
    if (
        total_inputs == 32
        and inputs_here == 1
        and chan_count == 2
        and lanes == 16 * LANES
        and spectra_count == LANES
    ):
        return fused(voltages, flags, station_row, stn_count, chan_count)
    flags_all, rows_all = (
        lax.all_gather(flags, "stn", axis=0, tiled=True),
        lax.all_gather(station_row, "stn", axis=0, tiled=True),
    )
    spectra = channelize(voltages, spectra_count)
    grouped = spectra.reshape(stn_count, chan_count, per_device, inputs_here, 2 * spectra_count)
    order = jnp.argsort(rows_all)
    rows = jnp.arange(total_inputs, dtype=jnp.int32)
    station_of = order[rows // 2]
    source = 2 * station_of + rows % 2
    moved = lax.all_to_all(
        lax.all_to_all(grouped, "stn", split_axis=0, concat_axis=3, tiled=True),
        "chan",
        split_axis=1,
        concat_axis=3,
        tiled=True,
    )
    from_stn = source // (chan_count * inputs_here)
    from_chan = source // inputs_here % chan_count
    within = source % inputs_here
    placed = from_chan * (stn_count * inputs_here) + from_stn * inputs_here + within
    arrived = moved.reshape(per_device, total_inputs, 2, spectra_count)
    weights = jnp.take(flags_all, station_of, axis=0)
    kept = (
        jnp.take(arrived, placed, axis=1).astype(jnp.float32) * weights[None, :, None, :]
    ).astype(jnp.bfloat16)
    plain = kept.reshape(per_device, total_inputs, 2 * spectra_count)
    turned = jnp.concatenate([-kept[:, :, 1], kept[:, :, 0]], axis=-1)
    count = jnp.dot(
        weights, weights.T, preferred_element_type=jnp.float32, precision=lax.Precision.HIGHEST
    )
    denom = jnp.maximum(count, 1.0)
    real_part, imag_part = square_products(plain, turned)
    below = rows[:, None] >= rows[None, :]
    return jnp.where(below[None], real_part / denom, imag_part / denom).astype(jnp.bfloat16)


def host_tables(taps, lanes, devices):
    outer = lanes // LANES
    quads = LANES // devices
    total = taps * lanes
    places = np.arange(total) + 0.5
    window = 0.5 - 0.5 * np.cos(2.0 * np.pi * places / total)
    taper = (np.sinc((places - 0.5 * total) / lanes) * window).reshape(taps, outer, LANES)
    taper = taper.transpose(1, 0, 2)
    angle = 2.0 * np.pi * (np.arange(outer)[:, None] * np.arange(LANES)[None, :]) / lanes
    scale = 1.0 / math.sqrt(lanes)
    twist = np.stack([np.cos(angle), np.sin(angle)]) * scale
    turn = 2.0 * np.pi * (np.arange(LANES)[:, None] * np.arange(LANES)[None, :] % LANES) / LANES
    cos, sin = np.cos(turn), np.sin(turn)
    real_rows = np.concatenate([cos, sin], axis=1).reshape(devices, 1, quads, 2 * LANES)
    imag_rows = np.concatenate([-sin, cos], axis=1).reshape(devices, 1, quads, 2 * LANES)
    matrix = np.concatenate([real_rows, imag_rows], axis=1).reshape(2 * LANES, 2 * LANES)
    rows = [
        np.repeat(taper.reshape(outer * taps, LANES), ROWS, axis=0),
        twist.reshape(2 * outer, LANES),
        matrix.astype(jnp.bfloat16).astype(np.float32)[:, :LANES],
        matrix.astype(jnp.bfloat16).astype(np.float32)[:, LANES:],
    ]
    return jnp.asarray(np.concatenate(rows, axis=0).astype(np.float32))


def dft4(a, b, c, d):
    s0 = (a[0] + c[0], a[1] + c[1])
    s1 = (a[0] - c[0], a[1] - c[1])
    s2 = (b[0] + d[0], b[1] + d[1])
    s3 = (b[0] - d[0], b[1] - d[1])
    return (
        (s0[0] + s2[0], s0[1] + s2[1]),
        (s1[0] + s3[1], s1[1] - s3[0]),
        (s0[0] - s2[0], s0[1] - s2[1]),
        (s1[0] - s3[1], s1[1] + s3[0]),
    )


def dft16(x):
    half = math.sqrt(0.5)
    mids = [dft4(x[p], x[4 + p], x[8 + p], x[12 + p]) for p in range(4)]
    out = [None] * 16
    for kx in range(4):
        turned = []
        for p in range(4):
            re, im = mids[p][kx]
            e = p * kx
            if e == 0:
                turned.append((re, im))
            elif e == 4:
                turned.append((im, -re))
            elif e == 2:
                turned.append(((re + im) * half, (im - re) * half))
            elif e == 6:
                turned.append(((im - re) * half, -(re + im) * half))
            else:
                c, s = math.cos(2 * math.pi * e / 16), math.sin(2 * math.pi * e / 16)
                turned.append((re * c + im * s, im * c - re * s))
        for ky, value in enumerate(dft4(*turned)):
            out[kx + 4 * ky] = value
    return out


def iota(shape, dim):
    return lax.broadcasted_iota(jnp.int32, shape, dim)


def kernel(
    stn_count, chan_count, chunks,
    volt_hbm, flags_ref, row_ref, table_hbm, out_ref,
    volt, taper_ref, twist_ref, matrix_f32, matrix_ref,
    wide, filt, mids, send, recv, meta, gathered, masks, acc,
    load_sem, send_sem, recv_sem, meta_send_sem, meta_recv_sem,
):
    devices = stn_count * chan_count
    frames = volt.shape[0]
    spectra = flags_ref.shape[1]
    taps = frames - spectra + 1
    outer = volt.shape[2] // LANES
    span = spectra // chunks
    packed = LANES // span
    groups = outer // packed
    quads = LANES // devices
    block = groups * ROWS
    stn, chan = lax.axis_index("stn"), lax.axis_index("chan")
    me = stn * chan_count + chan

    first_frames = spectra // chunks + taps
    head, rest = pl.ds(0, first_frames), pl.ds(first_frames, frames - first_frames)
    taper_rows, twist_rows, matrix_rows = outer * taps * ROWS, 2 * outer, 4 * LANES
    sources = (
        (volt_hbm.at[0, head], volt.at[head]),
        (table_hbm.at[pl.ds(0, taper_rows)], taper_ref),
        (table_hbm.at[pl.ds(taper_rows, twist_rows)], twist_ref),
        (table_hbm.at[pl.ds(taper_rows + twist_rows, matrix_rows)], matrix_f32),
        (volt_hbm.at[0, rest], volt.at[rest]),
    )
    loads = [
        pltpu.make_async_copy(source, target, load_sem.at[k])
        for k, (source, target) in enumerate(sources)
    ]
    for load in loads:
        load.start()

    stn_flips = [
        (1 - 2 * (stn // 2**bit % 2)) * 2**bit for bit in range(stn_count.bit_length() - 1)
    ]
    chan_flips = [
        (1 - 2 * (chan // 2**bit % 2)) * 2**bit for bit in range(chan_count.bit_length() - 1)
    ]

    def flipped(start, flips, step):
        for bit, flip in enumerate(flips):
            if step >> bit & 1:
                start = start + flip
        return start

    def partner(step):
        return (
            flipped(stn, stn_flips, step // chan_count),
            flipped(chan, chan_flips, step % chan_count),
        )

    barrier = pltpu.get_barrier_semaphore()
    for step in range(1, devices):
        pl.semaphore_signal(
            barrier, inc=1, device_id=partner(step), device_id_type=pl.DeviceIdType.MESH
        )

    lane8 = iota((ROWS, LANES), 1)
    flags8 = lax.fori_loop(
        0, spectra, lambda t, held: jnp.where(lane8 == t, flags_ref[0, t], held),
        jnp.zeros((ROWS, LANES), jnp.float32), unroll=8,
    )
    station = jnp.broadcast_to(row_ref[0], (ROWS, LANES)).astype(jnp.float32)
    meta[stn] = jnp.where(iota((ROWS, LANES), 0) == 0, flags8, station)

    def meta_copy(step):
        return pltpu.make_async_remote_copy(
            src_ref=meta.at[stn], dst_ref=meta.at[stn],
            send_sem=meta_send_sem, recv_sem=meta_recv_sem,
            device_id=(flipped(stn, stn_flips, step), chan), device_id_type=pl.DeviceIdType.MESH,
        )

    trips = {0: (0, 1), chunks - 2: (1, chunks - 2), chunks - 1: (chunks - 1, 1)}

    def block_copy(chunk, step):
        to_stn, to_chan = partner(step)
        batch = pl.ds(*trips[chunk])
        return pltpu.make_async_remote_copy(
            src_ref=send.at[to_stn * chan_count + to_chan, batch], dst_ref=recv.at[me, batch],
            send_sem=send_sem.at[chunk], recv_sem=recv_sem.at[chunk],
            device_id=(to_stn, to_chan), device_id_type=pl.DeviceIdType.MESH,
        )

    for load in loads[:3]:
        load.wait()
    for chunk in range(chunks):
        start = chunk * span
        low = 0 if chunk == 0 else start + taps
        high = min(start + span + taps, frames)

        def widen(a, carry, low=low, high=high):
            lanes = pl.ds(pl.multiple_of(a * LANES, LANES), LANES)
            pairs = volt[low:high, :, lanes].reshape(2 * (high - low), LANES)
            wide[a, 2 * low : 2 * high, :] = pairs.astype(jnp.float32)
            return carry

        if chunk == 1:
            loads[4].wait()
        lax.fori_loop(0, outer, widen, 0)

        def fir(a, carry, start=start):
            for part in range(2):
                def window(tap):
                    rows = wide[a, pl.ds(2 * (start + tap) + part, span, stride=2), :]
                    return rows.reshape(span // ROWS, ROWS, LANES)

                def weight(tap):
                    at = pl.multiple_of((a * taps + tap) * ROWS, ROWS)
                    return taper_ref[pl.ds(at, ROWS), :][None]

                total = weight(0) * window(0)
                for tap in range(1, taps):
                    total = total + weight(tap) * window(tap)
                filt[part, a] = total.reshape(span, LANES)
            return carry

        lax.fori_loop(0, outer, fir, 0)

        def first_stage(tile, carry):
            rows = pl.ds(pl.multiple_of(tile * ROWS, ROWS), ROWS)
            values = dft16([(filt[0, a, rows, :], filt[1, a, rows, :]) for a in range(outer)])
            for k in range(outer):
                re, im = values[k]
                c = twist_ref[k : k + 1, :]
                s = twist_ref[outer + k : outer + k + 1, :]
                mids[k, rows, 0:LANES] = re * c + im * s
                mids[k, rows, LANES:] = im * c - re * s
            return carry

        lax.fori_loop(0, span // ROWS, first_stage, 0)

        weights8 = jnp.zeros((ROWS, LANES), jnp.float32)
        for j in range(packed):
            shift = (span * j - start) % LANES
            rolled = pltpu.roll(flags8, shift, 1) if shift else flags8
            weights8 = jnp.where(lane8 // span == j, rolled, weights8)
        if chunk == 0:
            loads[3].wait()
            for half in range(2):
                columns = slice(half * LANES, (half + 1) * LANES)
                matrix_ref[:, columns] = matrix_f32[
                    2 * LANES * half : 2 * LANES * (half + 1)
                ].astype(jnp.bfloat16)
        for pair in range(groups // 2):
            halves = []
            for group in (2 * pair, 2 * pair + 1):
                data = mids[packed * group : packed * (group + 1)].reshape(LANES, 2 * LANES)
                spectrum = lax.dot_general(
                    matrix_ref[...], data.astype(jnp.bfloat16), (((1,), (1,)), ((), ())),
                    preferred_element_type=jnp.float32,
                )
                rounded = spectrum.astype(jnp.bfloat16).astype(jnp.float32)
                halves.append(rounded.reshape(devices, ROWS, LANES) * weights8[None])
            send[:, chunk, 2 * ROWS * pair : 2 * ROWS * (pair + 1), :] = jnp.concatenate(
                halves, axis=1
            ).astype(jnp.bfloat16)

        if chunk == 0:
            pl.semaphore_wait(barrier, devices - 1)
        recv[me, chunk] = send[me, chunk]
        if chunk not in trips:
            continue
        half = devices // 2
        for far in range(devices - 1, half - 1, -1):
            block_copy(chunk, far).start()
            if far > half:
                block_copy(chunk, far - half).start()
        if chunk == 0:
            for step in range(1, stn_count):
                meta_copy(step).start()

    told = meta.at[pl.ds(0, stn_count - 1)]
    pltpu.make_async_copy(told, told, meta_recv_sem).wait()
    tall = packed * devices
    exact = functools.partial(
        lax.dot_general, precision=lax.Precision.HIGHEST, preferred_element_type=jnp.float32
    )
    spread = (iota((tall, stn_count), 0) % devices // 2 == iota((tall, stn_count), 1)).astype(
        jnp.float32
    )
    all_flags = meta[:, 0, :]
    all_rows = meta[:, 1, :]
    weights = exact(spread, all_flags, (((1,), (0,)), ((), ())))
    count = exact(weights[:devices], weights, (((1,), (1,)), ((), ())))
    place = 2 * exact(spread, all_rows, (((1,), (0,)), ((), ()))).astype(jnp.int32)
    place = place + iota(place.shape, 0) % 2
    across = place.T
    lower = place[:devices] >= across[:devices]
    denom = jnp.maximum(count, 1.0)
    lane_at = iota((tall, tall), 1)
    columns = jnp.logical_and(
        place == lane_at % devices, iota((tall, tall), 0) // devices == lane_at // devices
    ).astype(jnp.bfloat16)
    rows = jnp.logical_and(
        across == iota((tall, tall), 0) % devices, iota((tall, tall), 0) // devices == lane_at // devices
    ).astype(jnp.bfloat16)
    lane = iota((devices, 2 * LANES), 1) % LANES // span
    for j in range(packed):
        masks[j] = (lane == j).astype(jnp.bfloat16)
    for chunk in range(chunks):
        for last, (low, size) in trips.items():
            if low == chunk:
                arrived = recv.at[pl.ds(0, devices - 1), pl.ds(low, size)]
                pltpu.make_async_copy(arrived, arrived, recv_sem.at[last]).wait()
        for source in range(devices):
            at = source * (block + 1)
            gathered[at : at + block, :] = recv[source, chunk].astype(jnp.float32)
        for quad in range(quads):
            for group in range(groups):
                at = group * ROWS + quad
                re = gathered[pl.ds(at, devices, stride=block + 1), :].astype(jnp.bfloat16)
                im = gathered[pl.ds(at + quads, devices, stride=block + 1), :].astype(jnp.bfloat16)
                plain = jnp.concatenate([re, im], axis=1)
                turned = jnp.concatenate([im, -re], axis=1)
                left = jnp.concatenate([plain, turned], axis=0)
                right = jnp.concatenate([plain * masks[j] for j in range(packed)], axis=0)
                product = lax.dot_general(
                    left, right, (((1,), (1,)), ((), ())), preferred_element_type=jnp.float32
                )
                if chunk == 0:
                    acc[quad * groups + group] = product
                else:
                    acc[quad * groups + group] += product

    for first in range(0, quads * groups, packed):
        chosen = [
            jnp.where(lower, acc[g, :devices], acc[g, devices:]) / denom
            for g in range(first, first + packed)
        ]
        moved = jnp.dot(
            jnp.concatenate(chosen, axis=0).astype(jnp.bfloat16),
            columns,
            preferred_element_type=jnp.float32,
        )
        moved = jnp.dot(
            rows, moved.astype(jnp.bfloat16), preferred_element_type=jnp.float32
        ).astype(jnp.bfloat16)
        for g in range(packed):
            for j in range(packed):
                out_ref[packed * (first + g) + j] = moved[
                    devices * g : devices * (g + 1), devices * j : devices * (j + 1)
                ]

    for last, (low, size) in trips.items():
        gone = send.at[pl.ds(0, devices - 1), pl.ds(low, size)]
        pltpu.make_async_copy(gone, gone, send_sem.at[last]).wait()
    pltpu.make_async_copy(told, told, meta_send_sem).wait()


def fused(voltages, flags, station_row, stn_count, chan_count):
    devices = stn_count * chan_count
    frames, lanes = voltages.shape[2], voltages.shape[3]
    spectra = flags.shape[1]
    taps = frames - spectra + 1
    outer = lanes // LANES
    chunks = 4
    span = spectra // chunks
    packed = LANES // span
    block = outer // packed * ROWS
    table = host_tables(taps, lanes, devices)
    vmem = pl.BlockSpec(memory_space=pltpu.VMEM)
    hbm = pl.BlockSpec(memory_space=pl.ANY)
    f32, bf16 = jnp.float32, jnp.bfloat16
    return pl.pallas_call(
        functools.partial(kernel, stn_count, chan_count, chunks),
        out_shape=jax.ShapeDtypeStruct((lanes // devices, devices, devices), bf16),
        in_specs=[
            hbm,
            pl.BlockSpec(memory_space=pltpu.SMEM),
            pl.BlockSpec(memory_space=pltpu.SMEM),
            hbm,
        ],
        out_specs=vmem,
        scratch_shapes=[
            pltpu.VMEM((frames, 2, lanes), bf16),
            pltpu.VMEM((outer * taps * ROWS, LANES), f32),
            pltpu.VMEM((2 * outer, LANES), f32),
            pltpu.VMEM((4 * LANES, LANES), f32),
            pltpu.VMEM((2 * LANES, 2 * LANES), bf16),
            pltpu.VMEM((outer, 2 * frames, LANES), f32),
            pltpu.VMEM((2, outer, span, LANES), f32),
            pltpu.VMEM((outer, span, 2 * LANES), f32),
            pltpu.VMEM((devices, chunks, block, LANES), bf16),
            pltpu.VMEM((devices, chunks, block, LANES), bf16),
            pltpu.VMEM((stn_count, ROWS, LANES), f32),
            pltpu.VMEM((devices * (block + 1), LANES), f32),
            pltpu.VMEM((packed, devices, 2 * LANES), bf16),
            pltpu.VMEM((outer * (LANES // devices) // packed, 2 * devices, packed * devices), f32),
            pltpu.SemaphoreType.DMA((5,)),
            pltpu.SemaphoreType.DMA((chunks,)),
            pltpu.SemaphoreType.DMA((chunks,)),
            pltpu.SemaphoreType.DMA,
            pltpu.SemaphoreType.DMA,
        ],
        compiler_params=pltpu.CompilerParams(
            collective_id=0, has_side_effects=True, vmem_limit_bytes=53 * 1024 * 1024
        ),
    )(jnp.transpose(voltages, (0, 2, 1, 3)), flags, station_row, table)


def solution(mesh):
    placed = (P(("stn", "chan"), None, None, None), P("stn", None), P("stn"))
    return jax.shard_map(
        on_device,
        mesh=mesh,
        in_specs=placed,
        out_specs=P(("stn", "chan"), None, None),
        check_vma=False,
    )
```

```python
import functools
import math

import jax
import jax.numpy as jnp
import numpy as np
from jax import lax
from jax.experimental import pallas as pl
from jax.experimental.pallas import tpu as pltpu
from jax.sharding import PartitionSpec as P

LANES = 128
ROWS = 8


def filter_table(taps, lanes):
    total = taps * lanes
    places = jnp.arange(total, dtype=jnp.float32) + 0.5
    window = 0.5 - 0.5 * jnp.cos(2.0 * math.pi * places / total)
    return (jnp.sinc((places - 0.5 * total) / lanes) * window).reshape(taps, lanes)


def dft_tables(length):
    places = jnp.arange(length, dtype=jnp.int32)
    product = places[:, None] * places[None, :] % length
    angle = 2.0 * math.pi * product.astype(jnp.float32) / length
    return (jnp.cos(angle), jnp.sin(angle))


def twiddle_tables(outer, inner):
    product = (
        jnp.arange(outer, dtype=jnp.int32)[:, None]
        * jnp.arange(inner, dtype=jnp.int32)[None, :]
        % (outer * inner)
    )
    angle = 2.0 * math.pi * product.astype(jnp.float32) / (outer * inner)
    return (jnp.cos(angle), jnp.sin(angle))


def contract(form, left, right):
    return jnp.einsum(form, left, right, precision=lax.Precision.HIGHEST)


def channelize(voltages, spectra_count):
    inputs_here = voltages.shape[0]
    lanes = voltages.shape[3]
    taps = voltages.shape[2] - spectra_count + 1
    taps_table = filter_table(taps, lanes)
    real_acc = taps_table[0] * voltages[:, 0, 0:spectra_count, :].astype(jnp.float32)
    imag_acc = taps_table[0] * voltages[:, 1, 0:spectra_count, :].astype(jnp.float32)
    for tap_index in range(1, taps):
        real_acc = real_acc + taps_table[tap_index] * voltages[
            :, 0, tap_index : tap_index + spectra_count, :
        ].astype(jnp.float32)
        imag_acc = imag_acc + taps_table[tap_index] * voltages[
            :, 1, tap_index : tap_index + spectra_count, :
        ].astype(jnp.float32)
    inner = 128
    outer = lanes // inner
    real_grid = real_acc.reshape(inputs_here, spectra_count, outer, inner)
    imag_grid = imag_acc.reshape(inputs_here, spectra_count, outer, inner)
    cos_outer, sin_outer = dft_tables(outer)
    real_mid = contract("gtmn,mk->gtkn", real_grid, cos_outer) + contract(
        "gtmn,mk->gtkn", imag_grid, sin_outer
    )
    imag_mid = contract("gtmn,mk->gtkn", imag_grid, cos_outer) - contract(
        "gtmn,mk->gtkn", real_grid, sin_outer
    )
    cos_twist, sin_twist = twiddle_tables(outer, inner)
    real_twisted = real_mid * cos_twist + imag_mid * sin_twist
    imag_twisted = imag_mid * cos_twist - real_mid * sin_twist
    cos_inner, sin_inner = dft_tables(inner)
    real_out = contract("gtkn,nj->jkgt", real_twisted, cos_inner) + contract(
        "gtkn,nj->jkgt", imag_twisted, sin_inner
    )
    imag_out = contract("gtkn,nj->jkgt", imag_twisted, cos_inner) - contract(
        "gtkn,nj->jkgt", real_twisted, sin_inner
    )
    scale = 1.0 / math.sqrt(lanes)
    stacked = (jnp.stack([real_out, imag_out], axis=3) * scale).astype(jnp.bfloat16)
    return stacked.reshape(lanes, inputs_here, 2 * spectra_count)


def square_products(plain, turned):
    real_part = jnp.einsum("cat,cbt->cab", plain, plain, preferred_element_type=jnp.float32)
    imag_part = jnp.einsum("cat,cbt->cab", plain, turned, preferred_element_type=jnp.float32)
    return (real_part, imag_part)


def on_device(voltages, flags, station_row):
    spectra_count = flags.shape[1]
    inputs_here = voltages.shape[0]
    lanes = voltages.shape[3]
    stn_count = lax.axis_size("stn")
    chan_count = lax.axis_size("chan")
    per_device = lanes // (stn_count * chan_count)
    total_inputs = inputs_here * stn_count * chan_count
    if (
        total_inputs == 32
        and inputs_here == 1
        and chan_count == 2
        and lanes == 16 * LANES
        and spectra_count == LANES
    ):
        return fused(voltages, flags, station_row, stn_count, chan_count)
    flags_all, rows_all = (
        lax.all_gather(flags, "stn", axis=0, tiled=True),
        lax.all_gather(station_row, "stn", axis=0, tiled=True),
    )
    spectra = channelize(voltages, spectra_count)
    grouped = spectra.reshape(stn_count, chan_count, per_device, inputs_here, 2 * spectra_count)
    order = jnp.argsort(rows_all)
    rows = jnp.arange(total_inputs, dtype=jnp.int32)
    station_of = order[rows // 2]
    source = 2 * station_of + rows % 2
    moved = lax.all_to_all(
        lax.all_to_all(grouped, "stn", split_axis=0, concat_axis=3, tiled=True),
        "chan",
        split_axis=1,
        concat_axis=3,
        tiled=True,
    )
    from_stn = source // (chan_count * inputs_here)
    from_chan = source // inputs_here % chan_count
    within = source % inputs_here
    placed = from_chan * (stn_count * inputs_here) + from_stn * inputs_here + within
    arrived = moved.reshape(per_device, total_inputs, 2, spectra_count)
    weights = jnp.take(flags_all, station_of, axis=0)
    kept = (
        jnp.take(arrived, placed, axis=1).astype(jnp.float32) * weights[None, :, None, :]
    ).astype(jnp.bfloat16)
    plain = kept.reshape(per_device, total_inputs, 2 * spectra_count)
    turned = jnp.concatenate([-kept[:, :, 1], kept[:, :, 0]], axis=-1)
    count = jnp.dot(
        weights, weights.T, preferred_element_type=jnp.float32, precision=lax.Precision.HIGHEST
    )
    denom = jnp.maximum(count, 1.0)
    real_part, imag_part = square_products(plain, turned)
    below = rows[:, None] >= rows[None, :]
    return jnp.where(below[None], real_part / denom, imag_part / denom).astype(jnp.bfloat16)


def host_tables(taps, lanes, devices):
    outer = lanes // LANES
    quads = LANES // devices
    total = taps * lanes
    places = np.arange(total) + 0.5
    window = 0.5 - 0.5 * np.cos(2.0 * np.pi * places / total)
    taper = (np.sinc((places - 0.5 * total) / lanes) * window).reshape(taps, outer, LANES)
    taper = taper.transpose(1, 0, 2)
    angle = 2.0 * np.pi * (np.arange(outer)[:, None] * np.arange(LANES)[None, :]) / lanes
    scale = 1.0 / math.sqrt(lanes)
    twist = np.stack([np.cos(angle), np.sin(angle)]) * scale
    turn = 2.0 * np.pi * (np.arange(LANES)[:, None] * np.arange(LANES)[None, :] % LANES) / LANES
    cos, sin = np.cos(turn), np.sin(turn)
    real_rows = np.concatenate([cos, sin], axis=1).reshape(devices, 1, quads, 2 * LANES)
    imag_rows = np.concatenate([-sin, cos], axis=1).reshape(devices, 1, quads, 2 * LANES)
    matrix = np.concatenate([real_rows, imag_rows], axis=1).reshape(2 * LANES, 2 * LANES)
    rows = [
        np.repeat(taper.reshape(outer * taps, LANES), ROWS, axis=0),
        twist.reshape(2 * outer, LANES),
        matrix.astype(jnp.bfloat16).astype(np.float32)[:, :LANES],
        matrix.astype(jnp.bfloat16).astype(np.float32)[:, LANES:],
    ]
    return jnp.asarray(np.concatenate(rows, axis=0).astype(np.float32))


def dft4(a, b, c, d):
    s0 = (a[0] + c[0], a[1] + c[1])
    s1 = (a[0] - c[0], a[1] - c[1])
    s2 = (b[0] + d[0], b[1] + d[1])
    s3 = (b[0] - d[0], b[1] - d[1])
    return (
        (s0[0] + s2[0], s0[1] + s2[1]),
        (s1[0] + s3[1], s1[1] - s3[0]),
        (s0[0] - s2[0], s0[1] - s2[1]),
        (s1[0] - s3[1], s1[1] + s3[0]),
    )


def dft16(x):
    half = math.sqrt(0.5)
    mids = [dft4(x[p], x[4 + p], x[8 + p], x[12 + p]) for p in range(4)]
    out = [None] * 16
    for kx in range(4):
        turned = []
        for p in range(4):
            re, im = mids[p][kx]
            e = p * kx
            if e == 0:
                turned.append((re, im))
            elif e == 4:
                turned.append((im, -re))
            elif e == 2:
                turned.append(((re + im) * half, (im - re) * half))
            elif e == 6:
                turned.append(((im - re) * half, -(re + im) * half))
            else:
                c, s = math.cos(2 * math.pi * e / 16), math.sin(2 * math.pi * e / 16)
                turned.append((re * c + im * s, im * c - re * s))
        for ky, value in enumerate(dft4(*turned)):
            out[kx + 4 * ky] = value
    return out


def iota(shape, dim):
    return lax.broadcasted_iota(jnp.int32, shape, dim)


def kernel(
    stn_count, chan_count, chunks,
    volt_hbm, flags_ref, row_ref, table_hbm, out_ref,
    volt, taper_ref, twist_ref, matrix_f32, matrix_ref,
    wide, filt, mids, send, recv, meta, gathered, masks, acc,
    load_sem, send_sem, recv_sem, meta_send_sem, meta_recv_sem,
):
    devices = stn_count * chan_count
    frames = volt.shape[0]
    spectra = flags_ref.shape[1]
    taps = frames - spectra + 1
    outer = volt.shape[2] // LANES
    span = spectra // chunks
    packed = LANES // span
    groups = outer // packed
    quads = LANES // devices
    block = groups * ROWS
    stn, chan = lax.axis_index("stn"), lax.axis_index("chan")
    me = stn * chan_count + chan

    first_frames = spectra // chunks + taps
    head, rest = pl.ds(0, first_frames), pl.ds(first_frames, frames - first_frames)
    taper_rows, twist_rows, matrix_rows = outer * taps * ROWS, 2 * outer, 4 * LANES
    sources = (
        (volt_hbm.at[0, head], volt.at[head]),
        (table_hbm.at[pl.ds(0, taper_rows)], taper_ref),
        (table_hbm.at[pl.ds(taper_rows, twist_rows)], twist_ref),
        (table_hbm.at[pl.ds(taper_rows + twist_rows, matrix_rows)], matrix_f32),
        (volt_hbm.at[0, rest], volt.at[rest]),
    )
    loads = [
        pltpu.make_async_copy(source, target, load_sem.at[k])
        for k, (source, target) in enumerate(sources)
    ]
    for load in loads:
        load.start()

    stn_flips = [
        (1 - 2 * (stn // 2**bit % 2)) * 2**bit for bit in range(stn_count.bit_length() - 1)
    ]
    chan_flips = [
        (1 - 2 * (chan // 2**bit % 2)) * 2**bit for bit in range(chan_count.bit_length() - 1)
    ]

    def flipped(start, flips, step):
        for bit, flip in enumerate(flips):
            if step >> bit & 1:
                start = start + flip
        return start

    def partner(step):
        return (
            flipped(stn, stn_flips, step // chan_count),
            flipped(chan, chan_flips, step % chan_count),
        )

    barrier = pltpu.get_barrier_semaphore()
    for step in range(1, devices):
        pl.semaphore_signal(
            barrier, inc=1, device_id=partner(step), device_id_type=pl.DeviceIdType.MESH
        )

    lane8 = iota((ROWS, LANES), 1)
    flags8 = lax.fori_loop(
        0, spectra, lambda t, held: jnp.where(lane8 == t, flags_ref[0, t], held),
        jnp.zeros((ROWS, LANES), jnp.float32), unroll=8,
    )
    station = jnp.broadcast_to(row_ref[0], (ROWS, LANES)).astype(jnp.float32)
    meta[stn] = jnp.where(iota((ROWS, LANES), 0) == 0, flags8, station)

    def meta_copy(step):
        return pltpu.make_async_remote_copy(
            src_ref=meta.at[stn], dst_ref=meta.at[stn],
            send_sem=meta_send_sem, recv_sem=meta_recv_sem,
            device_id=(flipped(stn, stn_flips, step), chan), device_id_type=pl.DeviceIdType.MESH,
        )

    def block_copy(chunk, step):
        to_stn, to_chan = partner(step)
        return pltpu.make_async_remote_copy(
            src_ref=send.at[chunk, to_stn * chan_count + to_chan], dst_ref=recv.at[chunk, me],
            send_sem=send_sem.at[chunk], recv_sem=recv_sem.at[chunk],
            device_id=(to_stn, to_chan), device_id_type=pl.DeviceIdType.MESH,
        )

    for load in loads[:3]:
        load.wait()
    for chunk in range(chunks):
        start = chunk * span
        low = 0 if chunk == 0 else start + taps
        high = min(start + span + taps, frames)

        def widen(a, carry, low=low, high=high):
            lanes = pl.ds(pl.multiple_of(a * LANES, LANES), LANES)
            pairs = volt[low:high, :, lanes].reshape(2 * (high - low), LANES)
            wide[a, 2 * low : 2 * high, :] = pairs.astype(jnp.float32)
            return carry

        if chunk == 1:
            loads[4].wait()
        lax.fori_loop(0, outer, widen, 0, unroll=4)

        def fir(a, carry, start=start):
            for part in range(2):
                def window(tap):
                    rows = wide[a, pl.ds(2 * (start + tap) + part, span, stride=2), :]
                    return rows.reshape(span // ROWS, ROWS, LANES)

                def weight(tap):
                    at = pl.multiple_of((a * taps + tap) * ROWS, ROWS)
                    return taper_ref[pl.ds(at, ROWS), :][None]

                total = weight(0) * window(0)
                for tap in range(1, taps):
                    total = total + weight(tap) * window(tap)
                filt[part, a] = total.reshape(span, LANES)
            return carry

        lax.fori_loop(0, outer, fir, 0, unroll=2)

        def first_stage(tile, carry):
            rows = pl.ds(pl.multiple_of(tile * ROWS, ROWS), ROWS)
            values = dft16([(filt[0, a, rows, :], filt[1, a, rows, :]) for a in range(outer)])
            for k in range(outer):
                re, im = values[k]
                c = twist_ref[k : k + 1, :]
                s = twist_ref[outer + k : outer + k + 1, :]
                mids[k, rows, 0:LANES] = re * c + im * s
                mids[k, rows, LANES:] = im * c - re * s
            return carry

        lax.fori_loop(0, span // ROWS, first_stage, 0, unroll=2)

        weights8 = jnp.zeros((ROWS, LANES), jnp.float32)
        for j in range(packed):
            shift = (span * j - start) % LANES
            rolled = pltpu.roll(flags8, shift, 1) if shift else flags8
            weights8 = jnp.where(lane8 // span == j, rolled, weights8)
        if chunk == 0:
            loads[3].wait()
            for half in range(2):
                columns = slice(half * LANES, (half + 1) * LANES)
                matrix_ref[:, columns] = matrix_f32[
                    2 * LANES * half : 2 * LANES * (half + 1)
                ].astype(jnp.bfloat16)
        for pair in range(groups // 2):
            halves = []
            for group in (2 * pair, 2 * pair + 1):
                data = mids[packed * group : packed * (group + 1)].reshape(LANES, 2 * LANES)
                spectrum = lax.dot_general(
                    matrix_ref[...], data.astype(jnp.bfloat16), (((1,), (1,)), ((), ())),
                    preferred_element_type=jnp.float32,
                )
                rounded = spectrum.astype(jnp.bfloat16).astype(jnp.float32)
                halves.append(rounded.reshape(devices, ROWS, LANES) * weights8[None])
            send[chunk, :, 2 * ROWS * pair : 2 * ROWS * (pair + 1), :] = jnp.concatenate(
                halves, axis=1
            ).astype(jnp.bfloat16)

        if chunk == 0:
            pl.semaphore_wait(barrier, devices - 1)
        half = devices // 2
        for far in range(devices - 1, half - 1, -1):
            block_copy(chunk, far).start()
            if far > half:
                block_copy(chunk, far - half).start()
        if chunk == 0:
            for step in range(1, stn_count):
                meta_copy(step).start()
        recv[chunk, me] = send[chunk, me]

    told = meta.at[pl.ds(0, stn_count - 1)]
    pltpu.make_async_copy(told, told, meta_recv_sem).wait()
    tall = packed * devices
    exact = functools.partial(
        lax.dot_general, precision=lax.Precision.HIGHEST, preferred_element_type=jnp.float32
    )
    spread = (iota((tall, stn_count), 0) % devices // 2 == iota((tall, stn_count), 1)).astype(
        jnp.float32
    )
    all_flags = meta[:, 0, :]
    all_rows = meta[:, 1, :]
    weights = exact(spread, all_flags, (((1,), (0,)), ((), ())))
    count = exact(weights[:devices], weights, (((1,), (1,)), ((), ())))
    place = 2 * exact(spread, all_rows, (((1,), (0,)), ((), ()))).astype(jnp.int32)
    place = place + iota(place.shape, 0) % 2
    across = place.T
    lower = place[:devices] >= across[:devices]
    denom = jnp.maximum(count, 1.0)
    lane_at = iota((tall, tall), 1)
    columns = jnp.logical_and(
        place == lane_at % devices, iota((tall, tall), 0) // devices == lane_at // devices
    ).astype(jnp.bfloat16)
    rows = jnp.logical_and(
        across == iota((tall, tall), 0) % devices, iota((tall, tall), 0) // devices == lane_at // devices
    ).astype(jnp.bfloat16)
    lane = iota((devices, 2 * LANES), 1) % LANES // span
    for j in range(packed):
        masks[j] = (lane == j).astype(jnp.bfloat16)
    for chunk in range(chunks):
        arrived = recv.at[chunk, pl.ds(0, devices - 1)]
        pltpu.make_async_copy(arrived, arrived, recv_sem.at[chunk]).wait()
        gathered[...] = recv[chunk].reshape(devices * block, LANES).astype(jnp.float32)
        for quad in range(quads):
            for group in range(groups):
                at = group * ROWS + quad
                re = gathered[pl.ds(at, devices, stride=block), :].astype(jnp.bfloat16)
                im = gathered[pl.ds(at + quads, devices, stride=block), :].astype(jnp.bfloat16)
                plain = jnp.concatenate([re, im], axis=1)
                turned = jnp.concatenate([im, -re], axis=1)
                left = jnp.concatenate([plain, turned], axis=0)
                right = jnp.concatenate([plain * masks[j] for j in range(packed)], axis=0)
                product = lax.dot_general(
                    left, right, (((1,), (1,)), ((), ())), preferred_element_type=jnp.float32
                )
                if chunk == 0:
                    acc[quad * groups + group] = product
                else:
                    acc[quad * groups + group] += product

    for first in range(0, quads * groups, packed):
        chosen = [
            jnp.where(lower, acc[g, :devices], acc[g, devices:]) / denom
            for g in range(first, first + packed)
        ]
        moved = jnp.dot(
            jnp.concatenate(chosen, axis=0).astype(jnp.bfloat16),
            columns,
            preferred_element_type=jnp.float32,
        )
        moved = jnp.dot(
            rows, moved.astype(jnp.bfloat16), preferred_element_type=jnp.float32
        ).astype(jnp.bfloat16)
        for g in range(packed):
            for j in range(packed):
                out_ref[packed * (first + g) + j] = moved[
                    devices * g : devices * (g + 1), devices * j : devices * (j + 1)
                ]

    for chunk in range(chunks):
        gone = send.at[chunk, pl.ds(0, devices - 1)]
        pltpu.make_async_copy(gone, gone, send_sem.at[chunk]).wait()
    pltpu.make_async_copy(told, told, meta_send_sem).wait()


def fused(voltages, flags, station_row, stn_count, chan_count):
    devices = stn_count * chan_count
    frames, lanes = voltages.shape[2], voltages.shape[3]
    spectra = flags.shape[1]
    taps = frames - spectra + 1
    outer = lanes // LANES
    chunks = 4
    span = spectra // chunks
    packed = LANES // span
    block = outer // packed * ROWS
    table = host_tables(taps, lanes, devices)
    vmem = pl.BlockSpec(memory_space=pltpu.VMEM)
    hbm = pl.BlockSpec(memory_space=pl.ANY)
    f32, bf16 = jnp.float32, jnp.bfloat16
    return pl.pallas_call(
        functools.partial(kernel, stn_count, chan_count, chunks),
        out_shape=jax.ShapeDtypeStruct((lanes // devices, devices, devices), bf16),
        in_specs=[
            hbm,
            pl.BlockSpec(memory_space=pltpu.SMEM),
            pl.BlockSpec(memory_space=pltpu.SMEM),
            hbm,
        ],
        out_specs=vmem,
        scratch_shapes=[
            pltpu.VMEM((frames, 2, lanes), bf16),
            pltpu.VMEM((outer * taps * ROWS, LANES), f32),
            pltpu.VMEM((2 * outer, LANES), f32),
            pltpu.VMEM((4 * LANES, LANES), f32),
            pltpu.VMEM((2 * LANES, 2 * LANES), bf16),
            pltpu.VMEM((outer, 2 * frames, LANES), f32),
            pltpu.VMEM((2, outer, span, LANES), f32),
            pltpu.VMEM((outer, span, 2 * LANES), f32),
            pltpu.VMEM((chunks, devices, block, LANES), bf16),
            pltpu.VMEM((chunks, devices, block, LANES), bf16),
            pltpu.VMEM((stn_count, ROWS, LANES), f32),
            pltpu.VMEM((devices * block, LANES), f32),
            pltpu.VMEM((packed, devices, 2 * LANES), bf16),
            pltpu.VMEM((outer * (LANES // devices) // packed, 2 * devices, packed * devices), f32),
            pltpu.SemaphoreType.DMA((5,)),
            pltpu.SemaphoreType.DMA((chunks,)),
            pltpu.SemaphoreType.DMA((chunks,)),
            pltpu.SemaphoreType.DMA,
            pltpu.SemaphoreType.DMA,
        ],
        compiler_params=pltpu.CompilerParams(
            collective_id=0, has_side_effects=True, vmem_limit_bytes=53 * 1024 * 1024
        ),
    )(jnp.transpose(voltages, (0, 2, 1, 3)), flags, station_row, table)


def solution(mesh):
    placed = (P(("stn", "chan"), None, None, None), P("stn", None), P("stn"))
    return jax.shard_map(
        on_device,
        mesh=mesh,
        in_specs=placed,
        out_specs=P(("stn", "chan"), None, None),
        check_vma=False,
    )
```

```python
import functools
import math

import jax
import jax.numpy as jnp
import numpy as np
from jax import lax
from jax.experimental import pallas as pl
from jax.experimental.pallas import tpu as pltpu
from jax.sharding import PartitionSpec as P

LANES = 128
ROWS = 8


def filter_table(taps, lanes):
    total = taps * lanes
    places = jnp.arange(total, dtype=jnp.float32) + 0.5
    window = 0.5 - 0.5 * jnp.cos(2.0 * math.pi * places / total)
    return (jnp.sinc((places - 0.5 * total) / lanes) * window).reshape(taps, lanes)


def dft_tables(length):
    places = jnp.arange(length, dtype=jnp.int32)
    product = places[:, None] * places[None, :] % length
    angle = 2.0 * math.pi * product.astype(jnp.float32) / length
    return (jnp.cos(angle), jnp.sin(angle))


def twiddle_tables(outer, inner):
    product = (
        jnp.arange(outer, dtype=jnp.int32)[:, None]
        * jnp.arange(inner, dtype=jnp.int32)[None, :]
        % (outer * inner)
    )
    angle = 2.0 * math.pi * product.astype(jnp.float32) / (outer * inner)
    return (jnp.cos(angle), jnp.sin(angle))


def contract(form, left, right):
    return jnp.einsum(form, left, right, precision=lax.Precision.HIGHEST)


def channelize(voltages, spectra_count):
    inputs_here = voltages.shape[0]
    lanes = voltages.shape[3]
    taps = voltages.shape[2] - spectra_count + 1
    taps_table = filter_table(taps, lanes)
    real_acc = taps_table[0] * voltages[:, 0, 0:spectra_count, :].astype(jnp.float32)
    imag_acc = taps_table[0] * voltages[:, 1, 0:spectra_count, :].astype(jnp.float32)
    for tap_index in range(1, taps):
        real_acc = real_acc + taps_table[tap_index] * voltages[
            :, 0, tap_index : tap_index + spectra_count, :
        ].astype(jnp.float32)
        imag_acc = imag_acc + taps_table[tap_index] * voltages[
            :, 1, tap_index : tap_index + spectra_count, :
        ].astype(jnp.float32)
    inner = 128
    outer = lanes // inner
    real_grid = real_acc.reshape(inputs_here, spectra_count, outer, inner)
    imag_grid = imag_acc.reshape(inputs_here, spectra_count, outer, inner)
    cos_outer, sin_outer = dft_tables(outer)
    real_mid = contract("gtmn,mk->gtkn", real_grid, cos_outer) + contract(
        "gtmn,mk->gtkn", imag_grid, sin_outer
    )
    imag_mid = contract("gtmn,mk->gtkn", imag_grid, cos_outer) - contract(
        "gtmn,mk->gtkn", real_grid, sin_outer
    )
    cos_twist, sin_twist = twiddle_tables(outer, inner)
    real_twisted = real_mid * cos_twist + imag_mid * sin_twist
    imag_twisted = imag_mid * cos_twist - real_mid * sin_twist
    cos_inner, sin_inner = dft_tables(inner)
    real_out = contract("gtkn,nj->jkgt", real_twisted, cos_inner) + contract(
        "gtkn,nj->jkgt", imag_twisted, sin_inner
    )
    imag_out = contract("gtkn,nj->jkgt", imag_twisted, cos_inner) - contract(
        "gtkn,nj->jkgt", real_twisted, sin_inner
    )
    scale = 1.0 / math.sqrt(lanes)
    stacked = (jnp.stack([real_out, imag_out], axis=3) * scale).astype(jnp.bfloat16)
    return stacked.reshape(lanes, inputs_here, 2 * spectra_count)


def square_products(plain, turned):
    real_part = jnp.einsum("cat,cbt->cab", plain, plain, preferred_element_type=jnp.float32)
    imag_part = jnp.einsum("cat,cbt->cab", plain, turned, preferred_element_type=jnp.float32)
    return (real_part, imag_part)


def on_device(voltages, flags, station_row):
    spectra_count = flags.shape[1]
    inputs_here = voltages.shape[0]
    lanes = voltages.shape[3]
    stn_count = lax.axis_size("stn")
    chan_count = lax.axis_size("chan")
    per_device = lanes // (stn_count * chan_count)
    total_inputs = inputs_here * stn_count * chan_count
    if (
        total_inputs == 32
        and inputs_here == 1
        and chan_count == 2
        and lanes == 16 * LANES
        and spectra_count == LANES
    ):
        return fused(voltages, flags, station_row, stn_count, chan_count)
    flags_all, rows_all = (
        lax.all_gather(flags, "stn", axis=0, tiled=True),
        lax.all_gather(station_row, "stn", axis=0, tiled=True),
    )
    spectra = channelize(voltages, spectra_count)
    grouped = spectra.reshape(stn_count, chan_count, per_device, inputs_here, 2 * spectra_count)
    order = jnp.argsort(rows_all)
    rows = jnp.arange(total_inputs, dtype=jnp.int32)
    station_of = order[rows // 2]
    source = 2 * station_of + rows % 2
    moved = lax.all_to_all(
        lax.all_to_all(grouped, "stn", split_axis=0, concat_axis=3, tiled=True),
        "chan",
        split_axis=1,
        concat_axis=3,
        tiled=True,
    )
    from_stn = source // (chan_count * inputs_here)
    from_chan = source // inputs_here % chan_count
    within = source % inputs_here
    placed = from_chan * (stn_count * inputs_here) + from_stn * inputs_here + within
    arrived = moved.reshape(per_device, total_inputs, 2, spectra_count)
    weights = jnp.take(flags_all, station_of, axis=0)
    kept = (
        jnp.take(arrived, placed, axis=1).astype(jnp.float32) * weights[None, :, None, :]
    ).astype(jnp.bfloat16)
    plain = kept.reshape(per_device, total_inputs, 2 * spectra_count)
    turned = jnp.concatenate([-kept[:, :, 1], kept[:, :, 0]], axis=-1)
    count = jnp.dot(
        weights, weights.T, preferred_element_type=jnp.float32, precision=lax.Precision.HIGHEST
    )
    denom = jnp.maximum(count, 1.0)
    real_part, imag_part = square_products(plain, turned)
    below = rows[:, None] >= rows[None, :]
    return jnp.where(below[None], real_part / denom, imag_part / denom).astype(jnp.bfloat16)


def host_tables(taps, lanes, devices):
    outer = lanes // LANES
    quads = LANES // devices
    total = taps * lanes
    places = np.arange(total) + 0.5
    window = 0.5 - 0.5 * np.cos(2.0 * np.pi * places / total)
    taper = (np.sinc((places - 0.5 * total) / lanes) * window).reshape(taps, outer, LANES)
    taper = taper.transpose(1, 0, 2)
    angle = 2.0 * np.pi * (np.arange(outer)[:, None] * np.arange(LANES)[None, :]) / lanes
    scale = 1.0 / math.sqrt(lanes)
    twist = np.stack([np.cos(angle), np.sin(angle)]) * scale
    turn = 2.0 * np.pi * (np.arange(LANES)[:, None] * np.arange(LANES)[None, :] % LANES) / LANES
    cos, sin = np.cos(turn), np.sin(turn)
    real_rows = np.concatenate([cos, sin], axis=1).reshape(devices, 1, quads, 2 * LANES)
    imag_rows = np.concatenate([-sin, cos], axis=1).reshape(devices, 1, quads, 2 * LANES)
    matrix = np.concatenate([real_rows, imag_rows], axis=1).reshape(2 * LANES, 2 * LANES)
    rows = [
        np.repeat(taper.reshape(outer * taps, LANES), ROWS, axis=0),
        twist.reshape(2 * outer, LANES),
        matrix.astype(jnp.bfloat16).astype(np.float32)[:, :LANES],
        matrix.astype(jnp.bfloat16).astype(np.float32)[:, LANES:],
    ]
    return jnp.asarray(np.concatenate(rows, axis=0).astype(np.float32))


def dft4(a, b, c, d):
    s0 = (a[0] + c[0], a[1] + c[1])
    s1 = (a[0] - c[0], a[1] - c[1])
    s2 = (b[0] + d[0], b[1] + d[1])
    s3 = (b[0] - d[0], b[1] - d[1])
    return (
        (s0[0] + s2[0], s0[1] + s2[1]),
        (s1[0] + s3[1], s1[1] - s3[0]),
        (s0[0] - s2[0], s0[1] - s2[1]),
        (s1[0] - s3[1], s1[1] + s3[0]),
    )


def dft16(x):
    half = math.sqrt(0.5)
    mids = [dft4(x[p], x[4 + p], x[8 + p], x[12 + p]) for p in range(4)]
    out = [None] * 16
    for kx in range(4):
        turned = []
        for p in range(4):
            re, im = mids[p][kx]
            e = p * kx
            if e == 0:
                turned.append((re, im))
            elif e == 4:
                turned.append((im, -re))
            elif e == 2:
                turned.append(((re + im) * half, (im - re) * half))
            elif e == 6:
                turned.append(((im - re) * half, -(re + im) * half))
            else:
                c, s = math.cos(2 * math.pi * e / 16), math.sin(2 * math.pi * e / 16)
                turned.append((re * c + im * s, im * c - re * s))
        for ky, value in enumerate(dft4(*turned)):
            out[kx + 4 * ky] = value
    return out


def iota(shape, dim):
    return lax.broadcasted_iota(jnp.int32, shape, dim)


def kernel(
    stn_count, chan_count, chunks,
    volt_hbm, flags_ref, row_ref, table_hbm, out_ref,
    volt, taper_ref, twist_ref, matrix_f32, matrix_ref,
    wide, filt, mids, send, recv, meta, gathered, masks, acc,
    load_sem, send_sem, recv_sem, meta_send_sem, meta_recv_sem,
):
    devices = stn_count * chan_count
    frames = volt.shape[0]
    spectra = flags_ref.shape[1]
    taps = frames - spectra + 1
    outer = volt.shape[2] // LANES
    span = spectra // chunks
    packed = LANES // span
    groups = outer // packed
    quads = LANES // devices
    block = groups * ROWS
    stn, chan = lax.axis_index("stn"), lax.axis_index("chan")
    me = stn * chan_count + chan

    first_frames = spectra // chunks + taps
    head, rest = pl.ds(0, first_frames), pl.ds(first_frames, frames - first_frames)
    taper_rows, twist_rows, matrix_rows = outer * taps * ROWS, 2 * outer, 4 * LANES
    sources = (
        (volt_hbm.at[0, head], volt.at[head]),
        (table_hbm.at[pl.ds(0, taper_rows)], taper_ref),
        (table_hbm.at[pl.ds(taper_rows, twist_rows)], twist_ref),
        (table_hbm.at[pl.ds(taper_rows + twist_rows, matrix_rows)], matrix_f32),
        (volt_hbm.at[0, rest], volt.at[rest]),
    )
    loads = [
        pltpu.make_async_copy(source, target, load_sem.at[k])
        for k, (source, target) in enumerate(sources)
    ]
    for load in loads:
        load.start()

    stn_flips = [
        (1 - 2 * (stn // 2**bit % 2)) * 2**bit for bit in range(stn_count.bit_length() - 1)
    ]
    chan_flips = [
        (1 - 2 * (chan // 2**bit % 2)) * 2**bit for bit in range(chan_count.bit_length() - 1)
    ]

    def flipped(start, flips, step):
        for bit, flip in enumerate(flips):
            if step >> bit & 1:
                start = start + flip
        return start

    def partner(step):
        return (
            flipped(stn, stn_flips, step // chan_count),
            flipped(chan, chan_flips, step % chan_count),
        )

    barrier = pltpu.get_barrier_semaphore()
    for step in range(1, devices):
        pl.semaphore_signal(
            barrier, inc=1, device_id=partner(step), device_id_type=pl.DeviceIdType.MESH
        )

    lane8 = iota((ROWS, LANES), 1)
    flags8 = lax.fori_loop(
        0, spectra, lambda t, held: jnp.where(lane8 == t, flags_ref[0, t], held),
        jnp.zeros((ROWS, LANES), jnp.float32), unroll=8,
    )
    station = jnp.broadcast_to(row_ref[0], (ROWS, LANES)).astype(jnp.float32)
    meta[stn] = jnp.where(iota((ROWS, LANES), 0) == 0, flags8, station)

    def meta_copy(step):
        return pltpu.make_async_remote_copy(
            src_ref=meta.at[stn], dst_ref=meta.at[stn],
            send_sem=meta_send_sem, recv_sem=meta_recv_sem,
            device_id=(flipped(stn, stn_flips, step), chan), device_id_type=pl.DeviceIdType.MESH,
        )

    inner = (stn // (stn_count // 2) + stn // (stn_count // 4)) % 2

    def block_copy(chunk, step, inner_step):
        to_stn, to_chan = (
            there + inner * (other - there)
            for there, other in zip(partner(step), partner(inner_step))
        )
        return pltpu.make_async_remote_copy(
            src_ref=send.at[chunk, to_stn * chan_count + to_chan], dst_ref=recv.at[chunk, me],
            send_sem=send_sem.at[chunk], recv_sem=recv_sem.at[chunk],
            device_id=(to_stn, to_chan), device_id_type=pl.DeviceIdType.MESH,
        )

    for load in loads[:3]:
        load.wait()
    for chunk in range(chunks):
        start = chunk * span
        low = 0 if chunk == 0 else start + taps
        high = min(start + span + taps, frames)

        def widen(a, carry, low=low, high=high):
            lanes = pl.ds(pl.multiple_of(a * LANES, LANES), LANES)
            pairs = volt[low:high, :, lanes].reshape(2 * (high - low), LANES)
            wide[a, 2 * low : 2 * high, :] = pairs.astype(jnp.float32)
            return carry

        if chunk == 1:
            loads[4].wait()
        lax.fori_loop(0, outer, widen, 0)

        def fir(a, carry, start=start):
            for part in range(2):
                def window(tap):
                    rows = wide[a, pl.ds(2 * (start + tap) + part, span, stride=2), :]
                    return rows.reshape(span // ROWS, ROWS, LANES)

                def weight(tap):
                    at = pl.multiple_of((a * taps + tap) * ROWS, ROWS)
                    return taper_ref[pl.ds(at, ROWS), :][None]

                total = weight(0) * window(0)
                for tap in range(1, taps):
                    total = total + weight(tap) * window(tap)
                filt[part, a] = total.reshape(span, LANES)
            return carry

        lax.fori_loop(0, outer, fir, 0)

        def first_stage(tile, carry):
            rows = pl.ds(pl.multiple_of(tile * ROWS, ROWS), ROWS)
            values = dft16([(filt[0, a, rows, :], filt[1, a, rows, :]) for a in range(outer)])
            for k in range(outer):
                re, im = values[k]
                c = twist_ref[k : k + 1, :]
                s = twist_ref[outer + k : outer + k + 1, :]
                mids[k, rows, 0:LANES] = re * c + im * s
                mids[k, rows, LANES:] = im * c - re * s
            return carry

        lax.fori_loop(0, span // ROWS, first_stage, 0)

        weights8 = jnp.zeros((ROWS, LANES), jnp.float32)
        for j in range(packed):
            shift = (span * j - start) % LANES
            rolled = pltpu.roll(flags8, shift, 1) if shift else flags8
            weights8 = jnp.where(lane8 // span == j, rolled, weights8)
        if chunk == 0:
            loads[3].wait()
            for half in range(2):
                columns = slice(half * LANES, (half + 1) * LANES)
                matrix_ref[:, columns] = matrix_f32[
                    2 * LANES * half : 2 * LANES * (half + 1)
                ].astype(jnp.bfloat16)
        for pair in range(groups // 2):
            halves = []
            for group in (2 * pair, 2 * pair + 1):
                data = mids[packed * group : packed * (group + 1)].reshape(LANES, 2 * LANES)
                spectrum = lax.dot_general(
                    matrix_ref[...], data.astype(jnp.bfloat16), (((1,), (1,)), ((), ())),
                    preferred_element_type=jnp.float32,
                )
                rounded = spectrum.astype(jnp.bfloat16).astype(jnp.float32)
                halves.append(rounded.reshape(devices, ROWS, LANES) * weights8[None])
            send[chunk, :, 2 * ROWS * pair : 2 * ROWS * (pair + 1), :] = jnp.concatenate(
                halves, axis=1
            ).astype(jnp.bfloat16)

        if chunk == 0:
            pl.semaphore_wait(barrier, devices - 1)
        half = devices // 2
        outer_order = range(devices - 1, 0, -1)
        inner_order = (*range(half - 1, 0, -1), *range(devices - 1, half - 1, -1))
        for step, inner_step in zip(outer_order, inner_order):
            block_copy(chunk, step, inner_step).start()
        if chunk == 0:
            for step in range(1, stn_count):
                meta_copy(step).start()
        recv[chunk, me] = send[chunk, me]

    told = meta.at[pl.ds(0, stn_count - 1)]
    pltpu.make_async_copy(told, told, meta_recv_sem).wait()
    tall = packed * devices
    exact = functools.partial(
        lax.dot_general, precision=lax.Precision.HIGHEST, preferred_element_type=jnp.float32
    )
    spread = (iota((tall, stn_count), 0) % devices // 2 == iota((tall, stn_count), 1)).astype(
        jnp.float32
    )
    all_flags = meta[:, 0, :]
    all_rows = meta[:, 1, :]
    weights = exact(spread, all_flags, (((1,), (0,)), ((), ())))
    count = exact(weights[:devices], weights, (((1,), (1,)), ((), ())))
    place = 2 * exact(spread, all_rows, (((1,), (0,)), ((), ()))).astype(jnp.int32)
    place = place + iota(place.shape, 0) % 2
    across = place.T
    lower = place[:devices] >= across[:devices]
    denom = jnp.maximum(count, 1.0)
    lane_at = iota((tall, tall), 1)
    columns = jnp.logical_and(
        place == lane_at % devices, iota((tall, tall), 0) // devices == lane_at // devices
    ).astype(jnp.bfloat16)
    rows = jnp.logical_and(
        across == iota((tall, tall), 0) % devices, iota((tall, tall), 0) // devices == lane_at // devices
    ).astype(jnp.bfloat16)
    lane = iota((devices, 2 * LANES), 1) % LANES // span
    for j in range(packed):
        masks[j] = (lane == j).astype(jnp.bfloat16)
    for chunk in range(chunks):
        arrived = recv.at[chunk, pl.ds(0, devices - 1)]
        pltpu.make_async_copy(arrived, arrived, recv_sem.at[chunk]).wait()
        gathered[...] = recv[chunk].reshape(devices * block, LANES).astype(jnp.float32)
        for quad in range(quads):
            for group in range(groups):
                at = group * ROWS + quad
                re = gathered[pl.ds(at, devices, stride=block), :].astype(jnp.bfloat16)
                im = gathered[pl.ds(at + quads, devices, stride=block), :].astype(jnp.bfloat16)
                plain = jnp.concatenate([re, im], axis=1)
                turned = jnp.concatenate([im, -re], axis=1)
                left = jnp.concatenate([plain, turned], axis=0)
                right = jnp.concatenate([plain * masks[j] for j in range(packed)], axis=0)
                product = lax.dot_general(
                    left, right, (((1,), (1,)), ((), ())), preferred_element_type=jnp.float32
                )
                if chunk == 0:
                    acc[quad * groups + group] = product
                else:
                    acc[quad * groups + group] += product

    for first in range(0, quads * groups, packed):
        chosen = [
            jnp.where(lower, acc[g, :devices], acc[g, devices:]) / denom
            for g in range(first, first + packed)
        ]
        moved = jnp.dot(
            jnp.concatenate(chosen, axis=0).astype(jnp.bfloat16),
            columns,
            preferred_element_type=jnp.float32,
        )
        moved = jnp.dot(
            rows, moved.astype(jnp.bfloat16), preferred_element_type=jnp.float32
        ).astype(jnp.bfloat16)
        for g in range(packed):
            for j in range(packed):
                out_ref[packed * (first + g) + j] = moved[
                    devices * g : devices * (g + 1), devices * j : devices * (j + 1)
                ]

    for chunk in range(chunks):
        gone = send.at[chunk, pl.ds(0, devices - 1)]
        pltpu.make_async_copy(gone, gone, send_sem.at[chunk]).wait()
    pltpu.make_async_copy(told, told, meta_send_sem).wait()


def fused(voltages, flags, station_row, stn_count, chan_count):
    devices = stn_count * chan_count
    frames, lanes = voltages.shape[2], voltages.shape[3]
    spectra = flags.shape[1]
    taps = frames - spectra + 1
    outer = lanes // LANES
    chunks = 4
    span = spectra // chunks
    packed = LANES // span
    block = outer // packed * ROWS
    table = host_tables(taps, lanes, devices)
    vmem = pl.BlockSpec(memory_space=pltpu.VMEM)
    hbm = pl.BlockSpec(memory_space=pl.ANY)
    f32, bf16 = jnp.float32, jnp.bfloat16
    return pl.pallas_call(
        functools.partial(kernel, stn_count, chan_count, chunks),
        out_shape=jax.ShapeDtypeStruct((lanes // devices, devices, devices), bf16),
        in_specs=[
            hbm,
            pl.BlockSpec(memory_space=pltpu.SMEM),
            pl.BlockSpec(memory_space=pltpu.SMEM),
            hbm,
        ],
        out_specs=vmem,
        scratch_shapes=[
            pltpu.VMEM((frames, 2, lanes), bf16),
            pltpu.VMEM((outer * taps * ROWS, LANES), f32),
            pltpu.VMEM((2 * outer, LANES), f32),
            pltpu.VMEM((4 * LANES, LANES), f32),
            pltpu.VMEM((2 * LANES, 2 * LANES), bf16),
            pltpu.VMEM((outer, 2 * frames, LANES), f32),
            pltpu.VMEM((2, outer, span, LANES), f32),
            pltpu.VMEM((outer, span, 2 * LANES), f32),
            pltpu.VMEM((chunks, devices, block, LANES), bf16),
            pltpu.VMEM((chunks, devices, block, LANES), bf16),
            pltpu.VMEM((stn_count, ROWS, LANES), f32),
            pltpu.VMEM((devices * block, LANES), f32),
            pltpu.VMEM((packed, devices, 2 * LANES), bf16),
            pltpu.VMEM((outer * (LANES // devices) // packed, 2 * devices, packed * devices), f32),
            pltpu.SemaphoreType.DMA((5,)),
            pltpu.SemaphoreType.DMA((chunks,)),
            pltpu.SemaphoreType.DMA((chunks,)),
            pltpu.SemaphoreType.DMA,
            pltpu.SemaphoreType.DMA,
        ],
        compiler_params=pltpu.CompilerParams(
            collective_id=0, has_side_effects=True, vmem_limit_bytes=53 * 1024 * 1024
        ),
    )(jnp.transpose(voltages, (0, 2, 1, 3)), flags, station_row, table)


def solution(mesh):
    placed = (P(("stn", "chan"), None, None, None), P("stn", None), P("stn"))
    return jax.shard_map(
        on_device,
        mesh=mesh,
        in_specs=placed,
        out_specs=P(("stn", "chan"), None, None),
        check_vma=False,
    )
```
